512 devices in a mesh: vocab: 16 (over z), rows: 32 (over y, x, core).
Axes of the slice: x: 4, y: 4, z: 16, core: 2. Of those that a mesh axis runs over, the one named last changes fastest.
Arguments:
- trunk_hidden: bfloat16 [128, 7168], P('rows'), may hold values from -8 to 8
- mtp_state: bfloat16 [128, 7168], P('rows'), may hold values from -24 to 24, as said below
- mtp_gain: bfloat16 [7168], replicated, may hold values from 0.099609375 to 1.8984375
- head_weight: bfloat16 [73728, 7168], P(('vocab', 'rows')), may hold values from -0.28347335 to 0.28347335, as said below
- target_ids: int32 [128], replicated, may hold values from 0 to 73727
- mtp_target_ids: int32 [128], replicated, may hold values from 0 to 73727
- attn_values: bfloat16 [128, 64, 128], P('rows'), may hold values from -6 to 6
- out_proj: bfloat16 [8192, 7168], P('rows', 'vocab'), may hold values from -0.0625 to 0.0625
Outputs:
- grad_trunk: bfloat16 [128, 7168], P('rows')
- grad_residual: bfloat16 [128, 7168], P('rows')
- grad_gain: float32 [7168], replicated
- grad_head: bfloat16 [73728, 7168], P(('vocab', 'rows'))
- grad_attn: bfloat16 [128, 64, 128], P('vocab', 'rows')
- grad_out_proj: bfloat16 [8192, 7168], P('rows', 'vocab')
The draws below stay inside these ranges and needn't reach their ends.
Inputs may be any that keep to these rules, and one draw needn't show every extreme that they name: `mtp_state`: block outputs; rows differ in scale. `head_weight`: head rows.
All inputs are finite; a program needn't handle non-finite values.
Results may differ from the reference program's by a relative error of at most 0.025.
Values may be sent and summed in bfloat16 or wider, within the bound.
A program may use at most 64 MiB of HBM per device.

```python
import math
import jax
import jax.numpy as jnp
import numpy as np
from jax import lax

D = 7168
VBLK = 144
HEAD_DIM = 128
TOKENS = 128
VOCAB = 73728
HEADS = 64


def head_table(key):
    raw = jax.random.normal(jax.random.fold_in(key, 101), (VOCAB, D), jnp.float32)
    return jnp.clip(raw, -6.0, 6.0) * (4.0 / math.sqrt(D))


def draw_head_weight(key, part):
    table = head_table(key)
    return table.astype(jnp.bfloat16)


def draw_trunk_hidden(key, part):
    base = jnp.clip(jax.random.normal(jax.random.fold_in(key, 102), (TOKENS, D), jnp.float32), -6.0, 6.0)
    return base.astype(jnp.bfloat16)


def draw_mtp_state(key, part):
    base = jnp.clip(jax.random.normal(jax.random.fold_in(key, 104), (TOKENS, D), jnp.float32), -6.0, 6.0)
    scales = jnp.exp(jax.random.uniform(jax.random.fold_in(key, 105), (TOKENS, 1), jnp.float32, math.log(0.3), math.log(3.0)))
    rows_out = base * scales
    return rows_out.astype(jnp.bfloat16)


def set_ends(values, stream_key, smallest, high):
    longest = values.shape.index(max(values.shape))
    spots = []
    for shift in (0, 1):
        where = [jax.random.randint(jax.random.fold_in(stream_key, axis), (), 0, length) for axis, length in enumerate(values.shape)]
        where[longest] = (where[longest] + shift) % values.shape[longest]
        spots.append(tuple(where))
    return values.at[spots[0]].set(smallest).at[spots[1]].set(high)


def block_scale(key, shape, cuts, smallest, high):
    level = 1.0
    for axis_at, blocks in cuts:
        draws = jax.random.uniform(jax.random.fold_in(jax.random.fold_in(key, 6), axis_at), (blocks,), jnp.float32, smallest / len(cuts), high / len(cuts))
        level = level * jnp.repeat(jnp.exp(draws), shape[axis_at] // blocks).reshape((-1,) + (1,) * (len(shape) - 1 - axis_at))
    return level


def ranked_wide(own_key, extent, amount, slope):
    portions = [min(1 << octave, amount + 1 - (1 << octave)) * (1 << 20) // math.isqrt((1 << octave) ** slope) + 1 for octave in range((amount + 1).bit_length()) if 1 << octave <= amount]
    deviation = 1 + sum(portions) // (1 << 30)
    grid = np.cumsum(np.array([max(1, weight // deviation) for weight in portions]))
    lot = jax.random.randint(jax.random.fold_in(own_key, 1), extent, 0, int(grid[len(portions) - 1]))
    start = jnp.left_shift(1, jnp.searchsorted(jnp.asarray(grid, jnp.int32), lot, side="right").astype(jnp.int32))
    grade = start - 1 + jax.random.randint(jax.random.fold_in(own_key, 4), extent, 0, 1 << 30) % jnp.minimum(start, amount + 1 - start)
    return jax.random.permutation(jax.random.fold_in(own_key, 2), amount)[grade].astype(jnp.int32)


def gaussian(key, extent, scale, bound, pieces=(), kind=jnp.bfloat16):
    result = jax.random.normal(key, extent, jnp.float32) * scale
    if len(pieces) > 0:
        result = block_scale(key, extent, pieces, -0.22, 0.18) * result
    return jnp.clip(result, min=-bound, max=bound).astype(kind)


def setup_inputs(seed: int = 0) -> dict:
    key_of = jax.random.split(jax.random.key(seed), 9)
    return {
        "trunk_hidden": draw_trunk_hidden(jax.random.fold_in(key_of[8], 71), 0),
        "mtp_state": draw_mtp_state(jax.random.fold_in(key_of[8], 71), 0),
        "mtp_gain": jnp.clip(1.0 + 0.18 * jax.random.normal(key_of[2], (D,), jnp.float32), 0.099609375, 1.8984375).astype(jnp.bfloat16),
        "head_weight": draw_head_weight(jax.random.fold_in(key_of[8], 71), 0),
        "target_ids": set_ends(ranked_wide(key_of[4], (TOKENS,), VOCAB, 2), jax.random.fold_in(key_of[4], 3), 0, VOCAB - 1).astype(jnp.int32),
        "mtp_target_ids": set_ends(ranked_wide(key_of[5], (TOKENS,), VOCAB, 2), jax.random.fold_in(key_of[5], 3), 0, VOCAB - 1).astype(jnp.int32),
        "attn_values": gaussian(key_of[6], (TOKENS, HEADS, HEAD_DIM), 1.0, 6.0, ((0, 32),)),
        "out_proj": gaussian(key_of[7], (HEADS * HEAD_DIM, D), (HEADS * HEAD_DIM) ** -0.5, 0.0625, ((0, 32), (1, 16))),
    }


loss_scale = 8.0
mtp_share = 0.3
norm_eps = 1e-06

def normalize(state):
    values = state.astype(jnp.float32)
    inverse = lax.rsqrt(lax.optimization_barrier(jnp.mean(values * values, axis=-1, keepdims=True)) + norm_eps)
    return (values * inverse, inverse)

def reference(trunk_hidden, mtp_state, mtp_gain, head_weight, target_ids, mtp_target_ids, attn_values, out_proj):
    gain = mtp_gain.astype(jnp.float32)
    normed, inverse = normalize(mtp_state)
    mtp_hidden = (normed * gain).astype(jnp.bfloat16)
    hidden = jnp.concatenate([trunk_hidden, mtp_hidden], axis=0)
    targets = jnp.concatenate([target_ids, mtp_target_ids]).astype(jnp.int32)
    shares = jnp.concatenate([jnp.full((TOKENS,), loss_scale, jnp.float32), jnp.full((TOKENS,), loss_scale * mtp_share, jnp.float32)])
    logits = lax.dot_general(hidden, head_weight, (((1,), (1,)), ((), ())), preferred_element_type=jnp.float32)
    top = lax.optimization_barrier(jnp.max(logits, axis=1, keepdims=True))
    total = lax.optimization_barrier(jnp.sum(jnp.exp(logits - top), axis=1, keepdims=True))
    onehot = (targets[:, None] == jnp.arange(VOCAB, dtype=jnp.int32)[None, :]).astype(jnp.float32)
    logit_grads = (shares[:, None] * (jnp.exp(logits - top) / total - onehot)).astype(jnp.bfloat16)
    blocks = VOCAB // VBLK
    weight_blocks = head_weight.reshape(blocks, VBLK, D)
    grad_blocks = logit_grads.reshape(2 * TOKENS, blocks, VBLK).transpose(1, 0, 2)

    def block_step(carry, pair):
        weight_block, grad_block = pair
        part = jnp.dot(grad_block, weight_block, preferred_element_type=jnp.float32).astype(jnp.bfloat16)
        part = lax.optimization_barrier(part).astype(jnp.float32)
        head_part = lax.dot_general(grad_block, hidden, (((0,), (0,)), ((), ())), preferred_element_type=jnp.float32).astype(jnp.bfloat16)
        return (carry + part, head_part)
    grad_hidden, head_parts = lax.scan(block_step, jnp.zeros((2 * TOKENS, D), jnp.float32), (weight_blocks, grad_blocks))
    grad_head = head_parts.reshape(VOCAB, D)
    grad_trunk = grad_hidden[:TOKENS].astype(jnp.bfloat16)
    mtp_grad = grad_hidden[TOKENS:]
    grad_gain = lax.optimization_barrier(jnp.sum(mtp_grad * normed, axis=0))
    scaled = mtp_grad * gain
    dot_mean = lax.optimization_barrier(jnp.mean(scaled * normed, axis=-1, keepdims=True))
    grad_residual = (inverse * (scaled - normed * dot_mean)).astype(jnp.bfloat16)
    grad_attn = lax.dot_general(grad_residual, out_proj, (((1,), (1,)), ((), ())), preferred_element_type=jnp.float32)
    grad_attn = grad_attn.astype(jnp.bfloat16).reshape(TOKENS, HEADS, HEAD_DIM)
    flat_values = attn_values.reshape(TOKENS, HEADS * HEAD_DIM)
    grad_out_proj = lax.dot_general(flat_values, grad_residual, (((0,), (0,)), ((), ())), preferred_element_type=jnp.float32).astype(jnp.bfloat16)
    return (grad_trunk, grad_residual, grad_gain, grad_head, grad_attn, grad_out_proj)
```

```python
import functools

import jax
import jax.numpy as jnp
from jax import lax
from jax.experimental import pallas as pl
from jax.experimental.pallas import tpu as pltpu
from jax.sharding import PartitionSpec as P

loss_scale = 8.0
mtp_share = 0.3
norm_eps = 1e-06
f32 = jnp.float32
bf16 = jnp.bfloat16
LANES = 512
HALF = LANES // 2


def nn(a, b):
    return lax.dot_general(a, b, (((1,), (0,)), ((), ())), preferred_element_type=f32)


def nt(a, b):
    return lax.dot_general(a, b, (((1,), (1,)), ((), ())), preferred_element_type=f32)


def iota(shape, axis):
    return lax.broadcasted_iota(jnp.int32, shape, axis)


def fold(block):
    w = block.shape[1] // 2
    return jnp.concatenate([block[:, :w], block[:, w:]], axis=0).astype(bf16)


def unfold(block):
    return jnp.concatenate([block[:8], block[8:]], axis=1)


def remote(src, dst, send, recv, device):
    return pltpu.make_async_remote_copy(
        src_ref=src,
        dst_ref=dst,
        send_sem=send,
        recv_sem=recv,
        device_id=device,
        device_id_type=pl.DeviceIdType.MESH,
    )


def kernel(
    dims,
    trunk, state, gain, w_hbm, tids, mids, attn, out_proj_t,
    o_trunk, o_res, o_gain, o_head, o_attn, o_proj_t,
    own8, st8, inv8, sib8, w2, hid, lt_own, lt_sib, st_plane, st_z,
    gt, part, head_out, rx, ry, axs, ays, rx2, ry2, sum8, zs, zr, zo, po, pr, sel, gather_v,
    a2a_s, a2a_r, vals, opw, zg, gs, gr, proj_s,
    cp_sem, sib_s, sib_r, ag_s1, ag_s2, ag_r, pst_s, pst_r, zst_s, zst_r,
    rs_s1, rs_r1, rs_s2, rs_r2, zrs_s, zrs_r, zag_s, zag_r, pag_s, pag_r,
    a2a_ss, a2a_rs, zg_s, zg_r, zga_s, zga_r,
):
    nx, ny, nz, width = dims
    rows = 2 * nx * ny
    chips = nx * ny
    tokens = 16 * chips
    half_tokens = tokens // 2
    vb = w_hbm.shape[0]
    dh = width // 2
    xw = dh // 2
    yw = dh - xw
    heads = attn.shape[1]
    hd = attn.shape[2]
    step = width // nz
    starts = [zz * step // 128 * 128 for zz in range(nz)]

    v = lax.axis_index("vocab")
    r = lax.axis_index("rows")
    c = lax.rem(r, 2)
    chip = r // 2
    x = lax.rem(chip, nx)
    y = chip // nx
    sibling = (v, r + 1 - 2 * c)
    window = pl.multiple_of(v * step // 128 * 128, 128)

    def at(yy, xx, core):
        return (v, (yy * nx + xx) * 2 + core)

    own_cols = pl.ds(pl.multiple_of(c * dh, 128), dh)
    sib_cols = pl.ds(pl.multiple_of((1 - c) * dh, 128), dh)
    w_copy = pltpu.make_async_copy(w_hbm.at[:, own_cols], w2.at[c], cp_sem.at[0])
    w_copy.start()

    bar = pltpu.get_barrier_semaphore()

    def greet_rows(i, carry):
        pl.semaphore_signal(
            bar, inc=1, device_id=(v, lax.rem(r + i, rows)), device_id_type=pl.DeviceIdType.MESH
        )
        return carry

    def greet_vocab(i, carry):
        pl.semaphore_signal(
            bar, inc=1, device_id=(lax.rem(v + i, nz), r), device_id_type=pl.DeviceIdType.MESH
        )
        return carry

    lax.fori_loop(1, rows, greet_rows, 0)
    lax.fori_loop(1, nz, greet_vocab, 0)

    sv = state[...].astype(f32)
    inverse = lax.rsqrt(jnp.mean(sv * sv, axis=-1, keepdims=True) + norm_eps)
    normed = sv * inverse
    own8[0:4, :] = trunk[...].astype(f32)
    own8[4:8, :] = (normed * gain[...].astype(f32)).astype(bf16).astype(f32)
    st8[0:4, :] = jnp.zeros((4, width), f32)
    st8[4:8, :] = normed
    inv8[0:4, :] = jnp.zeros((4, 128), f32)
    inv8[4:8, :] = jnp.broadcast_to(inverse, (4, 128))

    pl.semaphore_wait(bar, rows - 1 + nz - 1)

    tok_copy = remote(own8.at[:, sib_cols], sib8, sib_s.at[0], sib_r.at[0], sibling)
    tok_copy.start()
    w_send = remote(w_hbm.at[:, sib_cols], w2.at[c], sib_s.at[1], sib_r.at[1], sibling)
    w_send.start()
    mine = own8[:, own_cols]
    tok_copy.wait_recv()
    other = sib8[...]
    first = c == 0
    hid[y, x] = jnp.concatenate(
        [jnp.where(first, mine, other), jnp.where(first, other, mine)], axis=0
    ).astype(bf16)

    hx = pl.ds(0, xw)
    hy = pl.ds(xw, yw)
    sends = []

    def push(copy):
        copy.start()
        sends.append(copy)

    for j in range(1, nx):
        blk = hid.at[y, x, :, hx]
        push(remote(blk, blk, ag_s1.at[0, j - 1], ag_r.at[0, y, x], at(y, lax.rem(x + j, nx), c)))
    for j in range(1, ny):
        blk = hid.at[y, x, :, hy]
        push(remote(blk, blk, ag_s1.at[1, j - 1], ag_r.at[1, y, x], at(lax.rem(y + j, ny), x, c)))

    order = {4: (0, 1, 3, 2), 2: (0, 1), 1: (0,)}
    for i in range(max(nx, ny)):
        if i < nx:
            xx = lax.rem(x + order[nx][i], nx)
            blk = hid.at[y, xx, :, hx]
            if i > 0:
                remote(blk, blk, ag_s1.at[0, 0], ag_r.at[0, y, xx], sibling).wait_recv()
            for j in range(1, ny):
                push(remote(blk, blk, ag_s2.at[0, i, j - 1], ag_r.at[0, y, xx], at(lax.rem(y + j, ny), x, c)))
        if i < ny:
            yy = lax.rem(y + order[ny][i], ny)
            blk = hid.at[yy, x, :, hy]
            if i > 0:
                remote(blk, blk, ag_s1.at[1, 0], ag_r.at[1, yy, x], sibling).wait_recv()
            for j in range(1, nx):
                push(remote(blk, blk, ag_s2.at[1, i, j - 1], ag_r.at[1, yy, x], at(y, lax.rem(x + j, nx), c)))

    ir = iota((rows * 16, 4 * heads), 0)
    im = iota((rows * 16, 4 * heads), 1)
    kk = ir & 15
    pick = (kk < 8) & (im == (kk >> 1) * heads + 2 * (ir >> 4) + (kk & 1))
    a2a_s[...] = (
        nn(pick.astype(f32).astype(bf16), attn[...].reshape(4 * heads, hd)).astype(bf16).reshape(rows, 16, hd)
    )

    def a2a_copy(i):
        rr = lax.rem(r + i, rows)
        return remote(a2a_s.at[rr], a2a_r.at[r], a2a_ss.at[i], a2a_rs.at[r], (v, rr))

    def a2a_start(i, carry):
        a2a_copy(i).start()
        return carry

    lax.fori_loop(1, rows, a2a_start, 0)
    a2a_r[r] = a2a_s[r]

    it = iota((half_tokens, rows * 16), 0)
    il = iota((half_tokens, rows * 16), 1)
    base = 16 * (it >> 2) + (it & 3)
    sel[0:half_tokens, :] = (il == base + 4).astype(f32).astype(bf16)
    sel[half_tokens:tokens, :] = (il == base + 12).astype(f32).astype(bf16)
    ig = iota((16, rows * 16), 0)
    kg = iota((16, rows * 16), 1) & 15
    sel[tokens : tokens + 16, :] = (
        ((ig == 0) & (kg < 2)) | ((ig == 1) & (kg >= 8) & (kg < 10))
    ).astype(f32).astype(bf16)
    base = 16 * (it >> 2) + 2 * (it & 3)
    for h in range(2):
        gather_v[h * half_tokens : (h + 1) * half_tokens, :] = (il == base + h).astype(f32).astype(bf16)
    opw[...] = jnp.zeros(opw.shape, bf16)
    shift = pl.multiple_of(v * step % 128, 16)
    opw[pl.ds(shift, step), :] = out_proj_t[...]

    ids = jnp.concatenate([tids[...], mids[...]], axis=1)
    ip = iota((8, tokens), 0)
    digits = jnp.where(
        ip == 0, ids & 63, jnp.where(ip == 1, (ids >> 6) & 63, jnp.where(ip == 2, ids >> 12, 0))
    )
    im = iota((tokens, tokens), 0)
    il = iota((tokens, tokens), 1)
    jl = il & 7
    src = 4 * (il >> 3) + jnp.where(jl < 4, jl, jl - 4 + half_tokens)
    placed = nn(digits.astype(f32).astype(bf16), (im == src).astype(f32).astype(bf16))
    target = (placed[0:1] + 64.0 * placed[1:2] + 4096.0 * placed[2:3]).astype(jnp.int32)
    lane = iota((1, tokens), 1)
    share = jnp.where((lane & 7) < 4, loss_scale, loss_scale * mtp_share).astype(f32)
    vocab_id = iota((2 * vb, tokens), 0) + (v * rows + 2 * chip) * vb

    w_copy.wait()
    remote(w2.at[1 - c], w2.at[1 - c], sib_s.at[1], sib_r.at[1], sibling).wait_recv()

    def ag_wait(i, carry):
        xx = lax.rem(i, nx)
        yy = i // nx
        bx = hid.at[lax.rem(y + 1 + yy, ny), xx, :, hx]
        remote(bx, bx, ag_s1.at[0, 0], ag_r.at[0, lax.rem(y + 1 + yy, ny), xx], sibling).wait_recv()
        return carry

    def ag_wait_y(i, carry):
        yy = lax.rem(i, ny)
        xx = lax.rem(x + 1 + i // ny, nx)
        by = hid.at[yy, xx, :, hy]
        remote(by, by, ag_s1.at[1, 0], ag_r.at[1, yy, xx], sibling).wait_recv()
        return carry

    lax.fori_loop(0, nx * (ny - 1), ag_wait, 0)
    lax.fori_loop(0, ny * (nx - 1), ag_wait_y, 0)
    lt_own[...] = nt(w2[...].reshape(2 * vb, dh), hid[...].reshape(tokens, dh))
    lt_copy = remote(lt_own, lt_sib, sib_s.at[2], sib_r.at[2], sibling)
    lt_copy.start()
    lt_copy.wait()
    logits = lt_own[...] + lt_sib[...]
    onehot = (vocab_id == target).astype(f32)
    top_chip = jnp.max(logits, axis=0, keepdims=True)
    e = jnp.exp(logits - top_chip)
    lt_sib[...] = e
    i8 = iota((8, tokens), 0)
    stats = jnp.where(
        i8 == 0,
        top_chip,
        jnp.where(
            i8 == 1,
            jnp.sum(e, axis=0, keepdims=True),
            jnp.where(
                i8 == 2,
                jnp.sum(e * logits, axis=0, keepdims=True),
                jnp.where(i8 == 3, jnp.sum(onehot * logits, axis=0, keepdims=True), 0.0),
            ),
        ),
    )

    def merge(slots, count):
        top = slots[0][0:1]
        for s in range(1, count):
            top = jnp.maximum(top, slots[s][0:1])
        acc = jnp.zeros((8, tokens), f32)
        for s in range(count):
            tile = slots[s]
            weight = jnp.exp(tile[0:1] - top)
            acc = acc + jnp.where(i8 == 3, tile, tile * weight)
        return jnp.where(i8 == 0, top, acc)

    def pst_copy(i):
        cc = lax.rem(chip + i, chips)
        return remote(st_plane.at[chip], st_plane.at[chip], pst_s.at[i], pst_r.at[chip], (v, 2 * cc + c))

    def pst_start(i, carry):
        pst_copy(i).start()
        return carry

    def pst_wait(i, carry):
        cc = lax.rem(chip + i, chips)
        remote(st_plane.at[cc], st_plane.at[cc], pst_s.at[0], pst_r.at[cc], sibling).wait_recv()
        pst_copy(i).wait_send()
        return carry

    st_plane[chip] = stats
    lax.fori_loop(1, chips, pst_start, 0)
    lax.fori_loop(1, chips, pst_wait, 0)

    def zst_copy(i):
        zz = lax.rem(v + i, nz)
        return remote(st_z.at[v], st_z.at[v], zst_s.at[i], zst_r.at[v], (zz, r))

    def zst_start(i, carry):
        zst_copy(i).start()
        return carry

    def zst_wait(i, carry):
        zz = lax.rem(v + i, nz)
        remote(st_z.at[zz], st_z.at[zz], zst_s.at[0], zst_r.at[zz], sibling).wait_recv()
        zst_copy(i).wait_send()
        return carry

    st_z[v] = merge(st_plane, chips)
    lax.fori_loop(1, nz, zst_start, 0)
    lax.fori_loop(1, nz, zst_wait, 0)
    whole = merge(st_z, nz)
    top, total = whole[0:1], whole[1:2]
    grads = lt_sib[...] * (share * jnp.exp(top_chip - top) / total) - share * onehot
    gt[...] = grads.astype(bf16)
    dot = share * (whole[2:3] / total - whole[3:4])
    il = iota((8, tokens), 1)
    dot_mean = (
        jnp.sum(jnp.where(il == 8 * r + iota((8, tokens), 0), dot, 0.0), axis=1, keepdims=True) / width
    )

    grads_t = jnp.transpose(grads).astype(bf16)
    tile = 256 if dh % 256 == 0 else dh
    for n in range(0, dh, tile):
        res = nn(grads_t, w2[:, :, n : n + tile].reshape(2 * vb, tile))
        part[:, :, :, n : n + tile] = res.astype(bf16).reshape(ny, nx, 16, tile)
        if n + tile == xw or (n < xw < n + tile):
            for j in range(1, nx):
                xx = lax.rem(x + j, nx)
                push(remote(part.at[:, xx, :, hx], rx.at[j - 1], rs_s1.at[0, j - 1], rs_r1.at[0, j - 1], at(y, xx, c)))
    for j in range(1, ny):
        yy = lax.rem(y + j, ny)
        push(remote(part.at[yy, :, :, hy], ry.at[j - 1], rs_s1.at[1, j - 1], rs_r1.at[1, j - 1], at(yy, x, c)))

    for n in range(0, dh, tile):
        head_out[:, n : n + tile] = nn(
            gt[pl.ds(pl.multiple_of((1 - c) * vb, 16), vb), :], hid[:, :, :, n : n + tile].reshape(tokens, tile)
        ).astype(bf16)
    head_copy = remote(head_out, o_head.at[:, own_cols], sib_s.at[3], sib_r.at[3], sibling)
    head_copy.start()
    for n in range(0, dh, tile):
        o_head[:, pl.ds(pl.multiple_of(c * dh + n, 128), tile)] = nn(
            gt[pl.ds(pl.multiple_of(c * vb, 16), vb), :], hid[:, :, :, n : n + tile].reshape(tokens, tile)
        ).astype(bf16)

    def a2a_wait(i, carry):
        rr = lax.rem(r + i, rows)
        remote(a2a_r.at[rr], a2a_r.at[rr], a2a_ss.at[0], a2a_rs.at[rr], sibling).wait_recv()
        a2a_copy(i).wait_send()
        return carry

    lax.fori_loop(1, rows, a2a_wait, 0)
    received = a2a_r[...].reshape(rows * 16, hd)
    for h in range(2):
        vals[:, h * hd : (h + 1) * hd] = nn(
            gather_v[h * half_tokens : (h + 1) * half_tokens, :], received
        ).astype(bf16)

    for j in range(1, nx):
        remote(rx.at[j - 1], rx.at[j - 1], rs_s1.at[0, 0], rs_r1.at[0, j - 1], sibling).wait_recv()
    for jj in range(ny):
        j = (jj + 1) % ny
        yy = lax.rem(y + j, ny)
        total_x = part[yy, x, :, 0:xw].astype(f32)
        for k in range(nx - 1):
            total_x = total_x + rx[k, yy].astype(f32)
        for d in range(2):
            axs[j, d] = fold(total_x[8 * d : 8 * d + 8])
        if j > 0:
            for d in range(2):
                push(remote(axs.at[j, d], rx2.at[j, c], rs_s2.at[0, j, d], rs_r2.at[0, j, c], at(yy, x, d)))
        else:
            push(remote(axs.at[0, 1 - c], rx2.at[0, c], rs_s2.at[0, 0, 0], rs_r2.at[0, 0, c], sibling))
            rx2[0, c] = axs[0, c]
    for j in range(1, ny):
        remote(ry.at[j - 1], ry.at[j - 1], rs_s1.at[1, 0], rs_r1.at[1, j - 1], sibling).wait_recv()
    for jj in range(nx):
        j = (jj + 1) % nx
        xx = lax.rem(x + j, nx)
        total_y = part[y, xx, :, xw:dh].astype(f32)
        for k in range(ny - 1):
            total_y = total_y + ry[k, xx].astype(f32)
        for d in range(2):
            ays[j, d] = fold(total_y[8 * d : 8 * d + 8])
        if j > 0:
            for d in range(2):
                push(remote(ays.at[j, d], ry2.at[j, c], rs_s2.at[1, j, d], rs_r2.at[1, j, c], at(y, xx, d)))
        else:
            push(remote(ays.at[0, 1 - c], ry2.at[0, c], rs_s2.at[1, 0, 0], rs_r2.at[1, 0, c], sibling))
            ry2[0, c] = ays[0, c]
    for buf, axis, count, wid, off in ((rx2, 0, ny, xw, 0), (ry2, 1, nx, yw, xw)):
        for j in range(1, count):
            for s in range(2):
                remote(buf.at[j, s], buf.at[j, s], rs_s2.at[axis, 0, 0], rs_r2.at[axis, j, s], sibling).wait_recv()
        remote(buf.at[0, 1 - c], buf.at[0, 1 - c], rs_s2.at[axis, 0, 0], rs_r2.at[axis, 0, 1 - c], sibling).wait_recv()
        for s in range(2):
            acc = buf[0, s].astype(f32)
            for j in range(1, count):
                acc = acc + buf[j, s].astype(f32)
            sum8[:, s * dh + off : s * dh + off + wid] = unfold(acc)

    for zz in range(nz):
        zs[zz] = fold(sum8[:, starts[zz] : starts[zz] + LANES])

    def zrs_copy(i):
        zz = lax.rem(v + i, nz)
        return remote(zs.at[zz], zr.at[v], zrs_s.at[i], zrs_r.at[v], (zz, r))

    def zrs_start(i, carry):
        zrs_copy(i).start()
        return carry

    def zrs_wait(i, carry):
        zz = lax.rem(v + i, nz)
        remote(zr.at[zz], zr.at[zz], zrs_s.at[0], zrs_r.at[zz], sibling).wait_recv()
        zrs_copy(i).wait_send()
        return carry

    lax.fori_loop(1, nz, zrs_start, 0)
    zr[v] = zs[v]
    lax.fori_loop(1, nz, zrs_wait, 0)
    acc = zr[0].astype(f32)
    for zz in range(1, nz):
        acc = acc + zr[zz].astype(f32)
    grad = unfold(acc)

    cols = pl.ds(window, LANES)
    normed8 = st8[:, cols]
    scaled = grad * gain[:, cols].astype(f32)
    residual = inv8[:, 0:1] * (scaled - normed8 * dot_mean)
    gain_term = jnp.sum(grad * normed8, axis=0, keepdims=True)
    gain_high = gain_term.astype(bf16).astype(f32)
    row = iota((8, LANES), 0)
    po[...] = fold(
        jnp.where(
            row == 0, gain_high, jnp.where(row == 1, gain_term - gain_high, jnp.where(row < 4, 0.0, residual))
        )
    )

    def pag_copy(i):
        return remote(po, pr.at[r], pag_s.at[i], pag_r.at[r], (v, lax.rem(r + i, rows)))

    def pag_start(i, carry):
        pag_copy(i).start()
        return carry

    def pag_wait(i, carry):
        rr = lax.rem(r + i, rows)
        remote(pr.at[rr], pr.at[rr], pag_s.at[0], pag_r.at[rr], sibling).wait_recv()
        pag_copy(i).wait_send()
        return carry

    lax.fori_loop(1, rows, pag_start, 0)
    pr[r] = po[...]

    zo[v] = fold(jnp.where(row < 4, grad, residual))

    def zag_copy(i):
        return remote(zo.at[v], zo.at[v], zag_s.at[i], zag_r.at[v], (lax.rem(v + i, nz), r))

    def zag_start(i, carry):
        zag_copy(i).start()
        return carry

    def zag_wait(i, carry):
        zz = lax.rem(v + i, nz)
        remote(zo.at[zz], zo.at[zz], zag_s.at[0], zag_r.at[zz], sibling).wait_recv()
        zag_copy(i).wait_send()
        return carry

    lax.fori_loop(1, nz, zag_start, 0)
    lax.fori_loop(1, rows, pag_wait, 0)

    picked = nn(sel[...], pr[...].reshape(rows * 16, HALF))
    columns = jnp.concatenate([picked[0:half_tokens], picked[half_tokens:tokens]], axis=1)
    columns_b = columns.astype(bf16)
    attn_term = nn(columns_b, opw[...])
    for zz in range(nz):
        blk = attn_term[8 * zz : 8 * zz + 8]
        gs[zz] = fold(blk)

    def zga_copy(i):
        zz = lax.rem(v + i, nz)
        return remote(gs.at[zz], gr.at[v], zga_s.at[i], zga_r.at[v], (zz, r))

    def zga_start(i, carry):
        zga_copy(i).start()
        return carry

    def zga_wait(i, carry):
        zz = lax.rem(v + i, nz)
        remote(gr.at[zz], gr.at[zz], zga_s.at[0], zga_r.at[zz], sibling).wait_recv()
        zga_copy(i).wait_send()
        return carry

    lax.fori_loop(1, nz, zga_start, 0)
    gr[v] = gs[v]
    zg[v] = jnp.concatenate([picked[tokens : tokens + 1], picked[tokens + 1 : tokens + 2]], axis=1)

    def zg_copy(i):
        return remote(zg.at[v], zg.at[v], zg_s.at[i], zg_r.at[v], (lax.rem(v + i, nz), r))

    def zg_start(i, carry):
        zg_copy(i).start()
        return carry

    def zg_wait(i, carry):
        zz = lax.rem(v + i, nz)
        remote(zg.at[zz], zg.at[zz], zg_s.at[0], zg_r.at[zz], sibling).wait_recv()
        zg_copy(i).wait_send()
        return carry

    lax.fori_loop(1, nz, zg_start, 0)

    proj_s[...] = nn(jnp.transpose(columns).astype(bf16), vals[...]).astype(bf16)
    o_proj_t[...] = proj_s[pl.ds(shift, step), :]

    lax.fori_loop(1, nz, zag_wait, 0)
    for zz in range(nz):
        block = unfold(zo[zz].astype(f32)).astype(bf16)
        o_trunk[:, starts[zz] : starts[zz] + LANES] = block[0:4]
        o_res[:, starts[zz] : starts[zz] + LANES] = block[4:8]
    lax.fori_loop(1, nz, zg_wait, 0)
    for zz in range(nz):
        o_gain[:, starts[zz] : starts[zz] + LANES] = zg[zz]
    lax.fori_loop(1, nz, zga_wait, 0)
    acc = gr[0].astype(f32)
    for zz in range(1, nz):
        acc = acc + gr[zz].astype(f32)
    o_attn[...] = acc.astype(bf16)

    remote(head_out, o_head.at[:, sib_cols], sib_s.at[3], sib_r.at[3], sibling).wait_recv()
    head_copy.wait_send()
    tok_copy.wait_send()
    w_send.wait_send()
    for copy in sends:
        copy.wait_send()


def local(dims, trunk_hidden, mtp_state, mtp_gain, head_weight, target_ids, mtp_target_ids, attn_values, out_proj):
    nx, ny, nz, width = dims
    rows = 2 * nx * ny
    tokens = 8 * rows
    vb = head_weight.shape[0]
    dh = width // 2
    xw = dh // 2
    yw = dh - xw
    step = out_proj.shape[1]
    heads, hd = attn_values.shape[1:]
    vmem = pltpu.VMEM
    dma = pltpu.SemaphoreType.DMA
    scratch = [
        vmem((8, width), f32),
        vmem((8, width), f32),
        vmem((8, 128), f32),
        vmem((8, dh), f32),
        vmem((2, vb, dh), bf16),
        vmem((ny, nx, 16, dh), bf16),
        vmem((2 * vb, tokens), f32),
        vmem((2 * vb, tokens), f32),
        vmem((nx * ny, 8, tokens), f32),
        vmem((nz, 8, tokens), f32),
        vmem((2 * vb, tokens), bf16),
        vmem((ny, nx, 16, dh), bf16),
        vmem((vb, dh), bf16),
        vmem((max(nx - 1, 1), ny, 16, xw), bf16),
        vmem((max(ny - 1, 1), nx, 16, yw), bf16),
        vmem((ny, 2, 16, xw // 2), bf16),
        vmem((nx, 2, 16, yw // 2), bf16),
        vmem((ny, 2, 16, xw // 2), bf16),
        vmem((nx, 2, 16, yw // 2), bf16),
        vmem((8, width), f32),
        vmem((nz, 16, HALF), bf16),
        vmem((nz, 16, HALF), bf16),
        vmem((nz, 16, HALF), bf16),
        vmem((16, HALF), bf16),
        vmem((rows, 16, HALF), bf16),
        vmem((tokens + 16, rows * 16), bf16),
        vmem((tokens, rows * 16), bf16),
        vmem((rows, 16, hd), bf16),
        vmem((rows, 16, hd), bf16),
        vmem((tokens // 2, 2 * hd), bf16),
        vmem((LANES, 2 * hd), bf16),
        vmem((nz, 1, LANES), f32),
        vmem((nz, 16, hd), bf16),
        vmem((nz, 16, hd), bf16),
        vmem((LANES, 2 * hd), bf16),
        dma((1,)),
        dma((4,)),
        dma((4,)),
        dma((2, 3)),
        dma((2, 4, 3)),
        dma((2, ny, nx)),
        dma((nx * ny,)),
        dma((nx * ny,)),
        dma((nz,)),
        dma((nz,)),
        dma((2, 3)),
        dma((2, 3)),
        dma((2, 4, 2)),
        dma((2, 4, 2)),
        dma((nz,)),
        dma((nz,)),
        dma((nz,)),
        dma((nz,)),
        dma((rows,)),
        dma((rows,)),
        dma((rows,)),
        dma((rows,)),
        dma((nz,)),
        dma((nz,)),
        dma((nz,)),
        dma((nz,)),
    ]
    in_vmem = pl.BlockSpec(memory_space=pltpu.VMEM)
    in_hbm = pl.BlockSpec(memory_space=pl.ANY)
    shape = jax.ShapeDtypeStruct
    trunk_out, res_out, gain_out, head_out, attn_out, proj_out = pl.pallas_call(
        functools.partial(kernel, dims),
        out_shape=[
            shape((4, width), bf16),
            shape((4, width), bf16),
            shape((1, width), f32),
            shape((vb, width), bf16),
            shape((16, hd), bf16),
            shape((step, 2 * hd), bf16),
        ],
        in_specs=[in_vmem, in_vmem, in_vmem, in_hbm, in_vmem, in_vmem, in_vmem, in_vmem],
        out_specs=[in_vmem] * 6,
        scratch_shapes=scratch,
        compiler_params=pltpu.CompilerParams(
            collective_id=0, has_side_effects=True, vmem_limit_bytes=56 * 2**20
        ),
        name="head_backward",
    )(
        trunk_hidden,
        mtp_state,
        mtp_gain.reshape(1, width),
        head_weight,
        target_ids.reshape(1, -1),
        mtp_target_ids.reshape(1, -1),
        attn_values,
        out_proj.T,
    )
    grad_attn = attn_out.reshape(2, 8, hd).transpose(1, 0, 2)
    return (trunk_out, res_out, gain_out.reshape(width), head_out, grad_attn, proj_out.T)


def solution(mesh):
    nz, rows = mesh.shape["vocab"], mesh.shape["rows"]
    nx = {32: 4, 8: 2, 2: 1}[rows]

    def run(*args):
        dims = (nx, rows // 2 // nx, nz, args[0].shape[1])
        return local(dims, *args)

    return jax.shard_map(
        run,
        mesh=mesh,
        in_specs=(
            P("rows", None),
            P("rows", None),
            P(),
            P(("vocab", "rows"), None),
            P(),
            P(),
            P("rows", None, None),
            P("rows", "vocab"),
        ),
        out_specs=(
            P("rows", None),
            P("rows", None),
            P(),
            P(("vocab", "rows"), None),
            P("vocab", "rows", None),
            P("rows", "vocab"),
        ),
        check_vma=False,
    )
```

```python
import functools

import jax
import jax.numpy as jnp
from jax import lax
from jax.experimental import pallas as pl
from jax.experimental.pallas import tpu as pltpu
from jax.sharding import PartitionSpec as P

loss_scale = 8.0
mtp_share = 0.3
norm_eps = 1e-06
f32 = jnp.float32
bf16 = jnp.bfloat16
LANES = 512
HALF = LANES // 2


def nn(a, b):
    return lax.dot_general(a, b, (((1,), (0,)), ((), ())), preferred_element_type=f32)


def nt(a, b):
    return lax.dot_general(a, b, (((1,), (1,)), ((), ())), preferred_element_type=f32)


def iota(shape, axis):
    return lax.broadcasted_iota(jnp.int32, shape, axis)


def fold(block):
    w = block.shape[1] // 2
    return jnp.concatenate([block[:, :w], block[:, w:]], axis=0).astype(bf16)


def unfold(block):
    return jnp.concatenate([block[:8], block[8:]], axis=1)


def remote(src, dst, send, recv, device):
    return pltpu.make_async_remote_copy(
        src_ref=src,
        dst_ref=dst,
        send_sem=send,
        recv_sem=recv,
        device_id=device,
        device_id_type=pl.DeviceIdType.MESH,
    )


def kernel(
    dims,
    trunk_h, state_h, gain_h, w_hbm, tids_h, mids_h, attn_h, out_proj_h,
    o_trunk, o_res, o_gain, o_head, o_attn, o_proj_t,
    trunk, state, gain, tids, mids, attn, out_proj_t, gain_row, own8, st8, inv8, sib8, w2, hid, lt_own, lt_sib, st_plane, st_z,
    gt, part, head_out, rx, ry, axs, ays, rx2, ry2, sum8, zs, zr, zo, po, pr, sel, gather_v,
    a2a_s, a2a_r, vals, opw, zg, gs, gr, proj_s, attn_s,
    cp_sem, sib_s, sib_r, ag_s1, ag_s2, ag_r, pst_s, pst_r, zst_s, zst_r,
    rs_s1, rs_r1, rs_s2, rs_r2, zrs_s, zrs_r, zag_s, zag_r, pag_s, pag_r,
    a2a_ss, a2a_rs, zg_s, zg_r, zga_s, zga_r,
):
    nx, ny, nz, width = dims
    rows = 2 * nx * ny
    chips = nx * ny
    tokens = 16 * chips
    half_tokens = tokens // 2
    vb = w_hbm.shape[0]
    dh = width // 2
    xw = dh // 2
    yw = dh - xw
    heads, hd = attn.shape[1:]
    step = width // nz
    starts = [zz * step // 128 * 128 for zz in range(nz)]

    v = lax.axis_index("vocab")
    r = lax.axis_index("rows")
    c = lax.rem(r, 2)
    chip = r // 2
    x = lax.rem(chip, nx)
    y = chip // nx
    sibling = (v, r + 1 - 2 * c)
    window = pl.multiple_of(v * step // 128 * 128, 128)

    def at(yy, xx, core):
        return (v, (yy * nx + xx) * 2 + core)

    own_cols = pl.ds(pl.multiple_of(c * dh, 128), dh)
    sib_cols = pl.ds(pl.multiple_of((1 - c) * dh, 128), dh)
    w_copy = pltpu.make_async_copy(w_hbm.at[:, own_cols], w2.at[c], cp_sem.at[0])
    loads = [
        pltpu.make_async_copy(src, dst, cp_sem.at[1 + i])
        for i, (src, dst) in enumerate(
            ((state_h, state), (gain_h, gain), (trunk_h, trunk), (tids_h, tids), (mids_h, mids), (attn_h, attn), (out_proj_h, out_proj_t))
        )
    ]
    for load in loads:
        load.start()
    w_copy.start()

    bar = pltpu.get_barrier_semaphore()

    def greet_rows(i, carry):
        pl.semaphore_signal(
            bar, inc=1, device_id=(v, lax.rem(r + i, rows)), device_id_type=pl.DeviceIdType.MESH
        )
        return carry

    def greet_vocab(i, carry):
        pl.semaphore_signal(
            bar, inc=1, device_id=(lax.rem(v + i, nz), r), device_id_type=pl.DeviceIdType.MESH
        )
        return carry

    lax.fori_loop(1, rows, greet_rows, 0)
    lax.fori_loop(1, nz, greet_vocab, 0)

    for load in loads[:3]:
        load.wait()
    sv = state[...].astype(f32)
    inverse = lax.rsqrt(jnp.mean(sv * sv, axis=-1, keepdims=True) + norm_eps)
    normed = sv * inverse
    for k in range(width // 128):
        gain_row[0:1, k * 128 : (k + 1) * 128] = gain[k : k + 1, :].astype(f32)
    own8[0:4, :] = trunk[...].astype(f32)
    own8[4:8, :] = (normed * gain_row[...]).astype(bf16).astype(f32)
    st8[0:4, :] = jnp.zeros((4, width), f32)
    st8[4:8, :] = normed
    inv8[0:4, :] = jnp.zeros((4, 128), f32)
    inv8[4:8, :] = jnp.broadcast_to(inverse, (4, 128))

    pl.semaphore_wait(bar, rows - 1 + nz - 1)

    tok_copy = remote(own8.at[:, sib_cols], sib8, sib_s.at[0], sib_r.at[0], sibling)
    tok_copy.start()
    w_send = remote(w_hbm.at[:, sib_cols], w2.at[c], sib_s.at[1], sib_r.at[1], sibling)
    w_send.start()
    mine = own8[:, own_cols]
    tok_copy.wait_recv()
    other = sib8[...]
    first = c == 0
    hid[y, x] = jnp.concatenate(
        [jnp.where(first, mine, other), jnp.where(first, other, mine)], axis=0
    ).astype(bf16)

    hx = pl.ds(0, xw)
    hy = pl.ds(xw, yw)
    sends = []

    def push(copy):
        copy.start()
        sends.append(copy)

    for j in range(1, nx):
        blk = hid.at[y, x, :, hx]
        push(remote(blk, blk, ag_s1.at[0, j - 1], ag_r.at[0, y, x], at(y, lax.rem(x + j, nx), c)))
    for j in range(1, ny):
        blk = hid.at[y, x, :, hy]
        push(remote(blk, blk, ag_s1.at[1, j - 1], ag_r.at[1, y, x], at(lax.rem(y + j, ny), x, c)))

    order = {4: (0, 1, 3, 2), 2: (0, 1), 1: (0,)}
    for i in range(max(nx, ny)):
        if i < nx:
            xx = lax.rem(x + order[nx][i], nx)
            blk = hid.at[y, xx, :, hx]
            if i > 0:
                remote(blk, blk, ag_s1.at[0, 0], ag_r.at[0, y, xx], sibling).wait_recv()
            for j in range(1, ny):
                push(remote(blk, blk, ag_s2.at[0, i, j - 1], ag_r.at[0, y, xx], at(lax.rem(y + j, ny), x, c)))
        if i < ny:
            yy = lax.rem(y + order[ny][i], ny)
            blk = hid.at[yy, x, :, hy]
            if i > 0:
                remote(blk, blk, ag_s1.at[1, 0], ag_r.at[1, yy, x], sibling).wait_recv()
            for j in range(1, nx):
                push(remote(blk, blk, ag_s2.at[1, i, j - 1], ag_r.at[1, yy, x], at(y, lax.rem(x + j, nx), c)))

    for load in loads[3:]:
        load.wait()
    ir = iota((rows * 16, 4 * heads), 0)
    im = iota((rows * 16, 4 * heads), 1)
    kk = ir & 15
    pick = (kk < 8) & (im == (kk >> 1) * heads + 2 * (ir >> 4) + (kk & 1))
    a2a_s[...] = (
        nn(pick.astype(f32).astype(bf16), attn[...].reshape(4 * heads, hd)).astype(bf16).reshape(rows, 16, hd)
    )

    def a2a_copy(i):
        rr = lax.rem(r + i, rows)
        return remote(a2a_s.at[rr], a2a_r.at[r], a2a_ss.at[i], a2a_rs.at[r], (v, rr))

    def a2a_start(i, carry):
        a2a_copy(i).start()
        return carry

    lax.fori_loop(1, rows, a2a_start, 0)
    a2a_r[r] = a2a_s[r]

    it = iota((half_tokens, rows * 16), 0)
    il = iota((half_tokens, rows * 16), 1)
    base = 16 * (it >> 2) + (it & 3)
    sel[0:half_tokens, :] = (il == base + 4).astype(f32).astype(bf16)
    sel[half_tokens:tokens, :] = (il == base + 12).astype(f32).astype(bf16)
    ig = iota((16, rows * 16), 0)
    kg = iota((16, rows * 16), 1) & 15
    sel[tokens : tokens + 16, :] = (
        ((ig == 0) & (kg < 2)) | ((ig == 1) & (kg >= 8) & (kg < 10))
    ).astype(f32).astype(bf16)
    base = 16 * (it >> 2) + 2 * (it & 3)
    for h in range(2):
        gather_v[h * half_tokens : (h + 1) * half_tokens, :] = (il == base + h).astype(f32).astype(bf16)
    opw[...] = jnp.zeros(opw.shape, bf16)
    shift = pl.multiple_of(v * step % 128, 16)
    opw[pl.ds(shift, step), :] = out_proj_t[...]

    ids = jnp.concatenate([tids[...], mids[...]], axis=1)
    ip = iota((8, tokens), 0)
    digits = jnp.where(
        ip == 0, ids & 63, jnp.where(ip == 1, (ids >> 6) & 63, jnp.where(ip == 2, ids >> 12, 0))
    )
    im = iota((tokens, tokens), 0)
    il = iota((tokens, tokens), 1)
    jl = il & 7
    src = 4 * (il >> 3) + jnp.where(jl < 4, jl, jl - 4 + half_tokens)
    placed = nn(digits.astype(f32).astype(bf16), (im == src).astype(f32).astype(bf16))
    target = (placed[0:1] + 64.0 * placed[1:2] + 4096.0 * placed[2:3]).astype(jnp.int32)
    lane = iota((1, tokens), 1)
    share = jnp.where((lane & 7) < 4, loss_scale, loss_scale * mtp_share).astype(f32)
    vocab_id = iota((2 * vb, tokens), 0) + (v * rows + 2 * chip) * vb

    w_copy.wait()
    remote(w2.at[1 - c], w2.at[1 - c], sib_s.at[1], sib_r.at[1], sibling).wait_recv()

    def ag_wait(i, carry):
        xx = lax.rem(i, nx)
        yy = i // nx
        bx = hid.at[lax.rem(y + 1 + yy, ny), xx, :, hx]
        remote(bx, bx, ag_s1.at[0, 0], ag_r.at[0, lax.rem(y + 1 + yy, ny), xx], sibling).wait_recv()
        return carry

    def ag_wait_y(i, carry):
        yy = lax.rem(i, ny)
        xx = lax.rem(x + 1 + i // ny, nx)
        by = hid.at[yy, xx, :, hy]
        remote(by, by, ag_s1.at[1, 0], ag_r.at[1, yy, xx], sibling).wait_recv()
        return carry

    lax.fori_loop(0, nx * (ny - 1), ag_wait, 0)
    lax.fori_loop(0, ny * (nx - 1), ag_wait_y, 0)
    lt_own[...] = nt(w2[...].reshape(2 * vb, dh), hid[...].reshape(tokens, dh))
    lt_copy = remote(lt_own, lt_sib, sib_s.at[2], sib_r.at[2], sibling)
    lt_copy.start()
    lt_copy.wait()
    logits = lt_own[...] + lt_sib[...]
    onehot = (vocab_id == target).astype(f32)
    top_chip = jnp.max(logits, axis=0, keepdims=True)
    e = jnp.exp(logits - top_chip)
    lt_sib[...] = e
    i8 = iota((8, tokens), 0)
    stats = jnp.where(
        i8 == 0,
        top_chip,
        jnp.where(
            i8 == 1,
            jnp.sum(e, axis=0, keepdims=True),
            jnp.where(
                i8 == 2,
                jnp.sum(e * logits, axis=0, keepdims=True),
                jnp.where(i8 == 3, jnp.sum(onehot * logits, axis=0, keepdims=True), 0.0),
            ),
        ),
    )

    def merge(slots, count):
        top = slots[0][0:1]
        for s in range(1, count):
            top = jnp.maximum(top, slots[s][0:1])
        acc = jnp.zeros((8, tokens), f32)
        for s in range(count):
            tile = slots[s]
            weight = jnp.exp(tile[0:1] - top)
            acc = acc + jnp.where(i8 == 3, tile, tile * weight)
        return jnp.where(i8 == 0, top, acc)

    def pst_copy(i):
        cc = lax.rem(chip + i, chips)
        return remote(st_plane.at[chip], st_plane.at[chip], pst_s.at[i], pst_r.at[chip], (v, 2 * cc + c))

    def pst_start(i, carry):
        pst_copy(i).start()
        return carry

    def pst_wait(i, carry):
        cc = lax.rem(chip + i, chips)
        remote(st_plane.at[cc], st_plane.at[cc], pst_s.at[0], pst_r.at[cc], sibling).wait_recv()
        pst_copy(i).wait_send()
        return carry

    st_plane[chip] = stats
    lax.fori_loop(1, chips, pst_start, 0)
    lax.fori_loop(1, chips, pst_wait, 0)

    def zst_copy(i):
        zz = lax.rem(v + i, nz)
        return remote(st_z.at[v], st_z.at[v], zst_s.at[i], zst_r.at[v], (zz, r))

    def zst_start(i, carry):
        zst_copy(i).start()
        return carry

    def zst_wait(i, carry):
        zz = lax.rem(v + i, nz)
        remote(st_z.at[zz], st_z.at[zz], zst_s.at[0], zst_r.at[zz], sibling).wait_recv()
        zst_copy(i).wait_send()
        return carry

    st_z[v] = merge(st_plane, chips)
    lax.fori_loop(1, nz, zst_start, 0)
    lax.fori_loop(1, nz, zst_wait, 0)
    whole = merge(st_z, nz)
    top, total = whole[0:1], whole[1:2]
    grads = lt_sib[...] * (share * jnp.exp(top_chip - top) / total) - share * onehot
    gt[...] = grads.astype(bf16)
    dot = share * (whole[2:3] / total - whole[3:4])
    il = iota((8, tokens), 1)
    dot_mean = (
        jnp.sum(jnp.where(il == 8 * r + iota((8, tokens), 0), dot, 0.0), axis=1, keepdims=True) / width
    )

    grads_t = jnp.transpose(grads).astype(bf16)
    tile = 256 if dh % 256 == 0 else dh
    for n in range(0, dh, tile):
        res = nn(grads_t, w2[:, :, n : n + tile].reshape(2 * vb, tile))
        part[:, :, :, n : n + tile] = res.astype(bf16).reshape(ny, nx, 16, tile)
        if n + tile == xw or (n < xw < n + tile):
            for j in range(1, nx):
                xx = lax.rem(x + j, nx)
                push(remote(part.at[:, xx, :, hx], rx.at[j - 1], rs_s1.at[0, j - 1], rs_r1.at[0, j - 1], at(y, xx, c)))
    for j in range(1, ny):
        yy = lax.rem(y + j, ny)
        push(remote(part.at[yy, :, :, hy], ry.at[j - 1], rs_s1.at[1, j - 1], rs_r1.at[1, j - 1], at(yy, x, c)))

    for n in range(0, dh, tile):
        head_out[:, n : n + tile] = nn(
            gt[pl.ds(pl.multiple_of((1 - c) * vb, 16), vb), :], hid[:, :, :, n : n + tile].reshape(tokens, tile)
        ).astype(bf16)
    head_copy = remote(head_out, o_head.at[:, own_cols], sib_s.at[3], sib_r.at[3], sibling)
    head_copy.start()
    for n in range(0, dh, tile):
        o_head[:, pl.ds(pl.multiple_of(c * dh + n, 128), tile)] = nn(
            gt[pl.ds(pl.multiple_of(c * vb, 16), vb), :], hid[:, :, :, n : n + tile].reshape(tokens, tile)
        ).astype(bf16)

    def a2a_wait(i, carry):
        rr = lax.rem(r + i, rows)
        remote(a2a_r.at[rr], a2a_r.at[rr], a2a_ss.at[0], a2a_rs.at[rr], sibling).wait_recv()
        a2a_copy(i).wait_send()
        return carry

    lax.fori_loop(1, rows, a2a_wait, 0)
    received = a2a_r[...].reshape(rows * 16, hd)
    for h in range(2):
        vals[:, h * hd : (h + 1) * hd] = nn(
            gather_v[h * half_tokens : (h + 1) * half_tokens, :], received
        ).astype(bf16)

    for j in range(1, nx):
        remote(rx.at[j - 1], rx.at[j - 1], rs_s1.at[0, 0], rs_r1.at[0, j - 1], sibling).wait_recv()
    for jj in range(ny):
        j = (jj + 1) % ny
        yy = lax.rem(y + j, ny)
        total_x = part[yy, x, :, 0:xw].astype(f32)
        for k in range(nx - 1):
            total_x = total_x + rx[k, yy].astype(f32)
        for d in range(2):
            axs[j, d] = fold(total_x[8 * d : 8 * d + 8])
        if j > 0:
            for d in range(2):
                push(remote(axs.at[j, d], rx2.at[j, c], rs_s2.at[0, j, d], rs_r2.at[0, j, c], at(yy, x, d)))
        else:
            push(remote(axs.at[0, 1 - c], rx2.at[0, c], rs_s2.at[0, 0, 0], rs_r2.at[0, 0, c], sibling))
            rx2[0, c] = axs[0, c]
    for j in range(1, ny):
        remote(ry.at[j - 1], ry.at[j - 1], rs_s1.at[1, 0], rs_r1.at[1, j - 1], sibling).wait_recv()
    for jj in range(nx):
        j = (jj + 1) % nx
        xx = lax.rem(x + j, nx)
        total_y = part[y, xx, :, xw:dh].astype(f32)
        for k in range(ny - 1):
            total_y = total_y + ry[k, xx].astype(f32)
        for d in range(2):
            ays[j, d] = fold(total_y[8 * d : 8 * d + 8])
        if j > 0:
            for d in range(2):
                push(remote(ays.at[j, d], ry2.at[j, c], rs_s2.at[1, j, d], rs_r2.at[1, j, c], at(y, xx, d)))
        else:
            push(remote(ays.at[0, 1 - c], ry2.at[0, c], rs_s2.at[1, 0, 0], rs_r2.at[1, 0, c], sibling))
            ry2[0, c] = ays[0, c]
    for buf, axis, count, wid, off in ((rx2, 0, ny, xw, 0), (ry2, 1, nx, yw, xw)):
        for j in range(1, count):
            for s in range(2):
                remote(buf.at[j, s], buf.at[j, s], rs_s2.at[axis, 0, 0], rs_r2.at[axis, j, s], sibling).wait_recv()
        remote(buf.at[0, 1 - c], buf.at[0, 1 - c], rs_s2.at[axis, 0, 0], rs_r2.at[axis, 0, 1 - c], sibling).wait_recv()
        for s in range(2):
            acc = buf[0, s].astype(f32)
            for j in range(1, count):
                acc = acc + buf[j, s].astype(f32)
            sum8[:, s * dh + off : s * dh + off + wid] = unfold(acc)

    for zz in range(nz):
        zs[zz] = fold(sum8[:, starts[zz] : starts[zz] + LANES])

    def zrs_copy(i):
        zz = lax.rem(v + i, nz)
        return remote(zs.at[zz], zr.at[v], zrs_s.at[i], zrs_r.at[v], (zz, r))

    def zrs_start(i, carry):
        zrs_copy(i).start()
        return carry

    def zrs_wait(i, carry):
        zz = lax.rem(v + i, nz)
        remote(zr.at[zz], zr.at[zz], zrs_s.at[0], zrs_r.at[zz], sibling).wait_recv()
        zrs_copy(i).wait_send()
        return carry

    lax.fori_loop(1, nz, zrs_start, 0)
    zr[v] = zs[v]
    lax.fori_loop(1, nz, zrs_wait, 0)
    acc = zr[0].astype(f32)
    for zz in range(1, nz):
        acc = acc + zr[zz].astype(f32)
    grad = unfold(acc)

    cols = pl.ds(window, LANES)
    normed8 = st8[:, cols]
    scaled = grad * gain_row[:, cols]
    residual = inv8[:, 0:1] * (scaled - normed8 * dot_mean)
    gain_term = jnp.sum(grad * normed8, axis=0, keepdims=True)
    gain_high = gain_term.astype(bf16).astype(f32)
    row = iota((8, LANES), 0)
    po[...] = fold(
        jnp.where(
            row == 0, gain_high, jnp.where(row == 1, gain_term - gain_high, jnp.where(row < 4, 0.0, residual))
        )
    )

    def pag_copy(i):
        return remote(po, pr.at[r], pag_s.at[i], pag_r.at[r], (v, lax.rem(r + i, rows)))

    def pag_start(i, carry):
        pag_copy(i).start()
        return carry

    def pag_wait(i, carry):
        rr = lax.rem(r + i, rows)
        remote(pr.at[rr], pr.at[rr], pag_s.at[0], pag_r.at[rr], sibling).wait_recv()
        pag_copy(i).wait_send()
        return carry

    lax.fori_loop(1, rows, pag_start, 0)
    pr[r] = po[...]

    zo[v] = fold(jnp.where(row < 4, grad, residual))

    def zag_copy(i):
        return remote(zo.at[v], zo.at[v], zag_s.at[i], zag_r.at[v], (lax.rem(v + i, nz), r))

    def zag_start(i, carry):
        zag_copy(i).start()
        return carry

    def zag_wait(i, carry):
        zz = lax.rem(v + i, nz)
        remote(zo.at[zz], zo.at[zz], zag_s.at[0], zag_r.at[zz], sibling).wait_recv()
        zag_copy(i).wait_send()
        return carry

    lax.fori_loop(1, nz, zag_start, 0)
    lax.fori_loop(1, rows, pag_wait, 0)

    picked = nn(sel[...], pr[...].reshape(rows * 16, HALF))
    columns = jnp.concatenate([picked[0:half_tokens], picked[half_tokens:tokens]], axis=1)
    columns_b = columns.astype(bf16)
    attn_term = nn(columns_b, opw[...])
    for zz in range(nz):
        blk = attn_term[8 * zz : 8 * zz + 8]
        gs[zz] = fold(blk)

    def zga_copy(i):
        zz = lax.rem(v + i, nz)
        return remote(gs.at[zz], gr.at[v], zga_s.at[i], zga_r.at[v], (zz, r))

    def zga_start(i, carry):
        zga_copy(i).start()
        return carry

    def zga_wait(i, carry):
        zz = lax.rem(v + i, nz)
        remote(gr.at[zz], gr.at[zz], zga_s.at[0], zga_r.at[zz], sibling).wait_recv()
        zga_copy(i).wait_send()
        return carry

    lax.fori_loop(1, nz, zga_start, 0)
    gr[v] = gs[v]
    zg[v] = jnp.concatenate(
        [picked[tokens + k // 2 : tokens + k // 2 + 1, k % 2 * 128 : k % 2 * 128 + 128] for k in range(LANES // 128)],
        axis=0,
    )

    def zg_copy(i):
        return remote(zg.at[v], zg.at[v], zg_s.at[i], zg_r.at[v], (lax.rem(v + i, nz), r))

    def zg_start(i, carry):
        zg_copy(i).start()
        return carry

    def zg_wait(i, carry):
        zz = lax.rem(v + i, nz)
        remote(zg.at[zz], zg.at[zz], zg_s.at[0], zg_r.at[zz], sibling).wait_recv()
        zg_copy(i).wait_send()
        return carry

    lax.fori_loop(1, nz, zg_start, 0)

    proj_s[...] = nn(jnp.transpose(columns).astype(bf16), vals[...]).astype(bf16)
    o_proj_t[...] = proj_s[pl.ds(shift, step), :]

    lax.fori_loop(1, nz, zag_wait, 0)
    for zz in range(nz):
        block = unfold(zo[zz].astype(f32)).astype(bf16)
        o_trunk[:, starts[zz] : starts[zz] + LANES] = block[0:4]
        o_res[:, starts[zz] : starts[zz] + LANES] = block[4:8]
    lax.fori_loop(1, nz, zg_wait, 0)
    for zz in range(nz):
        o_gain[starts[zz] // 128 : (starts[zz] + LANES) // 128, :] = zg[zz]
    lax.fori_loop(1, nz, zga_wait, 0)
    acc = gr[0].astype(f32)
    for zz in range(1, nz):
        acc = acc + gr[zz].astype(f32)
    for h in range(2):
        attn_s[pl.ds(h, 8, stride=2), :] = acc[8 * h : 8 * h + 8]
    o_attn[...] = attn_s[...].astype(bf16)

    remote(head_out, o_head.at[:, sib_cols], sib_s.at[3], sib_r.at[3], sibling).wait_recv()
    head_copy.wait_send()
    tok_copy.wait_send()
    w_send.wait_send()
    for copy in sends:
        copy.wait_send()


def finish(*refs):
    count = len(refs) // 2
    copies = [pltpu.make_async_copy(refs[i], refs[count + i], refs[-1].at[i]) for i in range(count)]
    for copy in copies:
        copy.start()
    for copy in copies:
        copy.wait()


def local(dims, trunk_hidden, mtp_state, mtp_gain, head_weight, target_ids, mtp_target_ids, attn_values, out_proj):
    nx, ny, nz, width = dims
    rows = 2 * nx * ny
    tokens = 8 * rows
    vb = head_weight.shape[0]
    dh = width // 2
    xw = dh // 2
    yw = dh - xw
    step = out_proj.shape[1]
    heads, hd = attn_values.shape[1:]
    vmem = pltpu.VMEM
    dma = pltpu.SemaphoreType.DMA
    scratch = [
        vmem((4, width), bf16),
        vmem((4, width), bf16),
        vmem((width // 128, 128), bf16),
        vmem((1, tokens // 2), jnp.int32),
        vmem((1, tokens // 2), jnp.int32),
        vmem((4, heads, hd), bf16),
        vmem((step, 2 * hd), bf16),
        vmem((1, width), f32),
        vmem((8, width), f32),
        vmem((8, width), f32),
        vmem((8, 128), f32),
        vmem((8, dh), f32),
        vmem((2, vb, dh), bf16),
        vmem((ny, nx, 16, dh), bf16),
        vmem((2 * vb, tokens), f32),
        vmem((2 * vb, tokens), f32),
        vmem((nx * ny, 8, tokens), f32),
        vmem((nz, 8, tokens), f32),
        vmem((2 * vb, tokens), bf16),
        vmem((ny, nx, 16, dh), bf16),
        vmem((vb, dh), bf16),
        vmem((max(nx - 1, 1), ny, 16, xw), bf16),
        vmem((max(ny - 1, 1), nx, 16, yw), bf16),
        vmem((ny, 2, 16, xw // 2), bf16),
        vmem((nx, 2, 16, yw // 2), bf16),
        vmem((ny, 2, 16, xw // 2), bf16),
        vmem((nx, 2, 16, yw // 2), bf16),
        vmem((8, width), f32),
        vmem((nz, 16, HALF), bf16),
        vmem((nz, 16, HALF), bf16),
        vmem((nz, 16, HALF), bf16),
        vmem((16, HALF), bf16),
        vmem((rows, 16, HALF), bf16),
        vmem((tokens + 16, rows * 16), bf16),
        vmem((tokens, rows * 16), bf16),
        vmem((rows, 16, hd), bf16),
        vmem((rows, 16, hd), bf16),
        vmem((tokens // 2, 2 * hd), bf16),
        vmem((LANES, 2 * hd), bf16),
        vmem((nz, LANES // 128, 128), f32),
        vmem((nz, 16, hd), bf16),
        vmem((nz, 16, hd), bf16),
        vmem((LANES, 2 * hd), bf16),
        vmem((16, hd), f32),
        dma((8,)),
        dma((4,)),
        dma((4,)),
        dma((2, 3)),
        dma((2, 4, 3)),
        dma((2, ny, nx)),
        dma((nx * ny,)),
        dma((nx * ny,)),
        dma((nz,)),
        dma((nz,)),
        dma((2, 3)),
        dma((2, 3)),
        dma((2, 4, 2)),
        dma((2, 4, 2)),
        dma((nz,)),
        dma((nz,)),
        dma((nz,)),
        dma((nz,)),
        dma((rows,)),
        dma((rows,)),
        dma((rows,)),
        dma((rows,)),
        dma((nz,)),
        dma((nz,)),
        dma((nz,)),
        dma((nz,)),
    ]
    in_vmem = pl.BlockSpec(memory_space=pltpu.VMEM)
    in_hbm = pl.BlockSpec(memory_space=pl.ANY)
    shape = jax.ShapeDtypeStruct
    shapes = [
        shape((4, width), bf16),
        shape((4, width), bf16),
        shape((width // 128, 128), f32),
        shape((vb, width), bf16),
        shape((16, hd), bf16),
        shape((step, 2 * hd), bf16),
    ]
    results = pl.pallas_call(
        functools.partial(kernel, dims),
        out_shape=shapes,
        in_specs=[pl.BlockSpec(memory_space=pltpu.HBM)] * 8,
        out_specs=[in_vmem] * 6,
        scratch_shapes=scratch,
        compiler_params=pltpu.CompilerParams(
            collective_id=0, has_side_effects=True, vmem_limit_bytes=60 * 2**20
        ),
        name="head_backward",
    )(
        trunk_hidden,
        mtp_state,
        mtp_gain.reshape(width // 128, 128),
        head_weight,
        target_ids.reshape(1, -1),
        mtp_target_ids.reshape(1, -1),
        attn_values,
        out_proj.T,
    )
    trunk_out, res_out, gain_out, head_out, attn_out, proj_out = pl.pallas_call(
        finish,
        out_shape=shapes,
        in_specs=[in_hbm] * len(shapes),
        out_specs=[in_hbm] * len(shapes),
        scratch_shapes=[dma((len(shapes),))],
        compiler_params=pltpu.CompilerParams(vmem_limit_bytes=60 * 2**20),
        name="results",
    )(*results)
    grad_attn = attn_out.reshape(8, 2, hd)
    return (trunk_out, res_out, gain_out.reshape(width), head_out, grad_attn, proj_out.T)


def solution(mesh):
    nz, rows = mesh.shape["vocab"], mesh.shape["rows"]
    nx = {32: 4, 8: 2, 2: 1}[rows]

    def run(*args):
        dims = (nx, rows // 2 // nx, nz, args[0].shape[1])
        return local(dims, *args)

    return jax.shard_map(
        run,
        mesh=mesh,
        in_specs=(
            P("rows", None),
            P("rows", None),
            P(),
            P(("vocab", "rows"), None),
            P(),
            P(),
            P("rows", None, None),
            P("rows", "vocab"),
        ),
        out_specs=(
            P("rows", None),
            P("rows", None),
            P(),
            P(("vocab", "rows"), None),
            P("vocab", "rows", None),
            P("rows", "vocab"),
        ),
        check_vma=False,
    )
```

```python
import functools

import jax
import jax.numpy as jnp
from jax import lax
from jax.experimental import pallas as pl
from jax.experimental.pallas import tpu as pltpu
from jax.sharding import PartitionSpec as P

loss_scale = 8.0
mtp_share = 0.3
norm_eps = 1e-06
f32 = jnp.float32
bf16 = jnp.bfloat16
LANES = 512
HALF = LANES // 2


def nn(a, b):
    return lax.dot_general(a, b, (((1,), (0,)), ((), ())), preferred_element_type=f32)


def nt(a, b):
    return lax.dot_general(a, b, (((1,), (1,)), ((), ())), preferred_element_type=f32)


def iota(shape, axis):
    return lax.broadcasted_iota(jnp.int32, shape, axis)


def fold(block):
    w = block.shape[1] // 2
    return jnp.concatenate([block[:, :w], block[:, w:]], axis=0).astype(bf16)


def unfold(block):
    return jnp.concatenate([block[:8], block[8:]], axis=1)


def remote(src, dst, send, recv, device):
    return pltpu.make_async_remote_copy(
        src_ref=src,
        dst_ref=dst,
        send_sem=send,
        recv_sem=recv,
        device_id=device,
        device_id_type=pl.DeviceIdType.MESH,
    )


def kernel(
    dims,
    trunk_h, state_h, gain_h, w_hbm, tids_h, mids_h, attn_h, out_proj_h,
    o_trunk, o_res, o_gain, o_head, o_attn, o_proj_t,
    trunk, state, gain, tids, mids, attn, out_proj_t, gain_row, own8, st8, inv8, sib8, w2, hid, lt_own, lt_sib, st_plane, st_z,
    gt, part, head_out, rx, ry, axs, ays, rx2, ry2, sum8, zs, zr, zo, po, pr, sel, gather_v,
    a2a_s, a2a_r, vals, opw, zg, gs, gr, proj_s, attn_s,
    cp_sem, sib_s, sib_r, ag_s1, ag_s2, ag_r, pst_s, pst_r, zst_s, zst_r,
    rs_s1, rs_r1, rs_s2, rs_r2, zrs_s, zrs_r, zag_s, zag_r, pag_s, pag_r,
    a2a_ss, a2a_rs, zg_s, zg_r, zga_s, zga_r,
):
    nx, ny, nz, width = dims
    rows = 2 * nx * ny
    chips = nx * ny
    tokens = 16 * chips
    half_tokens = tokens // 2
    vb = w_hbm.shape[0]
    dh = width // 2
    xw = dh // 2
    yw = dh - xw
    heads, hd = attn.shape[1:]
    step = width // nz
    starts = [zz * step // 128 * 128 for zz in range(nz)]

    v = lax.axis_index("vocab")
    r = lax.axis_index("rows")
    c = lax.rem(r, 2)
    chip = r // 2
    x = lax.rem(chip, nx)
    y = chip // nx
    sibling = (v, r + 1 - 2 * c)
    window = pl.multiple_of(v * step // 128 * 128, 128)

    def at(yy, xx, core):
        return (v, (yy * nx + xx) * 2 + core)

    own_cols = pl.ds(pl.multiple_of(c * dh, 128), dh)
    sib_cols = pl.ds(pl.multiple_of((1 - c) * dh, 128), dh)
    w_copy = pltpu.make_async_copy(w_hbm.at[:, own_cols], w2.at[c], cp_sem.at[0])
    loads = [
        pltpu.make_async_copy(src, dst, cp_sem.at[1 + i])
        for i, (src, dst) in enumerate(
            ((state_h, state), (gain_h, gain), (trunk_h, trunk), (tids_h, tids), (mids_h, mids), (attn_h, attn), (out_proj_h, out_proj_t))
        )
    ]
    for load in loads:
        load.start()
    w_copy.start()

    bar = pltpu.get_barrier_semaphore()

    def greet_rows(i, carry):
        pl.semaphore_signal(
            bar, inc=1, device_id=(v, lax.rem(r + i, rows)), device_id_type=pl.DeviceIdType.MESH
        )
        return carry

    def greet_vocab(i, carry):
        pl.semaphore_signal(
            bar, inc=1, device_id=(lax.rem(v + i, nz), r), device_id_type=pl.DeviceIdType.MESH
        )
        return carry

    lax.fori_loop(1, rows, greet_rows, 0)
    lax.fori_loop(1, nz, greet_vocab, 0)

    for load in loads[:3]:
        load.wait()
    sv = state[...].astype(f32)
    inverse = lax.rsqrt(jnp.mean(sv * sv, axis=-1, keepdims=True) + norm_eps)
    normed = sv * inverse
    for k in range(width // 128):
        gain_row[0:1, k * 128 : (k + 1) * 128] = gain[k : k + 1, :].astype(f32)
    own8[0:4, :] = trunk[...].astype(f32)
    own8[4:8, :] = (normed * gain_row[...]).astype(bf16).astype(f32)
    st8[0:4, :] = jnp.zeros((4, width), f32)
    st8[4:8, :] = normed
    inv8[0:4, :] = jnp.zeros((4, 128), f32)
    inv8[4:8, :] = jnp.broadcast_to(inverse, (4, 128))

    pl.semaphore_wait(bar, rows - 1 + nz - 1)

    tok_copy = remote(own8.at[:, sib_cols], sib8, sib_s.at[0], sib_r.at[0], sibling)
    tok_copy.start()
    w_send = remote(w_hbm.at[:, sib_cols], w2.at[c], sib_s.at[1], sib_r.at[1], sibling)
    w_send.start()
    mine = own8[:, own_cols]
    tok_copy.wait_recv()
    other = sib8[...]
    first = c == 0
    hid[y, x] = jnp.concatenate(
        [jnp.where(first, mine, other), jnp.where(first, other, mine)], axis=0
    ).astype(bf16)

    hx = pl.ds(0, xw)
    hy = pl.ds(xw, yw)
    sends = []

    def push(copy):
        copy.start()
        sends.append(copy)

    for j in range(1, nx):
        blk = hid.at[y, x, :, hx]
        push(remote(blk, blk, ag_s1.at[0, j - 1], ag_r.at[0, y, x], at(y, lax.rem(x + j, nx), c)))
    for j in range(1, ny):
        blk = hid.at[y, x, :, hy]
        push(remote(blk, blk, ag_s1.at[1, j - 1], ag_r.at[1, y, x], at(lax.rem(y + j, ny), x, c)))

    order = {4: (0, 1, 3, 2), 2: (0, 1), 1: (0,)}
    for i in range(max(nx, ny)):
        if i < nx:
            xx = lax.rem(x + order[nx][i], nx)
            blk = hid.at[y, xx, :, hx]
            if i > 0:
                remote(blk, blk, ag_s1.at[0, 0], ag_r.at[0, y, xx], sibling).wait_recv()
            for j in range(1, ny):
                push(remote(blk, blk, ag_s2.at[0, i, j - 1], ag_r.at[0, y, xx], at(lax.rem(y + j, ny), x, c)))
        if i < ny:
            yy = lax.rem(y + order[ny][i], ny)
            blk = hid.at[yy, x, :, hy]
            if i > 0:
                remote(blk, blk, ag_s1.at[1, 0], ag_r.at[1, yy, x], sibling).wait_recv()
            for j in range(1, nx):
                push(remote(blk, blk, ag_s2.at[1, i, j - 1], ag_r.at[1, yy, x], at(y, lax.rem(x + j, nx), c)))

    for load in loads[3:]:
        load.wait()
    ir = iota((rows * 16, 4 * heads), 0)
    im = iota((rows * 16, 4 * heads), 1)
    kk = ir & 15
    pick = (kk < 8) & (im == (kk >> 1) * heads + 2 * (ir >> 4) + (kk & 1))
    a2a_s[...] = (
        nn(pick.astype(f32).astype(bf16), attn[...].reshape(4 * heads, hd)).astype(bf16).reshape(rows, 16, hd)
    )

    def a2a_copy(i):
        rr = lax.rem(r + i, rows)
        return remote(a2a_s.at[rr], a2a_r.at[r], a2a_ss.at[i], a2a_rs.at[r], (v, rr))

    def a2a_start(i, carry):
        a2a_copy(i).start()
        return carry

    lax.fori_loop(1, rows, a2a_start, 0)
    a2a_r[r] = a2a_s[r]

    it = iota((half_tokens, rows * 16), 0)
    il = iota((half_tokens, rows * 16), 1)
    base = 16 * (it >> 2) + (it & 3)
    sel[0:half_tokens, :] = (il == base + 4).astype(f32).astype(bf16)
    sel[half_tokens:tokens, :] = (il == base + 12).astype(f32).astype(bf16)
    ig = iota((16, rows * 16), 0)
    kg = iota((16, rows * 16), 1) & 15
    sel[tokens : tokens + 16, :] = (
        ((ig == 0) & (kg < 2)) | ((ig == 1) & (kg >= 8) & (kg < 10))
    ).astype(f32).astype(bf16)
    base = 16 * (it >> 2) + 2 * (it & 3)
    for h in range(2):
        gather_v[h * half_tokens : (h + 1) * half_tokens, :] = (il == base + h).astype(f32).astype(bf16)
    opw[...] = jnp.zeros(opw.shape, bf16)
    shift = pl.multiple_of(v * step % 128, 16)
    opw[pl.ds(shift, step), :] = out_proj_t[...]

    ids = jnp.concatenate([tids[...], mids[...]], axis=1)
    ip = iota((8, tokens), 0)
    digits = jnp.where(
        ip == 0, ids & 63, jnp.where(ip == 1, (ids >> 6) & 63, jnp.where(ip == 2, ids >> 12, 0))
    )
    im = iota((tokens, tokens), 0)
    il = iota((tokens, tokens), 1)
    jl = il & 7
    src = 4 * (il >> 3) + jnp.where(jl < 4, jl, jl - 4 + half_tokens)
    placed = nn(digits.astype(f32).astype(bf16), (im == src).astype(f32).astype(bf16))
    target = (placed[0:1] + 64.0 * placed[1:2] + 4096.0 * placed[2:3]).astype(jnp.int32)
    lane = iota((1, tokens), 1)
    share = jnp.where((lane & 7) < 4, loss_scale, loss_scale * mtp_share).astype(f32)
    vocab_id = iota((2 * vb, tokens), 0) + (v * rows + 2 * chip) * vb

    w_copy.wait()
    remote(w2.at[1 - c], w2.at[1 - c], sib_s.at[1], sib_r.at[1], sibling).wait_recv()

    def ag_wait(i, carry):
        xx = lax.rem(i, nx)
        yy = i // nx
        bx = hid.at[lax.rem(y + 1 + yy, ny), xx, :, hx]
        remote(bx, bx, ag_s1.at[0, 0], ag_r.at[0, lax.rem(y + 1 + yy, ny), xx], sibling).wait_recv()
        return carry

    def ag_wait_y(i, carry):
        yy = lax.rem(i, ny)
        xx = lax.rem(x + 1 + i // ny, nx)
        by = hid.at[yy, xx, :, hy]
        remote(by, by, ag_s1.at[1, 0], ag_r.at[1, yy, xx], sibling).wait_recv()
        return carry

    lax.fori_loop(0, nx * (ny - 1), ag_wait, 0)
    lax.fori_loop(0, ny * (nx - 1), ag_wait_y, 0)
    lt_own[...] = nt(w2[...].reshape(2 * vb, dh), hid[...].reshape(tokens, dh))
    lt_copy = remote(lt_own, lt_sib, sib_s.at[2], sib_r.at[2], sibling)
    lt_copy.start()
    lt_copy.wait()
    logits = lt_own[...] + lt_sib[...]
    onehot = (vocab_id == target).astype(f32)
    top_chip = jnp.max(logits, axis=0, keepdims=True)
    e = jnp.exp(logits - top_chip)
    lt_sib[...] = e
    i8 = iota((4, tokens), 0)
    stats = jnp.where(
        i8 == 0,
        top_chip,
        jnp.where(
            i8 == 1,
            jnp.sum(e, axis=0, keepdims=True),
            jnp.where(
                i8 == 2,
                jnp.sum(e * logits, axis=0, keepdims=True),
                jnp.sum(onehot * logits, axis=0, keepdims=True),
            ),
        ),
    )

    def merge(slots, count):
        top = slots[0][0:1]
        for s in range(1, count):
            top = jnp.maximum(top, slots[s][0:1])
        acc = jnp.zeros((4, tokens), f32)
        for s in range(count):
            tile = slots[s]
            weight = jnp.exp(tile[0:1] - top)
            acc = acc + jnp.where(i8 == 3, tile, tile * weight)
        return jnp.where(i8 == 0, top, acc)

    def pst_copy(i):
        cc = lax.rem(chip + i, chips)
        return remote(st_plane.at[chip], st_plane.at[chip], pst_s.at[i], pst_r.at[chip], (v, 2 * cc + c))

    def pst_start(i, carry):
        pst_copy(i).start()
        return carry

    def pst_wait(i, carry):
        cc = lax.rem(chip + i, chips)
        remote(st_plane.at[cc], st_plane.at[cc], pst_s.at[0], pst_r.at[cc], sibling).wait_recv()
        pst_copy(i).wait_send()
        return carry

    st_plane[chip] = stats
    lax.fori_loop(1, chips, pst_start, 0)
    lax.fori_loop(1, chips, pst_wait, 0)

    def zst_copy(i):
        zz = lax.rem(v + i, nz)
        return remote(st_z.at[v], st_z.at[v], zst_s.at[i], zst_r.at[v], (zz, r))

    def zst_start(i, carry):
        zst_copy(i).start()
        return carry

    def zst_wait(i, carry):
        zz = lax.rem(v + i, nz)
        remote(st_z.at[zz], st_z.at[zz], zst_s.at[0], zst_r.at[zz], sibling).wait_recv()
        zst_copy(i).wait_send()
        return carry

    st_z[v] = merge(st_plane, chips)
    lax.fori_loop(1, nz, zst_start, 0)
    lax.fori_loop(1, nz, zst_wait, 0)
    whole = merge(st_z, nz)
    top, total = whole[0:1], whole[1:2]
    grads = lt_sib[...] * (share * jnp.exp(top_chip - top) / total) - share * onehot
    gt[...] = grads.astype(bf16)
    dot = share * (whole[2:3] / total - whole[3:4])
    il = iota((8, tokens), 1)
    dot_mean = (
        jnp.sum(jnp.where(il == 8 * r + iota((8, tokens), 0), dot, 0.0), axis=1, keepdims=True) / width
    )

    grads_t = jnp.transpose(grads).astype(bf16)
    tile = 256 if dh % 256 == 0 else dh
    for n in range(0, dh, tile):
        res = nn(grads_t, w2[:, :, n : n + tile].reshape(2 * vb, tile))
        part[:, :, :, n : n + tile] = res.astype(bf16).reshape(ny, nx, 16, tile)
        if n + tile == xw or (n < xw < n + tile):
            for j in range(1, nx):
                xx = lax.rem(x + j, nx)
                push(remote(part.at[:, xx, :, hx], rx.at[j - 1], rs_s1.at[0, j - 1], rs_r1.at[0, j - 1], at(y, xx, c)))
    for j in range(1, ny):
        yy = lax.rem(y + j, ny)
        push(remote(part.at[yy, :, :, hy], ry.at[j - 1], rs_s1.at[1, j - 1], rs_r1.at[1, j - 1], at(yy, x, c)))

    for n in range(0, dh, tile):
        head_out[:, n : n + tile] = nn(
            gt[pl.ds(pl.multiple_of((1 - c) * vb, 16), vb), :], hid[:, :, :, n : n + tile].reshape(tokens, tile)
        ).astype(bf16)
    head_copy = remote(head_out, o_head.at[:, own_cols], sib_s.at[3], sib_r.at[3], sibling)
    head_copy.start()
    for n in range(0, dh, tile):
        o_head[:, pl.ds(pl.multiple_of(c * dh + n, 128), tile)] = nn(
            gt[pl.ds(pl.multiple_of(c * vb, 16), vb), :], hid[:, :, :, n : n + tile].reshape(tokens, tile)
        ).astype(bf16)

    def a2a_wait(i, carry):
        rr = lax.rem(r + i, rows)
        remote(a2a_r.at[rr], a2a_r.at[rr], a2a_ss.at[0], a2a_rs.at[rr], sibling).wait_recv()
        a2a_copy(i).wait_send()
        return carry

    lax.fori_loop(1, rows, a2a_wait, 0)
    received = a2a_r[...].reshape(rows * 16, hd)
    for h in range(2):
        vals[:, h * hd : (h + 1) * hd] = nn(
            gather_v[h * half_tokens : (h + 1) * half_tokens, :], received
        ).astype(bf16)

    for j in range(1, nx):
        remote(rx.at[j - 1], rx.at[j - 1], rs_s1.at[0, 0], rs_r1.at[0, j - 1], sibling).wait_recv()
    for jj in range(ny):
        j = (jj + 1) % ny
        yy = lax.rem(y + j, ny)
        total_x = part[yy, x, :, 0:xw].astype(f32)
        for k in range(nx - 1):
            total_x = total_x + rx[k, yy].astype(f32)
        for d in range(2):
            axs[j, d] = fold(total_x[8 * d : 8 * d + 8])
        if j > 0:
            for d in range(2):
                push(remote(axs.at[j, d], rx2.at[j, c], rs_s2.at[0, j, d], rs_r2.at[0, j, c], at(yy, x, d)))
        else:
            push(remote(axs.at[0, 1 - c], rx2.at[0, c], rs_s2.at[0, 0, 0], rs_r2.at[0, 0, c], sibling))
            rx2[0, c] = axs[0, c]
    for j in range(1, ny):
        remote(ry.at[j - 1], ry.at[j - 1], rs_s1.at[1, 0], rs_r1.at[1, j - 1], sibling).wait_recv()
    for jj in range(nx):
        j = (jj + 1) % nx
        xx = lax.rem(x + j, nx)
        total_y = part[y, xx, :, xw:dh].astype(f32)
        for k in range(ny - 1):
            total_y = total_y + ry[k, xx].astype(f32)
        for d in range(2):
            ays[j, d] = fold(total_y[8 * d : 8 * d + 8])
        if j > 0:
            for d in range(2):
                push(remote(ays.at[j, d], ry2.at[j, c], rs_s2.at[1, j, d], rs_r2.at[1, j, c], at(y, xx, d)))
        else:
            push(remote(ays.at[0, 1 - c], ry2.at[0, c], rs_s2.at[1, 0, 0], rs_r2.at[1, 0, c], sibling))
            ry2[0, c] = ays[0, c]
    for buf, axis, count, wid, off in ((rx2, 0, ny, xw, 0), (ry2, 1, nx, yw, xw)):
        for j in range(1, count):
            for s in range(2):
                remote(buf.at[j, s], buf.at[j, s], rs_s2.at[axis, 0, 0], rs_r2.at[axis, j, s], sibling).wait_recv()
        remote(buf.at[0, 1 - c], buf.at[0, 1 - c], rs_s2.at[axis, 0, 0], rs_r2.at[axis, 0, 1 - c], sibling).wait_recv()
        for s in range(2):
            acc = buf[0, s].astype(f32)
            for j in range(1, count):
                acc = acc + buf[j, s].astype(f32)
            sum8[:, s * dh + off : s * dh + off + wid] = unfold(acc)

    for zz in range(nz):
        zs[zz] = fold(sum8[:, starts[zz] : starts[zz] + LANES])

    def zrs_copy(i):
        zz = lax.rem(v + i, nz)
        return remote(zs.at[zz], zr.at[v], zrs_s.at[i], zrs_r.at[v], (zz, r))

    def zrs_start(i, carry):
        zrs_copy(i).start()
        return carry

    def zrs_wait(i, carry):
        zz = lax.rem(v + i, nz)
        remote(zr.at[zz], zr.at[zz], zrs_s.at[0], zrs_r.at[zz], sibling).wait_recv()
        zrs_copy(i).wait_send()
        return carry

    lax.fori_loop(1, nz, zrs_start, 0)
    zr[v] = zs[v]
    lax.fori_loop(1, nz, zrs_wait, 0)
    acc = zr[0].astype(f32)
    for zz in range(1, nz):
        acc = acc + zr[zz].astype(f32)
    grad = unfold(acc)

    cols = pl.ds(window, LANES)
    normed8 = st8[:, cols]
    scaled = grad * gain_row[:, cols]
    residual = inv8[:, 0:1] * (scaled - normed8 * dot_mean)
    gain_term = jnp.sum(grad * normed8, axis=0, keepdims=True)
    gain_high = gain_term.astype(bf16).astype(f32)
    row = iota((8, LANES), 0)
    po[...] = fold(
        jnp.where(
            row == 0, gain_high, jnp.where(row == 1, gain_term - gain_high, jnp.where(row < 4, 0.0, residual))
        )
    )

    def pag_copy(i):
        return remote(po, pr.at[r], pag_s.at[i], pag_r.at[r], (v, lax.rem(r + i, rows)))

    def pag_start(i, carry):
        pag_copy(i).start()
        return carry

    def pag_wait(i, carry):
        rr = lax.rem(r + i, rows)
        remote(pr.at[rr], pr.at[rr], pag_s.at[0], pag_r.at[rr], sibling).wait_recv()
        pag_copy(i).wait_send()
        return carry

    lax.fori_loop(1, rows, pag_start, 0)
    pr[r] = po[...]

    zo[v] = fold(jnp.where(row < 4, grad, residual))

    def zag_copy(i):
        return remote(zo.at[v], zo.at[v], zag_s.at[i], zag_r.at[v], (lax.rem(v + i, nz), r))

    def zag_start(i, carry):
        zag_copy(i).start()
        return carry

    def zag_wait(i, carry):
        zz = lax.rem(v + i, nz)
        remote(zo.at[zz], zo.at[zz], zag_s.at[0], zag_r.at[zz], sibling).wait_recv()
        zag_copy(i).wait_send()
        return carry

    lax.fori_loop(1, nz, zag_start, 0)
    lax.fori_loop(1, rows, pag_wait, 0)

    picked = nn(sel[...], pr[...].reshape(rows * 16, HALF))
    columns = jnp.concatenate([picked[0:half_tokens], picked[half_tokens:tokens]], axis=1)
    columns_b = columns.astype(bf16)
    attn_term = nn(columns_b, opw[...])
    for zz in range(nz):
        blk = attn_term[8 * zz : 8 * zz + 8]
        gs[zz] = fold(blk)

    def zga_copy(i):
        zz = lax.rem(v + i, nz)
        return remote(gs.at[zz], gr.at[v], zga_s.at[i], zga_r.at[v], (zz, r))

    def zga_start(i, carry):
        zga_copy(i).start()
        return carry

    def zga_wait(i, carry):
        zz = lax.rem(v + i, nz)
        remote(gr.at[zz], gr.at[zz], zga_s.at[0], zga_r.at[zz], sibling).wait_recv()
        zga_copy(i).wait_send()
        return carry

    lax.fori_loop(1, nz, zga_start, 0)
    gr[v] = gs[v]
    zg[v] = jnp.concatenate(
        [picked[tokens + k // 2 : tokens + k // 2 + 1, k % 2 * 128 : k % 2 * 128 + 128] for k in range(LANES // 128)],
        axis=0,
    )

    def zg_copy(i):
        return remote(zg.at[v], zg.at[v], zg_s.at[i], zg_r.at[v], (lax.rem(v + i, nz), r))

    def zg_start(i, carry):
        zg_copy(i).start()
        return carry

    def zg_wait(i, carry):
        zz = lax.rem(v + i, nz)
        remote(zg.at[zz], zg.at[zz], zg_s.at[0], zg_r.at[zz], sibling).wait_recv()
        zg_copy(i).wait_send()
        return carry

    lax.fori_loop(1, nz, zg_start, 0)

    proj_s[...] = nn(jnp.transpose(columns).astype(bf16), vals[...]).astype(bf16)
    o_proj_t[...] = proj_s[pl.ds(shift, step), :]

    lax.fori_loop(1, nz, zag_wait, 0)
    for zz in range(nz):
        block = unfold(zo[zz].astype(f32)).astype(bf16)
        o_trunk[:, starts[zz] : starts[zz] + LANES] = block[0:4]
        o_res[:, starts[zz] : starts[zz] + LANES] = block[4:8]
    lax.fori_loop(1, nz, zg_wait, 0)
    for zz in range(nz):
        o_gain[starts[zz] // 128 : (starts[zz] + LANES) // 128, :] = zg[zz]
    lax.fori_loop(1, nz, zga_wait, 0)
    acc = gr[0].astype(f32)
    for zz in range(1, nz):
        acc = acc + gr[zz].astype(f32)
    for h in range(2):
        attn_s[pl.ds(h, 8, stride=2), :] = acc[8 * h : 8 * h + 8]
    o_attn[...] = attn_s[...].astype(bf16)

    remote(head_out, o_head.at[:, sib_cols], sib_s.at[3], sib_r.at[3], sibling).wait_recv()
    head_copy.wait_send()
    tok_copy.wait_send()
    w_send.wait_send()
    for copy in sends:
        copy.wait_send()


def finish(*refs):
    sources, targets, held, sem_in, sem_out = refs[0:6], refs[6:12], refs[12:18], refs[18], refs[19]
    pieces = []
    for src, dst, buf in zip(sources, targets, held):
        rows = src.shape[0]
        cut = rows // 3 if rows % 48 == 0 else rows
        for at in range(0, rows, cut):
            pieces.append((src.at[at : at + cut], dst.at[at : at + cut], buf.at[at : at + cut]))
    pieces.sort(key=lambda piece: -piece[0].shape[0] * piece[0].shape[1])
    loads = [pltpu.make_async_copy(src, buf, sem_in.at[i]) for i, (src, _, buf) in enumerate(pieces)]
    stores = [pltpu.make_async_copy(buf, dst, sem_out.at[i]) for i, (_, dst, buf) in enumerate(pieces)]
    for load in loads:
        load.start()
    for load, store in zip(loads, stores):
        load.wait()
        store.start()
    for store in stores:
        store.wait()


def local(dims, trunk_hidden, mtp_state, mtp_gain, head_weight, target_ids, mtp_target_ids, attn_values, out_proj):
    nx, ny, nz, width = dims
    rows = 2 * nx * ny
    tokens = 8 * rows
    vb = head_weight.shape[0]
    dh = width // 2
    xw = dh // 2
    yw = dh - xw
    step = out_proj.shape[1]
    heads, hd = attn_values.shape[1:]
    vmem = pltpu.VMEM
    dma = pltpu.SemaphoreType.DMA
    scratch = [
        vmem((4, width), bf16),
        vmem((4, width), bf16),
        vmem((width // 128, 128), bf16),
        vmem((1, tokens // 2), jnp.int32),
        vmem((1, tokens // 2), jnp.int32),
        vmem((4, heads, hd), bf16),
        vmem((step, 2 * hd), bf16),
        vmem((1, width), f32),
        vmem((8, width), f32),
        vmem((8, width), f32),
        vmem((8, 128), f32),
        vmem((8, dh), f32),
        vmem((2, vb, dh), bf16),
        vmem((ny, nx, 16, dh), bf16),
        vmem((2 * vb, tokens), f32),
        vmem((2 * vb, tokens), f32),
        vmem((nx * ny, 4, tokens), f32),
        vmem((nz, 4, tokens), f32),
        vmem((2 * vb, tokens), bf16),
        vmem((ny, nx, 16, dh), bf16),
        vmem((vb, dh), bf16),
        vmem((max(nx - 1, 1), ny, 16, xw), bf16),
        vmem((max(ny - 1, 1), nx, 16, yw), bf16),
        vmem((ny, 2, 16, xw // 2), bf16),
        vmem((nx, 2, 16, yw // 2), bf16),
        vmem((ny, 2, 16, xw // 2), bf16),
        vmem((nx, 2, 16, yw // 2), bf16),
        vmem((8, width), f32),
        vmem((nz, 16, HALF), bf16),
        vmem((nz, 16, HALF), bf16),
        vmem((nz, 16, HALF), bf16),
        vmem((16, HALF), bf16),
        vmem((rows, 16, HALF), bf16),
        vmem((tokens + 16, rows * 16), bf16),
        vmem((tokens, rows * 16), bf16),
        vmem((rows, 16, hd), bf16),
        vmem((rows, 16, hd), bf16),
        vmem((tokens // 2, 2 * hd), bf16),
        vmem((LANES, 2 * hd), bf16),
        vmem((nz, LANES // 128, 128), f32),
        vmem((nz, 16, hd), bf16),
        vmem((nz, 16, hd), bf16),
        vmem((LANES, 2 * hd), bf16),
        vmem((16, hd), f32),
        dma((8,)),
        dma((4,)),
        dma((4,)),
        dma((2, 3)),
        dma((2, 4, 3)),
        dma((2, ny, nx)),
        dma((nx * ny,)),
        dma((nx * ny,)),
        dma((nz,)),
        dma((nz,)),
        dma((2, 3)),
        dma((2, 3)),
        dma((2, 4, 2)),
        dma((2, 4, 2)),
        dma((nz,)),
        dma((nz,)),
        dma((nz,)),
        dma((nz,)),
        dma((rows,)),
        dma((rows,)),
        dma((rows,)),
        dma((rows,)),
        dma((nz,)),
        dma((nz,)),
        dma((nz,)),
        dma((nz,)),
    ]
    in_vmem = pl.BlockSpec(memory_space=pltpu.VMEM)
    in_hbm = pl.BlockSpec(memory_space=pl.ANY)
    shape = jax.ShapeDtypeStruct
    shapes = [
        shape((4, width), bf16),
        shape((4, width), bf16),
        shape((width // 128, 128), f32),
        shape((vb, width), bf16),
        shape((16, hd), bf16),
        shape((step, 2 * hd), bf16),
    ]
    results = pl.pallas_call(
        functools.partial(kernel, dims),
        out_shape=shapes,
        in_specs=[pl.BlockSpec(memory_space=pltpu.HBM)] * 8,
        out_specs=[in_vmem] * 6,
        scratch_shapes=scratch,
        compiler_params=pltpu.CompilerParams(
            collective_id=0, has_side_effects=True, vmem_limit_bytes=60 * 2**20
        ),
        name="head_backward",
    )(
        trunk_hidden,
        mtp_state,
        mtp_gain.reshape(width // 128, 128),
        head_weight,
        target_ids.reshape(1, -1),
        mtp_target_ids.reshape(1, -1),
        attn_values,
        out_proj.T,
    )
    trunk_out, res_out, gain_out, head_out, attn_out, proj_out = pl.pallas_call(
        finish,
        out_shape=shapes,
        in_specs=[in_hbm] * len(shapes),
        out_specs=[in_hbm] * len(shapes),
        scratch_shapes=[vmem(s.shape, s.dtype) for s in shapes] + [dma((8,)), dma((8,))],
        compiler_params=pltpu.CompilerParams(vmem_limit_bytes=60 * 2**20),
        name="results",
    )(*results)
    grad_attn = attn_out.reshape(8, 2, hd)
    return (trunk_out, res_out, gain_out.reshape(width), head_out, grad_attn, proj_out.T)


def solution(mesh):
    nz, rows = mesh.shape["vocab"], mesh.shape["rows"]
    nx = {32: 4, 8: 2, 2: 1}[rows]

    def run(*args):
        dims = (nx, rows // 2 // nx, nz, args[0].shape[1])
        return local(dims, *args)

    return jax.shard_map(
        run,
        mesh=mesh,
        in_specs=(
            P("rows", None),
            P("rows", None),
            P(),
            P(("vocab", "rows"), None),
            P(),
            P(),
            P("rows", None, None),
            P("rows", "vocab"),
        ),
        out_specs=(
            P("rows", None),
            P("rows", None),
            P(),
            P(("vocab", "rows"), None),
            P("vocab", "rows", None),
            P("rows", "vocab"),
        ),
        check_vma=False,
    )
```

```python
import functools

import jax
import jax.numpy as jnp
from jax import lax
from jax.experimental import pallas as pl
from jax.experimental.pallas import tpu as pltpu
from jax.sharding import PartitionSpec as P

loss_scale = 8.0
mtp_share = 0.3
norm_eps = 1e-06
f32 = jnp.float32
bf16 = jnp.bfloat16
LANES = 512
HALF = LANES // 2


def nn(a, b):
    return lax.dot_general(a, b, (((1,), (0,)), ((), ())), preferred_element_type=f32)


def nt(a, b):
    return lax.dot_general(a, b, (((1,), (1,)), ((), ())), preferred_element_type=f32)


def iota(shape, axis):
    return lax.broadcasted_iota(jnp.int32, shape, axis)


def fold(block):
    w = block.shape[1] // 2
    return jnp.concatenate([block[:, :w], block[:, w:]], axis=0).astype(bf16)


def unfold(block):
    return jnp.concatenate([block[:8], block[8:]], axis=1)


def fold4(block):
    w = block.shape[1] // 4
    return jnp.concatenate([block[:, k * w : (k + 1) * w] for k in range(4)], axis=0).astype(bf16)


def unfold4(block):
    return jnp.concatenate([block[4 * k : 4 * k + 4] for k in range(4)], axis=1)


def remote(src, dst, send, recv, device):
    return pltpu.make_async_remote_copy(
        src_ref=src,
        dst_ref=dst,
        send_sem=send,
        recv_sem=recv,
        device_id=device,
        device_id_type=pl.DeviceIdType.MESH,
    )


def kernel(
    dims,
    trunk_h, state_h, gain_h, w_hbm, tids_h, mids_h, attn_h, out_proj_h,
    o_trunk, o_res, o_gain, o_head, o_attn, o_proj_t,
    trunk, state, gain, tids, mids, attn, out_proj_t,
    gain_row, own8, st4, inv4, sib8, w2, hx, hy, hid, lt_own, lt_sib, st_plane, st_z,
    gt, px, py, head_out, rx, ry, axs, ays, rx2, ry2, sum4, zs, zr, zo, po, pr, sel, gather_v,
    a2a_s, a2a_r, vals, opw, zg, gs, gr, proj_s, attn_s,
    cp_sem, sib_s, sib_r, ag_s1, ag_s2, ag_r, pst_s, pst_r, zst_s, zst_r,
    rs_s1, rs_r1, rs_s2, rs_r2, zrs_s, zrs_r, zag_s, zag_r, pag_s, pag_r,
    a2a_ss, a2a_rs, zg_s, zg_r, zga_s, zga_r,
):
    nx, ny, nz, width = dims
    rows = 2 * nx * ny
    chips = nx * ny
    tokens = 4 * rows
    vb = w_hbm.shape[0]
    dh = width // 2
    xw = dh // 2
    qw = xw // 2
    cut = -(-qw // 256) * 128
    heads, hd = attn.shape[1:]
    step = width // nz
    starts = [zz * step // 128 * 128 for zz in range(nz)]
    shares = (loss_scale * mtp_share, loss_scale)

    v = lax.axis_index("vocab")
    r = lax.axis_index("rows")
    c = lax.rem(r, 2)
    chip = r // 2
    x = lax.rem(chip, nx)
    y = chip // nx
    sibling = (v, r + 1 - 2 * c)
    window = pl.multiple_of(v * step // 128 * 128, 128)

    def at(yy, xx, core):
        return (v, (yy * nx + xx) * 2 + core)

    def arrived(ref, sem):
        remote(ref, ref, sib_s.at[0], sem, sibling).wait_recv()

    sends = []

    def push(copy):
        copy.start()
        sends.append(copy)

    def to_vocab(send, recv, source, target):
        def copy(i):
            zz = lax.rem(v + i, nz)
            return remote(source(zz), target(v), send.at[i], recv.at[v], (zz, r))

        def start(i, carry):
            copy(i).start()
            return carry

        def finish(i, carry):
            zz = lax.rem(v + i, nz)
            arrived(target(zz), recv.at[zz])
            copy(i).wait_send()
            return carry

        return (lambda: lax.fori_loop(1, nz, start, 0)), (lambda: lax.fori_loop(1, nz, finish, 0))

    def to_rows(send, recv, source, target):
        def copy(i):
            rr = lax.rem(r + i, rows)
            return remote(source(rr), target(r), send.at[i], recv.at[r], (v, rr))

        def start(i, carry):
            copy(i).start()
            return carry

        def finish(i, carry):
            rr = lax.rem(r + i, rows)
            arrived(target(rr), recv.at[rr])
            copy(i).wait_send()
            return carry

        return (lambda: lax.fori_loop(1, rows, start, 0)), (lambda: lax.fori_loop(1, rows, finish, 0))

    def to_chips(send, recv, buf):
        def copy(i):
            cc = lax.rem(chip + i, chips)
            return remote(buf.at[chip], buf.at[chip], send.at[i], recv.at[chip], (v, 2 * cc + c))

        def start(i, carry):
            copy(i).start()
            return carry

        def finish(i, carry):
            cc = lax.rem(chip + i, chips)
            arrived(buf.at[cc], recv.at[cc])
            copy(i).wait_send()
            return carry

        return (lambda: lax.fori_loop(1, chips, start, 0)), (lambda: lax.fori_loop(1, chips, finish, 0))

    own_cols = pl.ds(pl.multiple_of(c * dh, 128), dh)
    sib_cols = pl.ds(pl.multiple_of((1 - c) * dh, 128), dh)
    w_copy = pltpu.make_async_copy(w_hbm.at[:, own_cols], w2.at[c], cp_sem.at[0])
    loads = [
        pltpu.make_async_copy(src, dst, cp_sem.at[1 + i])
        for i, (src, dst) in enumerate(
            (
                (state_h, state), (gain_h, gain), (trunk_h, trunk), (tids_h, tids), (mids_h, mids),
                (attn_h, attn), (out_proj_h, out_proj_t),
            )
        )
    ]
    for load in loads:
        load.start()
    w_copy.start()

    bar = pltpu.get_barrier_semaphore()

    def greet_rows(i, carry):
        pl.semaphore_signal(
            bar, inc=1, device_id=(v, lax.rem(r + i, rows)), device_id_type=pl.DeviceIdType.MESH
        )
        return carry

    def greet_vocab(i, carry):
        pl.semaphore_signal(
            bar, inc=1, device_id=(lax.rem(v + i, nz), r), device_id_type=pl.DeviceIdType.MESH
        )
        return carry

    lax.fori_loop(1, nz, greet_vocab, 0)
    lax.fori_loop(1, rows, greet_rows, 0)

    for load in loads[:3]:
        load.wait()
    sv = state[...].astype(f32)
    inverse = lax.rsqrt(jnp.mean(sv * sv, axis=-1, keepdims=True) + norm_eps)
    normed = sv * inverse
    for k in range(width // 128):
        gain_row[0:1, k * 128 : (k + 1) * 128] = gain[k : k + 1, :].astype(f32)
    own8[0:4, :] = trunk[...].astype(f32)
    own8[4:8, :] = (normed * gain_row[...]).astype(bf16).astype(f32)
    st4[...] = normed
    inv4[...] = jnp.broadcast_to(inverse, (4, 128))

    pl.semaphore_wait(bar, rows - 1 + nz - 1)

    tok_copy = remote(own8.at[:, sib_cols], sib8, sib_s.at[0], sib_r.at[0], sibling)
    push(tok_copy)
    push(remote(w_hbm.at[:, sib_cols], w2.at[c], sib_s.at[1], sib_r.at[1], sibling))
    mine = own8[:, own_cols]
    tok_copy.wait_recv()
    other = sib8[...]
    first = c == 0
    low = jnp.where(first, mine, other)
    high = jnp.where(first, other, mine)
    for g, rng in ((0, slice(4, 8)), (1, slice(0, 4))):
        block = jnp.concatenate([low[rng], high[rng]], axis=0)
        hx[g, y, x] = fold(block[:, :xw])
        hy[g, y, x] = fold(block[:, xw:])

    def gather_first(g):
        for j in range(1, nx):
            blk = hx.at[g, y, x]
            push(remote(blk, blk, ag_s1.at[g, 0, j - 1], ag_r.at[g, 0, y, x], at(y, lax.rem(x + j, nx), c)))
        for j in range(1, ny):
            blk = hy.at[g, y, x]
            push(remote(blk, blk, ag_s1.at[g, 1, j - 1], ag_r.at[g, 1, y, x], at(lax.rem(y + j, ny), x, c)))

    order = {4: (0, 1, 3, 2), 2: (0, 1), 1: (0,)}

    def gather_second(g):
        for i in range(max(nx, ny)):
            if i < nx:
                xx = lax.rem(x + order[nx][i], nx)
                blk = hx.at[g, y, xx]
                if i > 0:
                    arrived(blk, ag_r.at[g, 0, y, xx])
                for j in range(1, ny):
                    push(remote(blk, blk, ag_s2.at[g, 0, i, j - 1], ag_r.at[g, 0, y, xx], at(lax.rem(y + j, ny), x, c)))
            if i < ny:
                yy = lax.rem(y + order[ny][i], ny)
                blk = hy.at[g, yy, x]
                if i > 0:
                    arrived(blk, ag_r.at[g, 1, yy, x])
                for j in range(1, nx):
                    push(remote(blk, blk, ag_s2.at[g, 1, i, j - 1], ag_r.at[g, 1, yy, x], at(y, lax.rem(x + j, nx), c)))

    def gather_wait(g):
        def wait_x(i, carry):
            yy, xx = lax.rem(y + 1 + i // nx, ny), lax.rem(i, nx)
            arrived(hx.at[g, yy, xx], ag_r.at[g, 0, yy, xx])
            return carry

        def wait_y(i, carry):
            yy, xx = lax.rem(i, ny), lax.rem(x + 1 + i // ny, nx)
            arrived(hy.at[g, yy, xx], ag_r.at[g, 1, yy, xx])
            return carry

        lax.fori_loop(0, nx * (ny - 1), wait_x, 0)
        lax.fori_loop(0, ny * (nx - 1), wait_y, 0)

    def logits_start(g):
        for buf, off in ((hx, 0), (hy, xw)):
            block = buf[g].astype(f32).reshape(chips, 2, 8, qw)
            for k in range(2):
                hid[g * tokens : (g + 1) * tokens, off + k * qw : off + (k + 1) * qw] = (
                    block[:, k].reshape(tokens, qw).astype(bf16)
                )
        lt_own[g] = nt(w2[...].reshape(2 * vb, dh), hid[g * tokens : (g + 1) * tokens, :])
        push(remote(lt_own.at[g], lt_sib.at[g], sib_s.at[2 + g], sib_r.at[2 + g], sibling))

    vocab_id = iota((2 * vb, tokens), 0) + (v * rows + 2 * chip) * vb
    i4 = iota((4, tokens), 0)

    def onehot(g):
        return (vocab_id == (mids, tids)[g][...]).astype(f32)

    pst = [to_chips(pst_s.at[g], pst_r.at[g], st_plane.at[g]) for g in range(2)]
    zst = [
        to_vocab(zst_s.at[g], zst_r.at[g], lambda zz, g=g: st_z.at[g, v], lambda zz, g=g: st_z.at[g, zz])
        for g in range(2)
    ]

    def stats_start(g):
        arrived(lt_sib.at[g], sib_r.at[2 + g])
        logits = lt_own[g] + lt_sib[g]
        top = jnp.max(logits, axis=0, keepdims=True)
        e = jnp.exp(logits - top)
        lt_sib[g] = e
        st_plane[g, chip] = jnp.where(
            i4 == 0,
            top,
            jnp.where(
                i4 == 1,
                jnp.sum(e, axis=0, keepdims=True),
                jnp.where(
                    i4 == 2,
                    jnp.sum(e * logits, axis=0, keepdims=True),
                    jnp.sum(onehot(g) * logits, axis=0, keepdims=True),
                ),
            ),
        )
        pst[g][0]()
        return top

    def merge(slots, count):
        top = slots[0][0:1]
        for s in range(1, count):
            top = jnp.maximum(top, slots[s][0:1])
        acc = jnp.zeros((4, tokens), f32)
        for s in range(count):
            tile = slots[s]
            acc = acc + jnp.where(i4 == 3, tile, tile * jnp.exp(tile[0:1] - top))
        return jnp.where(i4 == 0, top, acc)

    def stats_second(g):
        pst[g][1]()
        st_z[g, v] = merge(st_plane.at[g], chips)
        zst[g][0]()

    def grads_start(g, top_chip):
        zst[g][1]()
        whole = merge(st_z.at[g], nz)
        top, total = whole[0:1], whole[1:2]
        grads = lt_sib[g] * (shares[g] * jnp.exp(top_chip - top) / total) - shares[g] * onehot(g)
        gt[:, g * tokens : (g + 1) * tokens] = grads.astype(bf16)
        grads_t = jnp.transpose(grads).astype(bf16)
        for buf, off in ((px, 0), (py, xw)):
            halves = [
                nn(grads_t, w2[:, :, off + k * qw : off + (k + 1) * qw].reshape(2 * vb, qw)).reshape(chips, 8, qw)
                for k in range(2)
            ]
            buf[g] = jnp.concatenate(halves, axis=1).astype(bf16).reshape(ny, nx, 16, qw)
            if off == 0:
                for j in range(1, nx):
                    xx = lax.rem(x + j, nx)
                    push(remote(px.at[g, :, xx], rx.at[g, j - 1], rs_s1.at[g, 0, j - 1], rs_r1.at[g, 0, j - 1], at(y, xx, c)))
            else:
                for j in range(1, ny):
                    yy = lax.rem(y + j, ny)
                    push(remote(py.at[g, yy], ry.at[g, j - 1], rs_s1.at[g, 1, j - 1], rs_r1.at[g, 1, j - 1], at(yy, x, c)))
        dot = shares[g] * (whole[2:3] / total - whole[3:4])
        return (
            jnp.sum(jnp.where(iota((4, tokens), 1) == 4 * r + i4, dot, 0.0), axis=1, keepdims=True) / width
        )

    def sum_second(g):
        for axis, count, other_count, own_buf, got, out, out2 in (
            (0, ny, nx, px, rx, axs, rx2), (1, nx, ny, py, ry, ays, ry2),
        ):
            for j in range(1, other_count):
                arrived(got.at[g, j - 1], rs_r1.at[g, axis, j - 1])
            for jj in range(count):
                j = (jj + 1) % count
                k0 = lax.rem((y, x)[axis] + j, count)
                own_block = own_buf[g, k0, x] if axis == 0 else own_buf[g, y, k0]
                acc = own_block.astype(f32)
                for k in range(other_count - 1):
                    acc = acc + got[g, k, k0].astype(f32)
                for d in range(2):
                    four = jnp.concatenate([acc[4 * d : 4 * d + 4], acc[8 + 4 * d : 12 + 4 * d]], axis=0)
                    rest = four[:, cut:]
                    if 2 * cut > qw:
                        rest = jnp.concatenate([rest, jnp.zeros((8, 2 * cut - qw), f32)], axis=1)
                    out[g, j, d] = jnp.concatenate([four[:, :cut], rest], axis=0).astype(bf16)
                if j > 0:
                    for d in range(2):
                        device = at(k0, x, d) if axis == 0 else at(y, k0, d)
                        push(remote(out.at[g, j, d], out2.at[g, j, c], rs_s2.at[g, axis, j, d], rs_r2.at[g, axis, j, c], device))
                else:
                    push(remote(out.at[g, 0, 1 - c], out2.at[g, 0, c], rs_s2.at[g, axis, 0, 0], rs_r2.at[g, axis, 0, c], sibling))
                    out2[g, 0, c] = out[g, 0, c]

    zrs = [
        to_vocab(zrs_s.at[g], zrs_r.at[g], lambda zz, g=g: zs.at[g, zz], lambda zz, g=g: zr.at[g, zz])
        for g in range(2)
    ]
    zag = [
        to_vocab(zag_s.at[g], zag_r.at[g], lambda zz, g=g: zo.at[g, v], lambda zz, g=g: zo.at[g, zz])
        for g in range(2)
    ]

    def vocab_start(g):
        for buf, axis, count, off in ((rx2, 0, ny, 0), (ry2, 1, nx, xw)):
            for j in range(1, count):
                for s in range(2):
                    arrived(buf.at[g, j, s], rs_r2.at[g, axis, j, s])
            arrived(buf.at[g, 0, 1 - c], rs_r2.at[g, axis, 0, 1 - c])
            for s in range(2):
                acc = buf[g, 0, s].astype(f32)
                for j in range(1, count):
                    acc = acc + buf[g, j, s].astype(f32)
                wide = jnp.concatenate([acc[0:8], acc[8:16, : qw - cut]], axis=1)
                sum4[:, s * dh + off : s * dh + off + qw] = wide[0:4]
                sum4[:, s * dh + off + qw : s * dh + off + 2 * qw] = wide[4:8]
        for zz in range(nz):
            zs[g, zz] = fold4(sum4[:, starts[zz] : starts[zz] + LANES])
        zrs[g][0]()
        zr[g, v] = zs[g, v]

    def vocab_sum(g):
        zrs[g][1]()
        acc = zr[g, 0].astype(f32)
        for zz in range(1, nz):
            acc = acc + zr[g, zz].astype(f32)
        return unfold4(acc)

    def write(g, out):
        zag[g][1]()
        for zz in range(nz):
            out[:, starts[zz] : starts[zz] + LANES] = unfold4(zo[g, zz].astype(f32)).astype(bf16)

    a2a = to_rows(a2a_ss, a2a_rs, lambda rr: a2a_s.at[rr], lambda rr: a2a_r.at[rr])
    pag = to_rows(pag_s, pag_r, lambda rr: po, lambda rr: pr.at[rr])
    zga = to_vocab(zga_s, zga_r, lambda zz: gs.at[zz], lambda zz: gr.at[zz])
    zgs = to_vocab(zg_s, zg_r, lambda zz: zg.at[v], lambda zz: zg.at[zz])

    gather_first(0)
    gather_first(1)
    gather_second(0)

    for load in loads[3:]:
        load.wait()
    ir = iota((rows * 16, 4 * heads), 0)
    im = iota((rows * 16, 4 * heads), 1)
    kk = ir & 15
    pick = (kk < 8) & (im == (kk >> 1) * heads + 2 * (ir >> 4) + (kk & 1))
    a2a_s[...] = (
        nn(pick.astype(f32).astype(bf16), attn[...].reshape(4 * heads, hd)).astype(bf16).reshape(rows, 16, hd)
    )
    a2a_r[r] = a2a_s[r]

    it = iota((tokens, rows * 16), 0)
    il = iota((tokens, rows * 16), 1)
    base = 16 * (it >> 2) + (it & 3)
    sel[0:tokens, :] = (il == base + 4).astype(f32).astype(bf16)
    sel[tokens : 2 * tokens, :] = (il == base + 12).astype(f32).astype(bf16)
    ig = iota((16, rows * 16), 0)
    kg = iota((16, rows * 16), 1) & 15
    sel[2 * tokens : 2 * tokens + 16, :] = (
        ((ig == 0) & (kg < 2)) | ((ig == 1) & (kg >= 8) & (kg < 10))
    ).astype(f32).astype(bf16)
    base = 16 * (it >> 2) + 2 * (it & 3)
    for h in range(2):
        gather_v[h * tokens : (h + 1) * tokens, :] = (il == base + h).astype(f32).astype(bf16)
    opw[...] = jnp.zeros(opw.shape, bf16)
    shift = pl.multiple_of(v * step % 128, 16)
    opw[pl.ds(shift, step), :] = out_proj_t[...]

    w_copy.wait()
    arrived(w2.at[1 - c], sib_r.at[1])
    gather_wait(0)
    logits_start(0)
    gather_second(1)
    top_m = stats_start(0)
    a2a[0]()
    stats_second(0)
    gather_wait(1)
    logits_start(1)
    top_t = stats_start(1)
    dot_mean = grads_start(0, top_m)
    stats_second(1)
    sum_second(0)
    grads_start(1, top_t)
    vocab_start(0)

    for n in range(0, dh, qw):
        head_out[:, n : n + qw] = nn(gt[pl.ds(pl.multiple_of((1 - c) * vb, 16), vb), :], hid[:, n : n + qw]).astype(bf16)
    head_copy = remote(head_out, o_head.at[:, own_cols], sib_s.at[4], sib_r.at[4], sibling)
    push(head_copy)

    sum_second(1)
    grad = vocab_sum(0)

    cols = pl.ds(window, LANES)
    normed4 = st4[:, cols]
    residual = inv4[:, 0:1] * (grad * gain_row[:, cols] - normed4 * dot_mean)
    gain_term = jnp.sum(grad * normed4, axis=0, keepdims=True)
    gain_high = gain_term.astype(bf16).astype(f32)
    po[...] = fold(
        jnp.concatenate([gain_high, gain_term - gain_high, jnp.zeros((2, LANES), f32), residual], axis=0)
    )
    pag[0]()
    pr[r] = po[...]
    zo[0, v] = fold4(residual)
    zag[0][0]()
    vocab_start(1)

    a2a[1]()
    received = a2a_r[...].reshape(rows * 16, hd)
    for h in range(2):
        vals[:, h * hd : (h + 1) * hd] = nn(gather_v[h * tokens : (h + 1) * tokens, :], received).astype(bf16)

    pag[1]()
    picked = nn(sel[...], pr[...].reshape(rows * 16, HALF))
    columns = jnp.concatenate([picked[0:tokens], picked[tokens : 2 * tokens]], axis=1)
    attn_term = nn(columns.astype(bf16), opw[...])
    for zz in range(nz):
        gs[zz] = fold(attn_term[8 * zz : 8 * zz + 8])
    zga[0]()
    gr[v] = gs[v]
    zg[v] = jnp.concatenate(
        [picked[2 * tokens + k // 2 : 2 * tokens + k // 2 + 1, k % 2 * 128 : k % 2 * 128 + 128] for k in range(LANES // 128)],
        axis=0,
    )
    zgs[0]()
    zo[1, v] = fold4(vocab_sum(1))
    zag[1][0]()

    for n in range(0, dh, qw):
        o_head[:, pl.ds(pl.multiple_of(c * dh + n, 128), qw)] = nn(
            gt[pl.ds(pl.multiple_of(c * vb, 16), vb), :], hid[:, n : n + qw]
        ).astype(bf16)
    proj_s[...] = nn(jnp.transpose(columns).astype(bf16), vals[...]).astype(bf16)
    o_proj_t[...] = proj_s[pl.ds(shift, step), :]

    write(0, o_res)
    zgs[1]()
    for zz in range(nz):
        o_gain[starts[zz] // 128 : (starts[zz] + LANES) // 128, :] = zg[zz]
    zga[1]()
    acc = gr[0].astype(f32)
    for zz in range(1, nz):
        acc = acc + gr[zz].astype(f32)
    for h in range(2):
        attn_s[pl.ds(h, 8, stride=2), :] = acc[8 * h : 8 * h + 8]
    o_attn[...] = attn_s[...].astype(bf16)
    arrived(o_head.at[:, sib_cols], sib_r.at[4])
    for copy in sends:
        copy.wait_send()
    write(1, o_trunk)


def finish(*refs):
    sources, targets, held, sem_in, sem_out = refs[0:6], refs[6:12], refs[12:18], refs[18], refs[19]
    pieces = []
    for src, dst, buf in zip(sources, targets, held):
        rows = src.shape[0]
        cut = rows // 3 if rows % 48 == 0 else rows
        for at in range(0, rows, cut):
            pieces.append((src.at[at : at + cut], dst.at[at : at + cut], buf.at[at : at + cut]))
    pieces.sort(key=lambda piece: -piece[0].shape[0] * piece[0].shape[1])
    loads = [pltpu.make_async_copy(src, buf, sem_in.at[i]) for i, (src, _, buf) in enumerate(pieces)]
    stores = [pltpu.make_async_copy(buf, dst, sem_out.at[i]) for i, (_, dst, buf) in enumerate(pieces)]
    for load in loads:
        load.start()
    for load, store in zip(loads, stores):
        load.wait()
        store.start()
    for store in stores:
        store.wait()


def local(dims, trunk_hidden, mtp_state, mtp_gain, head_weight, target_ids, mtp_target_ids, attn_values, out_proj):
    nx, ny, nz, width = dims
    rows = 2 * nx * ny
    tokens = 4 * rows
    vb = head_weight.shape[0]
    dh = width // 2
    qw = dh // 4
    cut = -(-qw // 256) * 128
    step = out_proj.shape[1]
    heads, hd = attn_values.shape[1:]
    vmem = pltpu.VMEM
    dma = pltpu.SemaphoreType.DMA
    scratch = [
        vmem((4, width), bf16),
        vmem((4, width), bf16),
        vmem((width // 128, 128), bf16),
        vmem((1, tokens), jnp.int32),
        vmem((1, tokens), jnp.int32),
        vmem((4, heads, hd), bf16),
        vmem((step, 2 * hd), bf16),
        vmem((1, width), f32),
        vmem((8, width), f32),
        vmem((4, width), f32),
        vmem((4, 128), f32),
        vmem((8, dh), f32),
        vmem((2, vb, dh), bf16),
        vmem((2, ny, nx, 16, qw), bf16),
        vmem((2, ny, nx, 16, qw), bf16),
        vmem((2 * tokens, dh), bf16),
        vmem((2, 2 * vb, tokens), f32),
        vmem((2, 2 * vb, tokens), f32),
        vmem((2, nx * ny, 4, tokens), f32),
        vmem((2, nz, 4, tokens), f32),
        vmem((2 * vb, 2 * tokens), bf16),
        vmem((2, ny, nx, 16, qw), bf16),
        vmem((2, ny, nx, 16, qw), bf16),
        vmem((vb, dh), bf16),
        vmem((2, max(nx - 1, 1), ny, 16, qw), bf16),
        vmem((2, max(ny - 1, 1), nx, 16, qw), bf16),
        vmem((2, ny, 2, 16, cut), bf16),
        vmem((2, nx, 2, 16, cut), bf16),
        vmem((2, ny, 2, 16, cut), bf16),
        vmem((2, nx, 2, 16, cut), bf16),
        vmem((4, width), f32),
        vmem((2, nz, 16, LANES // 4), bf16),
        vmem((2, nz, 16, LANES // 4), bf16),
        vmem((2, nz, 16, LANES // 4), bf16),
        vmem((16, HALF), bf16),
        vmem((rows, 16, HALF), bf16),
        vmem((2 * tokens + 16, rows * 16), bf16),
        vmem((2 * tokens, rows * 16), bf16),
        vmem((rows, 16, hd), bf16),
        vmem((rows, 16, hd), bf16),
        vmem((tokens, 2 * hd), bf16),
        vmem((LANES, 2 * hd), bf16),
        vmem((nz, LANES // 128, 128), f32),
        vmem((nz, 16, hd), bf16),
        vmem((nz, 16, hd), bf16),
        vmem((LANES, 2 * hd), bf16),
        vmem((16, hd), f32),
        dma((8,)),
        dma((5,)),
        dma((5,)),
        dma((2, 2, 3)),
        dma((2, 2, 4, 3)),
        dma((2, 2, ny, nx)),
        dma((2, nx * ny)),
        dma((2, nx * ny)),
        dma((2, nz)),
        dma((2, nz)),
        dma((2, 2, 3)),
        dma((2, 2, 3)),
        dma((2, 2, 4, 2)),
        dma((2, 2, 4, 2)),
        dma((2, nz)),
        dma((2, nz)),
        dma((2, nz)),
        dma((2, nz)),
        dma((rows,)),
        dma((rows,)),
        dma((rows,)),
        dma((rows,)),
        dma((nz,)),
        dma((nz,)),
        dma((nz,)),
        dma((nz,)),
    ]
    in_vmem = pl.BlockSpec(memory_space=pltpu.VMEM)
    in_hbm = pl.BlockSpec(memory_space=pl.ANY)
    shape = jax.ShapeDtypeStruct
    shapes = [
        shape((4, width), bf16),
        shape((4, width), bf16),
        shape((width // 128, 128), f32),
        shape((vb, width), bf16),
        shape((16, hd), bf16),
        shape((step, 2 * hd), bf16),
    ]
    results = pl.pallas_call(
        functools.partial(kernel, dims),
        out_shape=shapes,
        in_specs=[pl.BlockSpec(memory_space=pltpu.HBM)] * 8,
        out_specs=[in_vmem] * 6,
        scratch_shapes=scratch,
        compiler_params=pltpu.CompilerParams(
            collective_id=0, has_side_effects=True, vmem_limit_bytes=60 * 2**20
        ),
        name="head_backward",
    )(
        trunk_hidden,
        mtp_state,
        mtp_gain.reshape(width // 128, 128),
        head_weight,
        target_ids.reshape(1, -1),
        mtp_target_ids.reshape(1, -1),
        attn_values,
        out_proj.T,
    )
    trunk_out, res_out, gain_out, head_out, attn_out, proj_out = pl.pallas_call(
        finish,
        out_shape=shapes,
        in_specs=[in_hbm] * len(shapes),
        out_specs=[in_hbm] * len(shapes),
        scratch_shapes=[vmem(s.shape, s.dtype) for s in shapes] + [dma((8,)), dma((8,))],
        compiler_params=pltpu.CompilerParams(vmem_limit_bytes=60 * 2**20),
        name="results",
    )(*results)
    grad_attn = attn_out.reshape(8, 2, hd)
    return (trunk_out, res_out, gain_out.reshape(width), head_out, grad_attn, proj_out.T)


def solution(mesh):
    nz, rows = mesh.shape["vocab"], mesh.shape["rows"]
    nx = {32: 4, 8: 2, 2: 1}[rows]

    def run(*args):
        dims = (nx, rows // 2 // nx, nz, args[0].shape[1])
        return local(dims, *args)

    return jax.shard_map(
        run,
        mesh=mesh,
        in_specs=(
            P("rows", None),
            P("rows", None),
            P(),
            P(("vocab", "rows"), None),
            P(),
            P(),
            P("rows", None, None),
            P("rows", "vocab"),
        ),
        out_specs=(
            P("rows", None),
            P("rows", None),
            P(),
            P(("vocab", "rows"), None),
            P("vocab", "rows", None),
            P("rows", "vocab"),
        ),
        check_vma=False,
    )
```

```python
import functools

import jax
import jax.numpy as jnp
from jax import lax
from jax.experimental import pallas as pl
from jax.experimental.pallas import tpu as pltpu
from jax.sharding import PartitionSpec as P

loss_scale = 8.0
mtp_share = 0.3
norm_eps = 1e-06
f32 = jnp.float32
bf16 = jnp.bfloat16
LANES = 512
HALF = LANES // 2


def nn(a, b):
    return lax.dot_general(a, b, (((1,), (0,)), ((), ())), preferred_element_type=f32)


def nt(a, b):
    return lax.dot_general(a, b, (((1,), (1,)), ((), ())), preferred_element_type=f32)


def iota(shape, axis):
    return lax.broadcasted_iota(jnp.int32, shape, axis)


def fold(block):
    w = block.shape[1] // 2
    return jnp.concatenate([block[:, :w], block[:, w:]], axis=0).astype(bf16)


def unfold(block):
    return jnp.concatenate([block[:8], block[8:]], axis=1)


def fold4(block):
    w = block.shape[1] // 4
    return jnp.concatenate([block[:, k * w : (k + 1) * w] for k in range(4)], axis=0).astype(bf16)


def unfold4(block):
    return jnp.concatenate([block[4 * k : 4 * k + 4] for k in range(4)], axis=1)


def remote(src, dst, send, recv, device):
    return pltpu.make_async_remote_copy(
        src_ref=src,
        dst_ref=dst,
        send_sem=send,
        recv_sem=recv,
        device_id=device,
        device_id_type=pl.DeviceIdType.MESH,
    )


def kernel(
    dims,
    trunk_h, state_h, gain_h, w_hbm, tids_h, mids_h, attn_h, out_proj_h,
    o_trunk, o_res, o_gain, o_head, o_attn, o_proj_t,
    trunk, state, gain, tids, mids, attn, out_proj_t,
    gain_row, own8, st4, inv4, sib8, w2, hx, hy, hid, lt_own, lt_sib, st_plane, st_z,
    gt, px, py, head_out, rx, ry, axs, ays, rx2, ry2, sum4, zs, zr, zo, po, pr, sel, gather_v,
    a2a_s, a2a_r, vals, opw, zg, gs, gr, proj_s, attn_s,
    cp_sem, sib_s, sib_r, ag_s1, ag_s2, ag_r, pst_s, pst_r, zst_s, zst_r,
    rs_s1, rs_r1, rs_s2, rs_r2, zrs_s, zrs_r, zag_s, zag_r, pag_s, pag_r,
    a2a_ss, a2a_rs, zg_s, zg_r, zga_s, zga_r,
):
    nx, ny, nz, width = dims
    rows = 2 * nx * ny
    chips = nx * ny
    tokens = 4 * rows
    vb = w_hbm.shape[0]
    dh = width // 2
    xw = dh // 2
    qw = xw // 2
    cut = -(-qw // 256) * 128
    heads, hd = attn.shape[1:]
    step = width // nz
    starts = [zz * step // 128 * 128 for zz in range(nz)]
    shares = (loss_scale * mtp_share, loss_scale)

    v = lax.axis_index("vocab")
    r = lax.axis_index("rows")
    c = lax.rem(r, 2)
    chip = r // 2
    x = lax.rem(chip, nx)
    y = chip // nx
    sibling = (v, r + 1 - 2 * c)
    window = pl.multiple_of(v * step // 128 * 128, 128)

    def at(yy, xx, core):
        return (v, (yy * nx + xx) * 2 + core)

    def arrived(ref, sem):
        remote(ref, ref, sib_s.at[0], sem, sibling).wait_recv()

    sends = []

    def push(copy):
        copy.start()
        sends.append(copy)

    def to_vocab(send, recv, source, target):
        def copy(i):
            zz = lax.rem(v + i, nz)
            return remote(source(zz), target(v), send.at[i], recv.at[v], (zz, r))

        def start(i, carry):
            copy(i).start()
            return carry

        def finish(i, carry):
            zz = lax.rem(v + i, nz)
            arrived(target(zz), recv.at[zz])
            copy(i).wait_send()
            return carry

        return (lambda: lax.fori_loop(1, nz, start, 0)), (lambda: lax.fori_loop(1, nz, finish, 0))

    def to_rows(send, recv, source, target):
        def copy(i):
            rr = lax.rem(r + i, rows)
            return remote(source(rr), target(r), send.at[i], recv.at[r], (v, rr))

        def start(i, carry):
            copy(i).start()
            return carry

        def finish(i, carry):
            rr = lax.rem(r + i, rows)
            arrived(target(rr), recv.at[rr])
            copy(i).wait_send()
            return carry

        return (lambda: lax.fori_loop(1, rows, start, 0)), (lambda: lax.fori_loop(1, rows, finish, 0))

    def to_chips(send, recv, buf):
        def copy(i):
            cc = lax.rem(chip + i, chips)
            return remote(buf.at[chip], buf.at[chip], send.at[i], recv.at[chip], (v, 2 * cc + c))

        def start(i, carry):
            copy(i).start()
            return carry

        def finish(i, carry):
            cc = lax.rem(chip + i, chips)
            arrived(buf.at[cc], recv.at[cc])
            copy(i).wait_send()
            return carry

        return (lambda: lax.fori_loop(1, chips, start, 0)), (lambda: lax.fori_loop(1, chips, finish, 0))

    own_cols = pl.ds(pl.multiple_of(c * dh, 128), dh)
    sib_cols = pl.ds(pl.multiple_of((1 - c) * dh, 128), dh)
    w_copy = pltpu.make_async_copy(w_hbm.at[:, own_cols], w2.at[c], cp_sem.at[0])
    loads = [
        pltpu.make_async_copy(src, dst, cp_sem.at[1 + i])
        for i, (src, dst) in enumerate(
            (
                (state_h, state), (gain_h, gain), (trunk_h, trunk), (tids_h, tids), (mids_h, mids),
                (attn_h, attn), (out_proj_h, out_proj_t),
            )
        )
    ]
    for load in loads:
        load.start()
    w_copy.start()

    bar = pltpu.get_barrier_semaphore()

    def greet_rows(i, carry):
        pl.semaphore_signal(
            bar, inc=1, device_id=(v, lax.rem(r + i, rows)), device_id_type=pl.DeviceIdType.MESH
        )
        return carry

    def greet_vocab(i, carry):
        pl.semaphore_signal(
            bar, inc=1, device_id=(lax.rem(v + i, nz), r), device_id_type=pl.DeviceIdType.MESH
        )
        return carry

    lax.fori_loop(1, nz, greet_vocab, 0)
    lax.fori_loop(1, rows, greet_rows, 0)

    for load in loads[:3]:
        load.wait()
    sv = state[...].astype(f32)
    inverse = lax.rsqrt(jnp.mean(sv * sv, axis=-1, keepdims=True) + norm_eps)
    normed = sv * inverse
    for k in range(width // 128):
        gain_row[0:1, k * 128 : (k + 1) * 128] = gain[k : k + 1, :].astype(f32)
    own8[0:4, :] = trunk[...].astype(f32)
    own8[4:8, :] = (normed * gain_row[...]).astype(bf16).astype(f32)
    st4[...] = normed
    inv4[...] = jnp.broadcast_to(inverse, (4, 128))

    pl.semaphore_wait(bar, rows - 1 + nz - 1)

    tok_copy = remote(own8.at[:, sib_cols], sib8, sib_s.at[0], sib_r.at[0], sibling)
    push(tok_copy)
    push(remote(w_hbm.at[:, sib_cols], w2.at[c], sib_s.at[1], sib_r.at[1], sibling))
    mine = own8[:, own_cols]
    tok_copy.wait_recv()
    other = sib8[...]
    first = c == 0
    low = jnp.where(first, mine, other)
    high = jnp.where(first, other, mine)
    for g, rng in ((0, slice(4, 8)), (1, slice(0, 4))):
        block = jnp.concatenate([low[rng], high[rng]], axis=0)
        hx[g, y, x] = fold(block[:, :xw])
        hy[g, y, x] = fold(block[:, xw:])

    def gather_first(g):
        for j in range(1, nx):
            blk = hx.at[g, y, x]
            push(remote(blk, blk, ag_s1.at[g, 0, j - 1], ag_r.at[g, 0, y, x], at(y, lax.rem(x + j, nx), c)))
        for j in range(1, ny):
            blk = hy.at[g, y, x]
            push(remote(blk, blk, ag_s1.at[g, 1, j - 1], ag_r.at[g, 1, y, x], at(lax.rem(y + j, ny), x, c)))

    order = {4: (0, 1, 3, 2), 2: (0, 1), 1: (0,)}

    def gather_second(g):
        for i in range(max(nx, ny)):
            if i < nx:
                xx = lax.rem(x + order[nx][i], nx)
                blk = hx.at[g, y, xx]
                if i > 0:
                    arrived(blk, ag_r.at[g, 0, y, xx])
                for j in range(1, ny):
                    push(remote(blk, blk, ag_s2.at[g, 0, i, j - 1], ag_r.at[g, 0, y, xx], at(lax.rem(y + j, ny), x, c)))
            if i < ny:
                yy = lax.rem(y + order[ny][i], ny)
                blk = hy.at[g, yy, x]
                if i > 0:
                    arrived(blk, ag_r.at[g, 1, yy, x])
                for j in range(1, nx):
                    push(remote(blk, blk, ag_s2.at[g, 1, i, j - 1], ag_r.at[g, 1, yy, x], at(y, lax.rem(x + j, nx), c)))

    def gather_wait(g):
        def wait_x(i, carry):
            yy, xx = lax.rem(y + 1 + i // nx, ny), lax.rem(i, nx)
            arrived(hx.at[g, yy, xx], ag_r.at[g, 0, yy, xx])
            return carry

        def wait_y(i, carry):
            yy, xx = lax.rem(i, ny), lax.rem(x + 1 + i // ny, nx)
            arrived(hy.at[g, yy, xx], ag_r.at[g, 1, yy, xx])
            return carry

        lax.fori_loop(0, nx * (ny - 1), wait_x, 0)
        lax.fori_loop(0, ny * (nx - 1), wait_y, 0)

    def logits_start(g):
        for buf, off in ((hx, 0), (hy, xw)):
            block = buf[g].astype(f32).reshape(chips, 2, 8, qw)
            for k in range(2):
                hid[g * tokens : (g + 1) * tokens, off + k * qw : off + (k + 1) * qw] = (
                    block[:, k].reshape(tokens, qw).astype(bf16)
                )
        lt_own[g] = nt(w2[...].reshape(2 * vb, dh), hid[g * tokens : (g + 1) * tokens, :])
        push(remote(lt_own.at[g], lt_sib.at[g], sib_s.at[2 + g], sib_r.at[2 + g], sibling))

    vocab_id = iota((2 * vb, tokens), 0) + (v * rows + 2 * chip) * vb
    i4 = iota((4, tokens), 0)

    def onehot(g):
        return (vocab_id == (mids, tids)[g][...]).astype(f32)

    pst = [to_chips(pst_s.at[g], pst_r.at[g], st_plane.at[g]) for g in range(2)]
    zst = [
        to_vocab(zst_s.at[g], zst_r.at[g], lambda zz, g=g: st_z.at[g, v], lambda zz, g=g: st_z.at[g, zz])
        for g in range(2)
    ]

    def stats_start(g):
        arrived(lt_sib.at[g], sib_r.at[2 + g])
        logits = lt_own[g] + lt_sib[g]
        top = jnp.max(logits, axis=0, keepdims=True)
        e = jnp.exp(logits - top)
        lt_sib[g] = e
        st_plane[g, chip] = jnp.where(
            i4 == 0,
            top,
            jnp.where(
                i4 == 1,
                jnp.sum(e, axis=0, keepdims=True),
                jnp.where(
                    i4 == 2,
                    jnp.sum(e * logits, axis=0, keepdims=True),
                    jnp.sum(onehot(g) * logits, axis=0, keepdims=True),
                ),
            ),
        )
        pst[g][0]()
        return top

    def merge(slots, count):
        top = slots[0][0:1]
        for s in range(1, count):
            top = jnp.maximum(top, slots[s][0:1])
        acc = jnp.zeros((4, tokens), f32)
        for s in range(count):
            tile = slots[s]
            acc = acc + jnp.where(i4 == 3, tile, tile * jnp.exp(tile[0:1] - top))
        return jnp.where(i4 == 0, top, acc)

    def stats_second(g):
        pst[g][1]()
        st_z[g, v] = merge(st_plane.at[g], chips)
        zst[g][0]()

    def sum_first(g, off):
        if off == 0:
            for j in range(1, nx):
                xx = lax.rem(x + j, nx)
                push(remote(px.at[g, :, xx], rx.at[g, j - 1], rs_s1.at[g, 0, j - 1], rs_r1.at[g, 0, j - 1], at(y, xx, c)))
        else:
            for j in range(1, ny):
                yy = lax.rem(y + j, ny)
                push(remote(py.at[g, yy], ry.at[g, j - 1], rs_s1.at[g, 1, j - 1], rs_r1.at[g, 1, j - 1], at(yy, x, c)))

    def grads_start(g, top_chip):
        zst[g][1]()
        whole = merge(st_z.at[g], nz)
        top, total = whole[0:1], whole[1:2]
        grads = lt_sib[g] * (shares[g] * jnp.exp(top_chip - top) / total) - shares[g] * onehot(g)
        gt[:, g * tokens : (g + 1) * tokens] = grads.astype(bf16)
        grads_t = jnp.transpose(grads).astype(bf16)
        for buf, off in ((px, 0), (py, xw)):
            halves = [
                nn(grads_t, w2[:, :, off + k * qw : off + (k + 1) * qw].reshape(2 * vb, qw)).reshape(chips, 8, qw)
                for k in range(2)
            ]
            buf[g] = jnp.concatenate(halves, axis=1).astype(bf16).reshape(ny, nx, 16, qw)
            if g == 0:
                sum_first(g, off)
        dot = shares[g] * (whole[2:3] / total - whole[3:4])
        return (
            jnp.sum(jnp.where(iota((4, tokens), 1) == 4 * r + i4, dot, 0.0), axis=1, keepdims=True) / width
        )

    def sum_second(g):
        for axis, count, other_count, own_buf, got, out, out2 in (
            (0, ny, nx, px, rx, axs, rx2), (1, nx, ny, py, ry, ays, ry2),
        ):
            for j in range(1, other_count):
                arrived(got.at[g, j - 1], rs_r1.at[g, axis, j - 1])
            for jj in range(count):
                j = (jj + 1) % count
                k0 = lax.rem((y, x)[axis] + j, count)
                own_block = own_buf[g, k0, x] if axis == 0 else own_buf[g, y, k0]
                acc = own_block.astype(f32)
                for k in range(other_count - 1):
                    acc = acc + got[g, k, k0].astype(f32)
                for d in range(2):
                    four = jnp.concatenate([acc[4 * d : 4 * d + 4], acc[8 + 4 * d : 12 + 4 * d]], axis=0)
                    rest = four[:, cut:]
                    if 2 * cut > qw:
                        rest = jnp.concatenate([rest, jnp.zeros((8, 2 * cut - qw), f32)], axis=1)
                    out[g, j, d] = jnp.concatenate([four[:, :cut], rest], axis=0).astype(bf16)
                if j > 0:
                    for d in range(2):
                        device = at(k0, x, d) if axis == 0 else at(y, k0, d)
                        push(remote(out.at[g, j, d], out2.at[g, j, c], rs_s2.at[g, axis, j, d], rs_r2.at[g, axis, j, c], device))
                else:
                    push(remote(out.at[g, 0, 1 - c], out2.at[g, 0, c], rs_s2.at[g, axis, 0, 0], rs_r2.at[g, axis, 0, c], sibling))
                    out2[g, 0, c] = out[g, 0, c]

    zrs = [
        to_vocab(zrs_s.at[g], zrs_r.at[g], lambda zz, g=g: zs.at[g, zz], lambda zz, g=g: zr.at[g, zz])
        for g in range(2)
    ]
    zag = [
        to_vocab(zag_s.at[g], zag_r.at[g], lambda zz, g=g: zo.at[g, v], lambda zz, g=g: zo.at[g, zz])
        for g in range(2)
    ]

    def vocab_start(g):
        for buf, axis, count, off in ((rx2, 0, ny, 0), (ry2, 1, nx, xw)):
            for j in range(1, count):
                for s in range(2):
                    arrived(buf.at[g, j, s], rs_r2.at[g, axis, j, s])
            arrived(buf.at[g, 0, 1 - c], rs_r2.at[g, axis, 0, 1 - c])
            for s in range(2):
                acc = buf[g, 0, s].astype(f32)
                for j in range(1, count):
                    acc = acc + buf[g, j, s].astype(f32)
                wide = jnp.concatenate([acc[0:8], acc[8:16, : qw - cut]], axis=1)
                sum4[:, s * dh + off : s * dh + off + qw] = wide[0:4]
                sum4[:, s * dh + off + qw : s * dh + off + 2 * qw] = wide[4:8]
        for zz in range(nz):
            zs[g, zz] = fold4(sum4[:, starts[zz] : starts[zz] + LANES])
        zrs[g][0]()
        zr[g, v] = zs[g, v]

    def vocab_sum(g):
        zrs[g][1]()
        acc = zr[g, 0].astype(f32)
        for zz in range(1, nz):
            acc = acc + zr[g, zz].astype(f32)
        return unfold4(acc)

    def write(g, out):
        zag[g][1]()
        for zz in range(nz):
            out[:, starts[zz] : starts[zz] + LANES] = unfold4(zo[g, zz].astype(f32)).astype(bf16)

    a2a = to_rows(a2a_ss, a2a_rs, lambda rr: a2a_s.at[rr], lambda rr: a2a_r.at[rr])
    pag = to_rows(pag_s, pag_r, lambda rr: po, lambda rr: pr.at[rr])
    zga = to_vocab(zga_s, zga_r, lambda zz: gs.at[zz], lambda zz: gr.at[zz])
    zgs = to_vocab(zg_s, zg_r, lambda zz: zg.at[v], lambda zz: zg.at[zz])

    gather_first(0)
    gather_second(0)
    gather_first(1)

    for load in loads[3:]:
        load.wait()
    ir = iota((rows * 16, 4 * heads), 0)
    im = iota((rows * 16, 4 * heads), 1)
    kk = ir & 15
    pick = (kk < 8) & (im == (kk >> 1) * heads + 2 * (ir >> 4) + (kk & 1))
    a2a_s[...] = (
        nn(pick.astype(f32).astype(bf16), attn[...].reshape(4 * heads, hd)).astype(bf16).reshape(rows, 16, hd)
    )
    a2a_r[r] = a2a_s[r]

    it = iota((tokens, rows * 16), 0)
    il = iota((tokens, rows * 16), 1)
    base = 16 * (it >> 2) + (it & 3)
    sel[0:tokens, :] = (il == base + 4).astype(f32).astype(bf16)
    sel[tokens : 2 * tokens, :] = (il == base + 12).astype(f32).astype(bf16)
    ig = iota((16, rows * 16), 0)
    kg = iota((16, rows * 16), 1) & 15
    sel[2 * tokens : 2 * tokens + 16, :] = (
        ((ig == 0) & (kg < 2)) | ((ig == 1) & (kg >= 8) & (kg < 10))
    ).astype(f32).astype(bf16)
    base = 16 * (it >> 2) + 2 * (it & 3)
    for h in range(2):
        gather_v[h * tokens : (h + 1) * tokens, :] = (il == base + h).astype(f32).astype(bf16)
    opw[...] = jnp.zeros(opw.shape, bf16)
    shift = pl.multiple_of(v * step % 128, 16)
    opw[pl.ds(shift, step), :] = out_proj_t[...]

    w_copy.wait()
    arrived(w2.at[1 - c], sib_r.at[1])
    gather_second(1)
    gather_wait(0)
    logits_start(0)
    top_m = stats_start(0)
    gather_wait(1)
    logits_start(1)
    stats_second(0)
    top_t = stats_start(1)
    a2a[0]()
    stats_second(1)
    dot_mean = grads_start(0, top_m)
    grads_start(1, top_t)
    sum_second(0)
    sum_first(1, 0)
    sum_first(1, xw)
    vocab_start(0)

    for n in range(0, dh, qw):
        head_out[:, n : n + qw] = nn(gt[pl.ds(pl.multiple_of((1 - c) * vb, 16), vb), :], hid[:, n : n + qw]).astype(bf16)
    head_copy = remote(head_out, o_head.at[:, own_cols], sib_s.at[4], sib_r.at[4], sibling)
    push(head_copy)

    sum_second(1)
    grad = vocab_sum(0)

    cols = pl.ds(window, LANES)
    normed4 = st4[:, cols]
    residual = inv4[:, 0:1] * (grad * gain_row[:, cols] - normed4 * dot_mean)
    gain_term = jnp.sum(grad * normed4, axis=0, keepdims=True)
    gain_high = gain_term.astype(bf16).astype(f32)
    po[...] = fold(
        jnp.concatenate([gain_high, gain_term - gain_high, jnp.zeros((2, LANES), f32), residual], axis=0)
    )
    pag[0]()
    pr[r] = po[...]
    zo[0, v] = fold4(residual)
    zag[0][0]()
    vocab_start(1)

    a2a[1]()
    received = a2a_r[...].reshape(rows * 16, hd)
    for h in range(2):
        vals[:, h * hd : (h + 1) * hd] = nn(gather_v[h * tokens : (h + 1) * tokens, :], received).astype(bf16)

    pag[1]()
    picked = nn(sel[...], pr[...].reshape(rows * 16, HALF))
    columns = jnp.concatenate([picked[0:tokens], picked[tokens : 2 * tokens]], axis=1)
    attn_term = nn(columns.astype(bf16), opw[...])
    for zz in range(nz):
        gs[zz] = fold(attn_term[8 * zz : 8 * zz + 8])
    zga[0]()
    gr[v] = gs[v]
    zg[v] = jnp.concatenate(
        [picked[2 * tokens + k // 2 : 2 * tokens + k // 2 + 1, k % 2 * 128 : k % 2 * 128 + 128] for k in range(LANES // 128)],
        axis=0,
    )
    zgs[0]()
    zo[1, v] = fold4(vocab_sum(1))
    zag[1][0]()

    for n in range(0, dh, qw):
        o_head[:, pl.ds(pl.multiple_of(c * dh + n, 128), qw)] = nn(
            gt[pl.ds(pl.multiple_of(c * vb, 16), vb), :], hid[:, n : n + qw]
        ).astype(bf16)
    proj_s[...] = nn(jnp.transpose(columns).astype(bf16), vals[...]).astype(bf16)
    o_proj_t[...] = proj_s[pl.ds(shift, step), :]

    write(0, o_res)
    zgs[1]()
    for zz in range(nz):
        o_gain[starts[zz] // 128 : (starts[zz] + LANES) // 128, :] = zg[zz]
    zga[1]()
    acc = gr[0].astype(f32)
    for zz in range(1, nz):
        acc = acc + gr[zz].astype(f32)
    for h in range(2):
        attn_s[pl.ds(h, 8, stride=2), :] = acc[8 * h : 8 * h + 8]
    o_attn[...] = attn_s[...].astype(bf16)
    arrived(o_head.at[:, sib_cols], sib_r.at[4])
    for copy in sends:
        copy.wait_send()
    write(1, o_trunk)


def finish(*refs):
    sources, targets, held, sem_in, sem_out = refs[0:6], refs[6:12], refs[12:18], refs[18], refs[19]
    pieces = []
    for src, dst, buf in zip(sources, targets, held):
        rows = src.shape[0]
        cut = rows // 3 if rows % 48 == 0 else rows
        for at in range(0, rows, cut):
            pieces.append((src.at[at : at + cut], dst.at[at : at + cut], buf.at[at : at + cut]))
    pieces.sort(key=lambda piece: -piece[0].shape[0] * piece[0].shape[1])
    loads = [pltpu.make_async_copy(src, buf, sem_in.at[i]) for i, (src, _, buf) in enumerate(pieces)]
    stores = [pltpu.make_async_copy(buf, dst, sem_out.at[i]) for i, (_, dst, buf) in enumerate(pieces)]
    for load in loads:
        load.start()
    for load, store in zip(loads, stores):
        load.wait()
        store.start()
    for store in stores:
        store.wait()


def local(dims, trunk_hidden, mtp_state, mtp_gain, head_weight, target_ids, mtp_target_ids, attn_values, out_proj):
    nx, ny, nz, width = dims
    rows = 2 * nx * ny
    tokens = 4 * rows
    vb = head_weight.shape[0]
    dh = width // 2
    qw = dh // 4
    cut = -(-qw // 256) * 128
    step = out_proj.shape[1]
    heads, hd = attn_values.shape[1:]
    vmem = pltpu.VMEM
    dma = pltpu.SemaphoreType.DMA
    scratch = [
        vmem((4, width), bf16),
        vmem((4, width), bf16),
        vmem((width // 128, 128), bf16),
        vmem((1, tokens), jnp.int32),
        vmem((1, tokens), jnp.int32),
        vmem((4, heads, hd), bf16),
        vmem((step, 2 * hd), bf16),
        vmem((1, width), f32),
        vmem((8, width), f32),
        vmem((4, width), f32),
        vmem((4, 128), f32),
        vmem((8, dh), f32),
        vmem((2, vb, dh), bf16),
        vmem((2, ny, nx, 16, qw), bf16),
        vmem((2, ny, nx, 16, qw), bf16),
        vmem((2 * tokens, dh), bf16),
        vmem((2, 2 * vb, tokens), f32),
        vmem((2, 2 * vb, tokens), f32),
        vmem((2, nx * ny, 4, tokens), f32),
        vmem((2, nz, 4, tokens), f32),
        vmem((2 * vb, 2 * tokens), bf16),
        vmem((2, ny, nx, 16, qw), bf16),
        vmem((2, ny, nx, 16, qw), bf16),
        vmem((vb, dh), bf16),
        vmem((2, max(nx - 1, 1), ny, 16, qw), bf16),
        vmem((2, max(ny - 1, 1), nx, 16, qw), bf16),
        vmem((2, ny, 2, 16, cut), bf16),
        vmem((2, nx, 2, 16, cut), bf16),
        vmem((2, ny, 2, 16, cut), bf16),
        vmem((2, nx, 2, 16, cut), bf16),
        vmem((4, width), f32),
        vmem((2, nz, 16, LANES // 4), bf16),
        vmem((2, nz, 16, LANES // 4), bf16),
        vmem((2, nz, 16, LANES // 4), bf16),
        vmem((16, HALF), bf16),
        vmem((rows, 16, HALF), bf16),
        vmem((2 * tokens + 16, rows * 16), bf16),
        vmem((2 * tokens, rows * 16), bf16),
        vmem((rows, 16, hd), bf16),
        vmem((rows, 16, hd), bf16),
        vmem((tokens, 2 * hd), bf16),
        vmem((LANES, 2 * hd), bf16),
        vmem((nz, LANES // 128, 128), f32),
        vmem((nz, 16, hd), bf16),
        vmem((nz, 16, hd), bf16),
        vmem((LANES, 2 * hd), bf16),
        vmem((16, hd), f32),
        dma((8,)),
        dma((5,)),
        dma((5,)),
        dma((2, 2, 3)),
        dma((2, 2, 4, 3)),
        dma((2, 2, ny, nx)),
        dma((2, nx * ny)),
        dma((2, nx * ny)),
        dma((2, nz)),
        dma((2, nz)),
        dma((2, 2, 3)),
        dma((2, 2, 3)),
        dma((2, 2, 4, 2)),
        dma((2, 2, 4, 2)),
        dma((2, nz)),
        dma((2, nz)),
        dma((2, nz)),
        dma((2, nz)),
        dma((rows,)),
        dma((rows,)),
        dma((rows,)),
        dma((rows,)),
        dma((nz,)),
        dma((nz,)),
        dma((nz,)),
        dma((nz,)),
    ]
    in_vmem = pl.BlockSpec(memory_space=pltpu.VMEM)
    in_hbm = pl.BlockSpec(memory_space=pl.ANY)
    shape = jax.ShapeDtypeStruct
    shapes = [
        shape((4, width), bf16),
        shape((4, width), bf16),
        shape((width // 128, 128), f32),
        shape((vb, width), bf16),
        shape((16, hd), bf16),
        shape((step, 2 * hd), bf16),
    ]
    results = pl.pallas_call(
        functools.partial(kernel, dims),
        out_shape=shapes,
        in_specs=[pl.BlockSpec(memory_space=pltpu.HBM)] * 8,
        out_specs=[in_vmem] * 6,
        scratch_shapes=scratch,
        compiler_params=pltpu.CompilerParams(
            collective_id=0, has_side_effects=True, vmem_limit_bytes=60 * 2**20
        ),
        name="head_backward",
    )(
        trunk_hidden,
        mtp_state,
        mtp_gain.reshape(width // 128, 128),
        head_weight,
        target_ids.reshape(1, -1),
        mtp_target_ids.reshape(1, -1),
        attn_values,
        out_proj.T,
    )
    trunk_out, res_out, gain_out, head_out, attn_out, proj_out = pl.pallas_call(
        finish,
        out_shape=shapes,
        in_specs=[in_hbm] * len(shapes),
        out_specs=[in_hbm] * len(shapes),
        scratch_shapes=[vmem(s.shape, s.dtype) for s in shapes] + [dma((8,)), dma((8,))],
        compiler_params=pltpu.CompilerParams(vmem_limit_bytes=60 * 2**20),
        name="results",
    )(*results)
    grad_attn = attn_out.reshape(8, 2, hd)
    return (trunk_out, res_out, gain_out.reshape(width), head_out, grad_attn, proj_out.T)


def solution(mesh):
    nz, rows = mesh.shape["vocab"], mesh.shape["rows"]
    nx = {32: 4, 8: 2, 2: 1}[rows]

    def run(*args):
        dims = (nx, rows // 2 // nx, nz, args[0].shape[1])
        return local(dims, *args)

    return jax.shard_map(
        run,
        mesh=mesh,
        in_specs=(
            P("rows", None),
            P("rows", None),
            P(),
            P(("vocab", "rows"), None),
            P(),
            P(),
            P("rows", None, None),
            P("rows", "vocab"),
        ),
        out_specs=(
            P("rows", None),
            P("rows", None),
            P(),
            P(("vocab", "rows"), None),
            P("vocab", "rows", None),
            P("rows", "vocab"),
        ),
        check_vma=False,
    )
```

```python
import functools

import jax
import jax.numpy as jnp
from jax import lax
from jax.experimental import pallas as pl
from jax.experimental.pallas import tpu as pltpu
from jax.sharding import PartitionSpec as P

loss_scale = 8.0
mtp_share = 0.3
norm_eps = 1e-06
f32 = jnp.float32
bf16 = jnp.bfloat16
LANES = 512
HALF = LANES // 2


def nn(a, b):
    return lax.dot_general(a, b, (((1,), (0,)), ((), ())), preferred_element_type=f32)


def nt(a, b):
    return lax.dot_general(a, b, (((1,), (1,)), ((), ())), preferred_element_type=f32)


def iota(shape, axis):
    return lax.broadcasted_iota(jnp.int32, shape, axis)


def fold(block):
    w = block.shape[1] // 2
    return jnp.concatenate([block[:, :w], block[:, w:]], axis=0).astype(bf16)


def unfold(block):
    return jnp.concatenate([block[:8], block[8:]], axis=1)


def fold4(block):
    w = block.shape[1] // 4
    return jnp.concatenate([block[:, k * w : (k + 1) * w] for k in range(4)], axis=0).astype(bf16)


def unfold4(block):
    return jnp.concatenate([block[4 * k : 4 * k + 4] for k in range(4)], axis=1)


def remote(src, dst, send, recv, device):
    return pltpu.make_async_remote_copy(
        src_ref=src,
        dst_ref=dst,
        send_sem=send,
        recv_sem=recv,
        device_id=device,
        device_id_type=pl.DeviceIdType.MESH,
    )


def kernel(
    dims,
    trunk_h, state_h, gain_h, w_hbm, tids_h, mids_h, attn_h, out_proj_h,
    o_trunk, o_res, o_gain, o_head, o_attn, o_proj_t,
    trunk, state, gain, tids, mids, attn, out_proj_t,
    gain_row, own8, st4, inv4, sib8, w2, hx, hy, hid, lt_own, lt_sib, st_plane, st_z,
    gt, px, py, head_out, rx, ry, axs, ays, rx2, ry2, sum4, zs, zr, zo, po, pr, sel, gather_v,
    a2a_s, a2a_r, vals, opw, zg, gs, gr, proj_s, attn_s,
    cp_sem, sib_s, sib_r, ag_s1, ag_s2, ag_r, ag_r2, pst_s, pst_r, zst_s, zst_r,
    rs_s1, rs_r1, rs_s2, rs_r2, zrs_s, zrs_r, zag_s, zag_r, pag_s, pag_r,
    a2a_ss, a2a_rs, zg_s, zg_r, zga_s, zga_r,
):
    nx, ny, nz, width = dims
    rows = 2 * nx * ny
    chips = nx * ny
    tokens = 4 * rows
    vb = w_hbm.shape[0]
    dh = width // 2
    xw = dh // 2
    qw = xw // 2
    cut = -(-qw // 256) * 128
    heads, hd = attn.shape[1:]
    step = width // nz
    starts = [zz * step // 128 * 128 for zz in range(nz)]
    shares = (loss_scale * mtp_share, loss_scale)
    far_chip = (ny // 2) * nx + nx // 2
    far_row = 2 * far_chip

    v = lax.axis_index("vocab")
    r = lax.axis_index("rows")
    c = lax.rem(r, 2)
    chip = r // 2
    x = lax.rem(chip, nx)
    y = chip // nx
    sibling = (v, r + 1 - 2 * c)
    window = pl.multiple_of(v * step // 128 * 128, 128)

    def at(yy, xx, core):
        return (v, (yy * nx + xx) * 2 + core)

    def arrived(ref, sem):
        remote(ref, ref, sib_s.at[0], sem, sibling).wait_recv()

    sends = []

    def push(copy):
        copy.start()
        sends.append(copy)

    def exchange(count, copy, slots, send, recv):
        def start(i, carry):
            copy(i).start()
            return carry

        def finish():
            whole = slots.at[0 : count - 1]
            done = remote(whole, whole, send, recv, sibling)
            done.wait_recv()
            done.wait_send()

        return (lambda: lax.fori_loop(1, count, start, 0)), finish

    def to_vocab(send, recv, source, slots):
        def copy(i):
            zz = lax.rem(v + nz // 2 + (1 - 2 * lax.rem(i + 1, 2)) * (i // 2), nz)
            return remote(source(zz), slots.at[v], send, recv, (zz, r))

        return exchange(nz, copy, slots, send, recv)

    def to_rows(send, recv, source, slots):
        def copy(i):
            rr = lax.rem(r + 1 + lax.rem(i + far_row - 2, rows - 1), rows)
            return remote(source(rr), slots.at[r], send, recv, (v, rr))

        return exchange(rows, copy, slots, send, recv)

    def to_chips(send, recv, slots):
        def copy(i):
            cc = lax.rem(chip + 1 + lax.rem(i + far_chip - 2, chips - 1), chips)
            return remote(slots.at[chip], slots.at[chip], send, recv, (v, 2 * cc + c))

        return exchange(chips, copy, slots, send, recv)

    own_cols = pl.ds(pl.multiple_of(c * dh, 128), dh)
    sib_cols = pl.ds(pl.multiple_of((1 - c) * dh, 128), dh)
    w_copy = pltpu.make_async_copy(w_hbm.at[:, own_cols], w2.at[c], cp_sem.at[0])
    loads = [
        pltpu.make_async_copy(src, dst, cp_sem.at[1 + i])
        for i, (src, dst) in enumerate(
            (
                (state_h, state), (gain_h, gain), (trunk_h, trunk), (tids_h, tids), (mids_h, mids),
                (attn_h, attn), (out_proj_h, out_proj_t),
            )
        )
    ]
    for load in loads:
        load.start()
    w_copy.start()

    bar = pltpu.get_barrier_semaphore()

    def greet_rows(i, carry):
        pl.semaphore_signal(
            bar, inc=1, device_id=(v, lax.rem(r + i, rows)), device_id_type=pl.DeviceIdType.MESH
        )
        return carry

    def greet_vocab(i, carry):
        pl.semaphore_signal(
            bar, inc=1, device_id=(lax.rem(v + i, nz), r), device_id_type=pl.DeviceIdType.MESH
        )
        return carry

    lax.fori_loop(1, nz, greet_vocab, 0)
    lax.fori_loop(1, rows, greet_rows, 0)

    for load in loads[:3]:
        load.wait()
    sv = state[...].astype(f32)
    inverse = lax.rsqrt(jnp.mean(sv * sv, axis=-1, keepdims=True) + norm_eps)
    normed = sv * inverse
    for k in range(width // 128):
        gain_row[0:1, k * 128 : (k + 1) * 128] = gain[k : k + 1, :].astype(f32)
    own8[0:4, :] = trunk[...].astype(f32)
    own8[4:8, :] = (normed * gain_row[...]).astype(bf16).astype(f32)
    st4[...] = normed
    inv4[...] = jnp.broadcast_to(inverse, (4, 128))

    pl.semaphore_wait(bar, rows - 1 + nz - 1)

    tok_copy = remote(own8.at[:, sib_cols], sib8, sib_s.at[0], sib_r.at[0], sibling)
    push(tok_copy)
    push(remote(w_hbm.at[:, sib_cols], w2.at[c], sib_s.at[1], sib_r.at[1], sibling))
    mine = own8[:, own_cols]
    tok_copy.wait_recv()
    other = sib8[...]
    first = c == 0
    low = jnp.where(first, mine, other)
    high = jnp.where(first, other, mine)
    for g, rng in ((0, slice(4, 8)), (1, slice(0, 4))):
        block = jnp.concatenate([low[rng], high[rng]], axis=0)
        hx[g, y, x] = fold(block[:, :xw])
        hy[g, y, x] = fold(block[:, xw:])

    def gather_first(g):
        for j in range(1, nx):
            blk = hx.at[g, y, x]
            push(remote(blk, blk, ag_s1.at[g, 0, j - 1], ag_r.at[g, 0, y, x], at(y, lax.rem(x + j, nx), c)))
        for j in range(1, ny):
            blk = hy.at[g, y, x]
            push(remote(blk, blk, ag_s1.at[g, 1, j - 1], ag_r.at[g, 1, y, x], at(lax.rem(y + j, ny), x, c)))

    order = {4: (0, 1, 3, 2), 2: (0, 1), 1: (0,)}

    def gather_second(g):
        for i in range(max(nx, ny)):
            if i < nx:
                xx = lax.rem(x + order[nx][i], nx)
                blk = hx.at[g, y, xx]
                if i > 0:
                    arrived(blk, ag_r.at[g, 0, y, xx])
                for j in range(1, ny):
                    push(remote(blk, blk, ag_s2.at[g, 0, i, j - 1], ag_r2.at[g, 0], at(lax.rem(y + j, ny), x, c)))
            if i < ny:
                yy = lax.rem(y + order[ny][i], ny)
                blk = hy.at[g, yy, x]
                if i > 0:
                    arrived(blk, ag_r.at[g, 1, yy, x])
                for j in range(1, nx):
                    push(remote(blk, blk, ag_s2.at[g, 1, i, j - 1], ag_r2.at[g, 1], at(y, lax.rem(x + j, nx), c)))

    def gather_wait(g):
        arrived(hx.at[g, 0 : ny - 1], ag_r2.at[g, 0])
        arrived(hy.at[g, 0 : nx - 1] if nx == ny else hy.at[g, :, 0 : nx - 1], ag_r2.at[g, 1])

    def logits_start(g):
        for buf, off in ((hx, 0), (hy, xw)):
            block = buf[g].astype(f32).reshape(chips, 2, 8, qw)
            for k in range(2):
                hid[g * tokens : (g + 1) * tokens, off + k * qw : off + (k + 1) * qw] = (
                    block[:, k].reshape(tokens, qw).astype(bf16)
                )
        lt_own[g] = nt(w2[...].reshape(2 * vb, dh), hid[g * tokens : (g + 1) * tokens, :])
        push(remote(lt_own.at[g], lt_sib.at[g], sib_s.at[2 + g], sib_r.at[2 + g], sibling))

    vocab_id = iota((2 * vb, tokens), 0) + (v * rows + 2 * chip) * vb
    i4 = iota((4, tokens), 0)

    def onehot(g):
        return (vocab_id == (mids, tids)[g][...]).astype(f32)

    pst = [to_chips(pst_s.at[g], pst_r.at[g], st_plane.at[g]) for g in range(2)]
    zst = [
        to_vocab(zst_s.at[g], zst_r.at[g], lambda zz, g=g: st_z.at[g, v], st_z.at[g])
        for g in range(2)
    ]

    def stats_start(g):
        arrived(lt_sib.at[g], sib_r.at[2 + g])
        logits = lt_own[g] + lt_sib[g]
        top = jnp.max(logits, axis=0, keepdims=True)
        e = jnp.exp(logits - top)
        lt_sib[g] = e
        st_plane[g, chip] = jnp.where(
            i4 == 0,
            top,
            jnp.where(
                i4 == 1,
                jnp.sum(e, axis=0, keepdims=True),
                jnp.where(
                    i4 == 2,
                    jnp.sum(e * logits, axis=0, keepdims=True),
                    jnp.sum(onehot(g) * logits, axis=0, keepdims=True),
                ),
            ),
        )
        pst[g][0]()
        return top

    def merge(slots, count):
        top = slots[0][0:1]
        for s in range(1, count):
            top = jnp.maximum(top, slots[s][0:1])
        acc = jnp.zeros((4, tokens), f32)
        for s in range(count):
            tile = slots[s]
            acc = acc + jnp.where(i4 == 3, tile, tile * jnp.exp(tile[0:1] - top))
        return jnp.where(i4 == 0, top, acc)

    def stats_second(g):
        pst[g][1]()
        st_z[g, v] = merge(st_plane.at[g], chips)
        zst[g][0]()

    def sum_first(g, off):
        if off == 0:
            for j in range(1, nx):
                xx = lax.rem(x + j, nx)
                push(remote(px.at[g, :, xx], rx.at[g, j - 1], rs_s1.at[g, 0, j - 1], rs_r1.at[g, 0, j - 1], at(y, xx, c)))
        else:
            for j in range(1, ny):
                yy = lax.rem(y + j, ny)
                push(remote(py.at[g, yy], ry.at[g, j - 1], rs_s1.at[g, 1, j - 1], rs_r1.at[g, 1, j - 1], at(yy, x, c)))

    def grads_start(g, top_chip):
        zst[g][1]()
        whole = merge(st_z.at[g], nz)
        top, total = whole[0:1], whole[1:2]
        grads = lt_sib[g] * (shares[g] * jnp.exp(top_chip - top) / total) - shares[g] * onehot(g)
        gt[:, g * tokens : (g + 1) * tokens] = grads.astype(bf16)
        grads_t = jnp.transpose(grads).astype(bf16)
        for buf, off in ((px, 0), (py, xw)):
            halves = [
                nn(grads_t, w2[:, :, off + k * qw : off + (k + 1) * qw].reshape(2 * vb, qw)).reshape(chips, 8, qw)
                for k in range(2)
            ]
            buf[g] = jnp.concatenate(halves, axis=1).astype(bf16).reshape(ny, nx, 16, qw)
            if g == 0:
                sum_first(g, off)
        dot = shares[g] * (whole[2:3] / total - whole[3:4])
        return (
            jnp.sum(jnp.where(iota((4, tokens), 1) == 4 * r + i4, dot, 0.0), axis=1, keepdims=True) / width
        )

    def sum_second(g):
        for axis, count, other_count, own_buf, got, out, out2 in (
            (0, ny, nx, px, rx, axs, rx2), (1, nx, ny, py, ry, ays, ry2),
        ):
            for j in range(1, other_count):
                arrived(got.at[g, j - 1], rs_r1.at[g, axis, j - 1])
            for jj in range(count):
                j = (jj + 1) % count
                k0 = lax.rem((y, x)[axis] + j, count)
                own_block = own_buf[g, k0, x] if axis == 0 else own_buf[g, y, k0]
                acc = own_block.astype(f32)
                for k in range(other_count - 1):
                    acc = acc + got[g, k, k0].astype(f32)
                for d in range(2):
                    four = jnp.concatenate([acc[4 * d : 4 * d + 4], acc[8 + 4 * d : 12 + 4 * d]], axis=0)
                    rest = four[:, cut:]
                    if 2 * cut > qw:
                        rest = jnp.concatenate([rest, jnp.zeros((8, 2 * cut - qw), f32)], axis=1)
                    out[g, j, d] = jnp.concatenate([four[:, :cut], rest], axis=0).astype(bf16)
                if j > 0:
                    for d in range(2):
                        device = at(k0, x, d) if axis == 0 else at(y, k0, d)
                        push(remote(out.at[g, j, d], out2.at[g, j, c], rs_s2.at[g, axis, j, d], rs_r2.at[g, axis, j, c], device))
                else:
                    push(remote(out.at[g, 0, 1 - c], out2.at[g, 0, c], rs_s2.at[g, axis, 0, 0], rs_r2.at[g, axis, 0, c], sibling))
                    out2[g, 0, c] = out[g, 0, c]

    zrs = [
        to_vocab(zrs_s.at[g], zrs_r.at[g], lambda zz, g=g: zs.at[g, zz], zr.at[g])
        for g in range(2)
    ]
    zag = [
        to_vocab(zag_s.at[g], zag_r.at[g], lambda zz, g=g: zo.at[g, v], zo.at[g])
        for g in range(2)
    ]

    def vocab_start(g):
        for buf, axis, count, off in ((rx2, 0, ny, 0), (ry2, 1, nx, xw)):
            for j in range(1, count):
                for s in range(2):
                    arrived(buf.at[g, j, s], rs_r2.at[g, axis, j, s])
            arrived(buf.at[g, 0, 1 - c], rs_r2.at[g, axis, 0, 1 - c])
            for s in range(2):
                acc = buf[g, 0, s].astype(f32)
                for j in range(1, count):
                    acc = acc + buf[g, j, s].astype(f32)
                wide = jnp.concatenate([acc[0:8], acc[8:16, : qw - cut]], axis=1)
                sum4[:, s * dh + off : s * dh + off + qw] = wide[0:4]
                sum4[:, s * dh + off + qw : s * dh + off + 2 * qw] = wide[4:8]
        for zz in range(nz):
            zs[g, zz] = fold4(sum4[:, starts[zz] : starts[zz] + LANES])
        zrs[g][0]()
        zr[g, v] = zs[g, v]

    def vocab_sum(g):
        zrs[g][1]()
        acc = zr[g, 0].astype(f32)
        for zz in range(1, nz):
            acc = acc + zr[g, zz].astype(f32)
        return unfold4(acc)

    def write(g, out):
        zag[g][1]()
        for zz in range(nz):
            out[:, starts[zz] : starts[zz] + LANES] = unfold4(zo[g, zz].astype(f32)).astype(bf16)

    a2a = to_rows(a2a_ss.at[0], a2a_rs.at[0], lambda rr: a2a_s.at[rr], a2a_r)
    pag = to_rows(pag_s.at[0], pag_r.at[0], lambda rr: po, pr)
    zga = to_vocab(zga_s.at[0], zga_r.at[0], lambda zz: gs.at[zz], gr)
    zgs = to_vocab(zg_s.at[0], zg_r.at[0], lambda zz: zg.at[v], zg)

    gather_first(0)
    gather_second(0)
    gather_first(1)

    for load in loads[3:]:
        load.wait()
    ir = iota((rows * 16, 4 * heads), 0)
    im = iota((rows * 16, 4 * heads), 1)
    kk = ir & 15
    pick = (kk < 8) & (im == (kk >> 1) * heads + 2 * (ir >> 4) + (kk & 1))
    a2a_s[...] = (
        nn(pick.astype(f32).astype(bf16), attn[...].reshape(4 * heads, hd)).astype(bf16).reshape(rows, 16, hd)
    )
    a2a_r[r] = a2a_s[r]

    it = iota((tokens, rows * 16), 0)
    il = iota((tokens, rows * 16), 1)
    base = 16 * (it >> 2) + (it & 3)
    sel[0:tokens, :] = (il == base + 4).astype(f32).astype(bf16)
    sel[tokens : 2 * tokens, :] = (il == base + 12).astype(f32).astype(bf16)
    ig = iota((16, rows * 16), 0)
    kg = iota((16, rows * 16), 1) & 15
    sel[2 * tokens : 2 * tokens + 16, :] = (
        ((ig == 0) & (kg < 2)) | ((ig == 1) & (kg >= 8) & (kg < 10))
    ).astype(f32).astype(bf16)
    base = 16 * (it >> 2) + 2 * (it & 3)
    for h in range(2):
        gather_v[h * tokens : (h + 1) * tokens, :] = (il == base + h).astype(f32).astype(bf16)
    opw[...] = jnp.zeros(opw.shape, bf16)
    shift = pl.multiple_of(v * step % 128, 16)
    opw[pl.ds(shift, step), :] = out_proj_t[...]

    w_copy.wait()
    arrived(w2.at[1 - c], sib_r.at[1])
    gather_second(1)
    gather_wait(0)
    logits_start(0)
    top_m = stats_start(0)
    gather_wait(1)
    logits_start(1)
    stats_second(0)
    top_t = stats_start(1)
    a2a[0]()
    stats_second(1)
    dot_mean = grads_start(0, top_m)
    grads_start(1, top_t)
    sum_second(0)
    sum_first(1, 0)
    sum_first(1, xw)
    vocab_start(0)

    for n in range(0, dh, qw):
        head_out[:, n : n + qw] = nn(gt[pl.ds(pl.multiple_of((1 - c) * vb, 16), vb), :], hid[:, n : n + qw]).astype(bf16)
    head_copy = remote(head_out, o_head.at[:, own_cols], sib_s.at[4], sib_r.at[4], sibling)
    push(head_copy)

    sum_second(1)
    grad = vocab_sum(0)

    cols = pl.ds(window, LANES)
    normed4 = st4[:, cols]
    residual = inv4[:, 0:1] * (grad * gain_row[:, cols] - normed4 * dot_mean)
    gain_term = jnp.sum(grad * normed4, axis=0, keepdims=True)
    gain_high = gain_term.astype(bf16).astype(f32)
    po[...] = fold(
        jnp.concatenate([gain_high, gain_term - gain_high, jnp.zeros((2, LANES), f32), residual], axis=0)
    )
    pag[0]()
    pr[r] = po[...]
    zo[0, v] = fold4(residual)
    zag[0][0]()
    vocab_start(1)

    a2a[1]()
    received = a2a_r[...].reshape(rows * 16, hd)
    for h in range(2):
        vals[:, h * hd : (h + 1) * hd] = nn(gather_v[h * tokens : (h + 1) * tokens, :], received).astype(bf16)

    pag[1]()
    picked = nn(sel[...], pr[...].reshape(rows * 16, HALF))
    columns = jnp.concatenate([picked[0:tokens], picked[tokens : 2 * tokens]], axis=1)
    attn_term = nn(columns.astype(bf16), opw[...])
    for zz in range(nz):
        gs[zz] = fold(attn_term[8 * zz : 8 * zz + 8])
    zga[0]()
    gr[v] = gs[v]
    zg[v] = jnp.concatenate(
        [picked[2 * tokens + k // 2 : 2 * tokens + k // 2 + 1, k % 2 * 128 : k % 2 * 128 + 128] for k in range(LANES // 128)],
        axis=0,
    )
    zgs[0]()
    zo[1, v] = fold4(vocab_sum(1))
    zag[1][0]()

    for n in range(0, dh, qw):
        o_head[:, pl.ds(pl.multiple_of(c * dh + n, 128), qw)] = nn(
            gt[pl.ds(pl.multiple_of(c * vb, 16), vb), :], hid[:, n : n + qw]
        ).astype(bf16)
    proj_s[...] = nn(jnp.transpose(columns).astype(bf16), vals[...]).astype(bf16)
    o_proj_t[...] = proj_s[pl.ds(shift, step), :]

    arrived(o_head.at[:, sib_cols], sib_r.at[4])
    for copy in sends:
        copy.wait_send()
    write(0, o_res)
    zgs[1]()
    for zz in range(nz):
        o_gain[starts[zz] // 128 : (starts[zz] + LANES) // 128, :] = zg[zz]
    zga[1]()
    acc = gr[0].astype(f32)
    for zz in range(1, nz):
        acc = acc + gr[zz].astype(f32)
    for h in range(2):
        attn_s[pl.ds(h, 8, stride=2), :] = acc[8 * h : 8 * h + 8]
    o_attn[...] = attn_s[...].astype(bf16)
    write(1, o_trunk)


def finish(*refs):
    sources, targets, held, sem_in, sem_out = refs[0:6], refs[6:12], refs[12:18], refs[18], refs[19]
    pieces = []
    for src, dst, buf in zip(sources, targets, held):
        rows = src.shape[0]
        cut = rows // 9 * 3 if rows % 144 == 0 else rows
        for at in range(0, rows, cut):
            pieces.append((src.at[at : at + cut], dst.at[at : at + cut], buf.at[at : at + cut]))
    pieces.sort(key=lambda piece: -piece[0].shape[0] * piece[0].shape[1])
    loads = [pltpu.make_async_copy(src, buf, sem_in.at[i]) for i, (src, _, buf) in enumerate(pieces)]
    stores = [pltpu.make_async_copy(buf, dst, sem_out.at[i]) for i, (_, dst, buf) in enumerate(pieces)]
    for load in loads:
        load.start()
    for load, store in zip(loads, stores):
        load.wait()
        store.start()
    for store in stores:
        store.wait()


def local(dims, trunk_hidden, mtp_state, mtp_gain, head_weight, target_ids, mtp_target_ids, attn_values, out_proj):
    nx, ny, nz, width = dims
    rows = 2 * nx * ny
    tokens = 4 * rows
    vb = head_weight.shape[0]
    dh = width // 2
    qw = dh // 4
    cut = -(-qw // 256) * 128
    step = out_proj.shape[1]
    heads, hd = attn_values.shape[1:]
    vmem = pltpu.VMEM
    dma = pltpu.SemaphoreType.DMA
    scratch = [
        vmem((4, width), bf16),
        vmem((4, width), bf16),
        vmem((width // 128, 128), bf16),
        vmem((1, tokens), jnp.int32),
        vmem((1, tokens), jnp.int32),
        vmem((4, heads, hd), bf16),
        vmem((step, 2 * hd), bf16),
        vmem((1, width), f32),
        vmem((8, width), f32),
        vmem((4, width), f32),
        vmem((4, 128), f32),
        vmem((8, dh), f32),
        vmem((2, vb, dh), bf16),
        vmem((2, ny, nx, 16, qw), bf16),
        vmem((2, ny, nx, 16, qw), bf16),
        vmem((2 * tokens, dh), bf16),
        vmem((2, 2 * vb, tokens), f32),
        vmem((2, 2 * vb, tokens), f32),
        vmem((2, nx * ny, 4, tokens), f32),
        vmem((2, nz, 4, tokens), f32),
        vmem((2 * vb, 2 * tokens), bf16),
        vmem((2, ny, nx, 16, qw), bf16),
        vmem((2, ny, nx, 16, qw), bf16),
        vmem((vb, dh), bf16),
        vmem((2, max(nx - 1, 1), ny, 16, qw), bf16),
        vmem((2, max(ny - 1, 1), nx, 16, qw), bf16),
        vmem((2, ny, 2, 16, cut), bf16),
        vmem((2, nx, 2, 16, cut), bf16),
        vmem((2, ny, 2, 16, cut), bf16),
        vmem((2, nx, 2, 16, cut), bf16),
        vmem((4, width), f32),
        vmem((2, nz, 16, LANES // 4), bf16),
        vmem((2, nz, 16, LANES // 4), bf16),
        vmem((2, nz, 16, LANES // 4), bf16),
        vmem((16, HALF), bf16),
        vmem((rows, 16, HALF), bf16),
        vmem((2 * tokens + 16, rows * 16), bf16),
        vmem((2 * tokens, rows * 16), bf16),
        vmem((rows, 16, hd), bf16),
        vmem((rows, 16, hd), bf16),
        vmem((tokens, 2 * hd), bf16),
        vmem((LANES, 2 * hd), bf16),
        vmem((nz, LANES // 128, 128), f32),
        vmem((nz, 16, hd), bf16),
        vmem((nz, 16, hd), bf16),
        vmem((LANES, 2 * hd), bf16),
        vmem((16, hd), f32),
        dma((8,)),
        dma((5,)),
        dma((5,)),
        dma((2, 2, 3)),
        dma((2, 2, 4, 3)),
        dma((2, 2, ny, nx)),
        dma((2, 2)),
        dma((2,)),
        dma((2,)),
        dma((2,)),
        dma((2,)),
        dma((2, 2, 3)),
        dma((2, 2, 3)),
        dma((2, 2, 4, 2)),
        dma((2, 2, 4, 2)),
        dma((2,)),
        dma((2,)),
        dma((2,)),
        dma((2,)),
        dma((1,)),
        dma((1,)),
        dma((1,)),
        dma((1,)),
        dma((1,)),
        dma((1,)),
        dma((1,)),
        dma((1,)),
    ]
    in_vmem = pl.BlockSpec(memory_space=pltpu.VMEM)
    in_hbm = pl.BlockSpec(memory_space=pl.ANY)
    shape = jax.ShapeDtypeStruct
    shapes = [
        shape((4, width), bf16),
        shape((4, width), bf16),
        shape((width // 128, 128), f32),
        shape((vb, width), bf16),
        shape((16, hd), bf16),
        shape((step, 2 * hd), bf16),
    ]
    results = pl.pallas_call(
        functools.partial(kernel, dims),
        out_shape=shapes,
        in_specs=[pl.BlockSpec(memory_space=pltpu.HBM)] * 8,
        out_specs=[in_vmem] * 6,
        scratch_shapes=scratch,
        compiler_params=pltpu.CompilerParams(
            collective_id=0, has_side_effects=True, vmem_limit_bytes=60 * 2**20
        ),
        name="head_backward",
    )(
        trunk_hidden,
        mtp_state,
        mtp_gain.reshape(width // 128, 128),
        head_weight,
        target_ids.reshape(1, -1),
        mtp_target_ids.reshape(1, -1),
        attn_values,
        out_proj.T,
    )
    trunk_out, res_out, gain_out, head_out, attn_out, proj_out = pl.pallas_call(
        finish,
        out_shape=shapes,
        in_specs=[in_hbm] * len(shapes),
        out_specs=[in_hbm] * len(shapes),
        scratch_shapes=[vmem(s.shape, s.dtype) for s in shapes] + [dma((8,)), dma((8,))],
        compiler_params=pltpu.CompilerParams(vmem_limit_bytes=60 * 2**20),
        name="results",
    )(*results)
    grad_attn = attn_out.reshape(8, 2, hd)
    return (trunk_out, res_out, gain_out.reshape(width), head_out, grad_attn, proj_out.T)


def solution(mesh):
    nz, rows = mesh.shape["vocab"], mesh.shape["rows"]
    nx = {32: 4, 8: 2, 2: 1}[rows]

    def run(*args):
        dims = (nx, rows // 2 // nx, nz, args[0].shape[1])
        return local(dims, *args)

    return jax.shard_map(
        run,
        mesh=mesh,
        in_specs=(
            P("rows", None),
            P("rows", None),
            P(),
            P(("vocab", "rows"), None),
            P(),
            P(),
            P("rows", None, None),
            P("rows", "vocab"),
        ),
        out_specs=(
            P("rows", None),
            P("rows", None),
            P(),
            P(("vocab", "rows"), None),
            P("vocab", "rows", None),
            P("rows", "vocab"),
        ),
        check_vma=False,
    )
```

```python
import functools

import jax
import jax.numpy as jnp
from jax import lax
from jax.experimental import pallas as pl
from jax.experimental.pallas import tpu as pltpu
from jax.sharding import PartitionSpec as P

loss_scale = 8.0
mtp_share = 0.3
norm_eps = 1e-06
f32 = jnp.float32
bf16 = jnp.bfloat16
LANES = 512
HALF = LANES // 2


def nn(a, b):
    return lax.dot_general(a, b, (((1,), (0,)), ((), ())), preferred_element_type=f32)


def nt(a, b):
    return lax.dot_general(a, b, (((1,), (1,)), ((), ())), preferred_element_type=f32)


def iota(shape, axis):
    return lax.broadcasted_iota(jnp.int32, shape, axis)


def fold(block):
    w = block.shape[1] // 2
    return jnp.concatenate([block[:, :w], block[:, w:]], axis=0).astype(bf16)


def unfold(block):
    return jnp.concatenate([block[:8], block[8:]], axis=1)


def fold4(block):
    w = block.shape[1] // 4
    return jnp.concatenate([block[:, k * w : (k + 1) * w] for k in range(4)], axis=0).astype(bf16)


def unfold4(block):
    return jnp.concatenate([block[4 * k : 4 * k + 4] for k in range(4)], axis=1)


def remote(src, dst, send, recv, device):
    return pltpu.make_async_remote_copy(
        src_ref=src,
        dst_ref=dst,
        send_sem=send,
        recv_sem=recv,
        device_id=device,
        device_id_type=pl.DeviceIdType.MESH,
    )


def kernel(
    dims,
    trunk_h, state_h, gain_h, w_hbm, tids_h, mids_h, attn_h, out_proj_h,
    o_trunk, o_res, o_gain, o_head, o_attn, o_proj_t,
    trunk, state, gain, tids, mids, attn, out_proj_t,
    gain_row, own8, st4, inv4, sib8, w2, hx, hy, hid, lt_own, lt_sib, st_plane, st_z,
    gt, px, py, head_out, head_own, head_in, rx, ry, axs, ays, rx2, ry2, sum4, zs, zr, zo, po, pr, sel, gather_v,
    a2a_s, a2a_r, vals, opw, zg, gs, gr, proj_s, attn_s,
    cp_sem, sib_s, sib_r, ag_s1, ag_s2, ag_r, ag_r2, pst_s, pst_r, zst_s, zst_r,
    rs_s1, rs_r1, rs_s2, rs_r2, zrs_s, zrs_r, zag_s, zag_r, pag_s, pag_r,
    a2a_ss, a2a_rs, zg_s, zg_r, zga_s, zga_r,
):
    nx, ny, nz, width = dims
    rows = 2 * nx * ny
    chips = nx * ny
    tokens = 4 * rows
    vb = w_hbm.shape[0]
    dh = width // 2
    xw = dh // 2
    qw = xw // 2
    cut = -(-qw // 256) * 128
    heads, hd = attn.shape[1:]
    step = width // nz
    starts = [zz * step // 128 * 128 for zz in range(nz)]
    shares = (loss_scale * mtp_share, loss_scale)
    far_chip = (ny // 2) * nx + nx // 2
    far_row = 2 * far_chip

    v = lax.axis_index("vocab")
    r = lax.axis_index("rows")
    c = lax.rem(r, 2)
    chip = r // 2
    x = lax.rem(chip, nx)
    y = chip // nx
    sibling = (v, r + 1 - 2 * c)
    window = pl.multiple_of(v * step // 128 * 128, 128)

    def at(yy, xx, core):
        return (v, (yy * nx + xx) * 2 + core)

    def arrived(ref, sem):
        remote(ref, ref, sib_s.at[0], sem, sibling).wait_recv()

    sends = []

    def push(copy):
        copy.start()
        sends.append(copy)

    def drain():
        for copy in sends:
            copy.wait_send()
        sends.clear()

    def exchange(count, copy, slots, send, recv):
        def start(i, carry):
            copy(i).start()
            return carry

        def finish():
            whole = slots.at[0 : count - 1]
            done = remote(whole, whole, send, recv, sibling)
            done.wait_recv()
            done.wait_send()

        return (lambda: lax.fori_loop(1, count, start, 0)), finish

    def to_vocab(send, recv, source, slots):
        def copy(i):
            zz = lax.rem(v + nz // 2 + (1 - 2 * lax.rem(i + 1, 2)) * (i // 2), nz)
            return remote(source(zz), slots.at[v], send, recv, (zz, r))

        return exchange(nz, copy, slots, send, recv)

    def to_rows(send, recv, source, slots):
        def copy(i):
            rr = lax.rem(r + 1 + lax.rem(i + far_row - 2, rows - 1), rows)
            return remote(source(rr), slots.at[r], send, recv, (v, rr))

        return exchange(rows, copy, slots, send, recv)

    def to_chips(send, recv, slots):
        def copy(i):
            cc = lax.rem(chip + 1 + lax.rem(i + far_chip - 2, chips - 1), chips)
            return remote(slots.at[chip], slots.at[chip], send, recv, (v, 2 * cc + c))

        return exchange(chips, copy, slots, send, recv)

    own_cols = pl.ds(pl.multiple_of(c * dh, 128), dh)
    sib_cols = pl.ds(pl.multiple_of((1 - c) * dh, 128), dh)
    w_copy = pltpu.make_async_copy(w_hbm.at[:, own_cols], w2.at[c], cp_sem.at[0])
    loads = [
        pltpu.make_async_copy(src, dst, cp_sem.at[1 + i])
        for i, (src, dst) in enumerate(
            (
                (state_h, state), (gain_h, gain), (trunk_h, trunk), (tids_h, tids), (mids_h, mids),
                (attn_h, attn), (out_proj_h, out_proj_t),
            )
        )
    ]
    for load in loads:
        load.start()
    w_copy.start()

    bar = pltpu.get_barrier_semaphore()

    def greet_rows(i, carry):
        pl.semaphore_signal(
            bar, inc=1, device_id=(v, lax.rem(r + i, rows)), device_id_type=pl.DeviceIdType.MESH
        )
        return carry

    def greet_vocab(i, carry):
        pl.semaphore_signal(
            bar, inc=1, device_id=(lax.rem(v + i, nz), r), device_id_type=pl.DeviceIdType.MESH
        )
        return carry

    lax.fori_loop(1, nz, greet_vocab, 0)
    lax.fori_loop(1, rows, greet_rows, 0)

    for load in loads[:3]:
        load.wait()
    sv = state[...].astype(f32)
    inverse = lax.rsqrt(jnp.mean(sv * sv, axis=-1, keepdims=True) + norm_eps)
    normed = sv * inverse
    for k in range(width // 128):
        gain_row[0:1, k * 128 : (k + 1) * 128] = gain[k : k + 1, :].astype(f32)
    own8[0:4, :] = trunk[...].astype(f32)
    own8[4:8, :] = (normed * gain_row[...]).astype(bf16).astype(f32)
    st4[...] = normed
    inv4[...] = jnp.broadcast_to(inverse, (4, 128))

    pl.semaphore_wait(bar, rows - 1 + nz - 1)

    tok_copy = remote(own8.at[:, sib_cols], sib8, sib_s.at[0], sib_r.at[0], sibling)
    push(tok_copy)
    push(remote(w_hbm.at[:, sib_cols], w2.at[c], sib_s.at[1], sib_r.at[1], sibling))
    mine = own8[:, own_cols]
    tok_copy.wait_recv()
    other = sib8[...]
    first = c == 0
    low = jnp.where(first, mine, other)
    high = jnp.where(first, other, mine)

    def place(g, rng):
        block = jnp.concatenate([low[rng], high[rng]], axis=0)
        hx[g, y, x] = fold(block[:, :xw])
        hy[g, y, x] = fold(block[:, xw:])

    place(0, slice(4, 8))

    def gather_first(g):
        for j in range(1, nx):
            blk = hx.at[g, y, x]
            push(remote(blk, blk, ag_s1.at[g, 0, j - 1], ag_r.at[g, 0, y, x], at(y, lax.rem(x + j, nx), c)))
        for j in range(1, ny):
            blk = hy.at[g, y, x]
            push(remote(blk, blk, ag_s1.at[g, 1, j - 1], ag_r.at[g, 1, y, x], at(lax.rem(y + j, ny), x, c)))

    order = {4: (0, 1, 3, 2), 2: (0, 1), 1: (0,)}

    def gather_second(g):
        for i in range(max(nx, ny)):
            if i < nx:
                xx = lax.rem(x + order[nx][i], nx)
                blk = hx.at[g, y, xx]
                if i > 0:
                    arrived(blk, ag_r.at[g, 0, y, xx])
                for j in range(1, ny):
                    push(remote(blk, blk, ag_s2.at[g, 0, i, j - 1], ag_r2.at[g, 0], at(lax.rem(y + j, ny), x, c)))
            if i < ny:
                yy = lax.rem(y + order[ny][i], ny)
                blk = hy.at[g, yy, x]
                if i > 0:
                    arrived(blk, ag_r.at[g, 1, yy, x])
                for j in range(1, nx):
                    push(remote(blk, blk, ag_s2.at[g, 1, i, j - 1], ag_r2.at[g, 1], at(y, lax.rem(x + j, nx), c)))

    def gather_wait(g):
        arrived(hx.at[g, 0 : ny - 1], ag_r2.at[g, 0])
        arrived(hy.at[g, 0 : nx - 1] if nx == ny else hy.at[g, :, 0 : nx - 1], ag_r2.at[g, 1])

    def logits_start(g):
        for buf, off in ((hx, 0), (hy, xw)):
            block = buf[g].astype(f32).reshape(chips, 2, 8, qw)
            for k in range(2):
                hid[g * tokens : (g + 1) * tokens, off + k * qw : off + (k + 1) * qw] = (
                    block[:, k].reshape(tokens, qw).astype(bf16)
                )
        lt_own[g] = nt(w2[...].reshape(2 * vb, dh), hid[g * tokens : (g + 1) * tokens, :])
        push(remote(lt_own.at[g], lt_sib.at[g], sib_s.at[2 + g], sib_r.at[2 + g], sibling))

    vocab_id = iota((2 * vb, tokens), 0) + (v * rows + 2 * chip) * vb
    i4 = iota((4, tokens), 0)

    def onehot(g):
        return (vocab_id == (mids, tids)[g][...]).astype(f32)

    pst = [to_chips(pst_s.at[g], pst_r.at[g], st_plane.at[g]) for g in range(2)]
    zst = [
        to_vocab(zst_s.at[g], zst_r.at[g], lambda zz, g=g: st_z.at[g, v], st_z.at[g])
        for g in range(2)
    ]

    def stats_start(g):
        arrived(lt_sib.at[g], sib_r.at[2 + g])
        logits = lt_own[g] + lt_sib[g]
        top = jnp.max(logits, axis=0, keepdims=True)
        e = jnp.exp(logits - top)
        lt_sib[g] = e
        st_plane[g, chip] = jnp.where(
            i4 == 0,
            top,
            jnp.where(
                i4 == 1,
                jnp.sum(e, axis=0, keepdims=True),
                jnp.where(
                    i4 == 2,
                    jnp.sum(e * logits, axis=0, keepdims=True),
                    jnp.sum(onehot(g) * logits, axis=0, keepdims=True),
                ),
            ),
        )
        pst[g][0]()
        return top

    def merge(slots, count):
        top = slots[0][0:1]
        for s in range(1, count):
            top = jnp.maximum(top, slots[s][0:1])
        acc = jnp.zeros((4, tokens), f32)
        for s in range(count):
            tile = slots[s]
            acc = acc + jnp.where(i4 == 3, tile, tile * jnp.exp(tile[0:1] - top))
        return jnp.where(i4 == 0, top, acc)

    def stats_second(g):
        pst[g][1]()
        st_z[g, v] = merge(st_plane.at[g], chips)
        zst[g][0]()

    def sum_first(g, off):
        if off == 0:
            for j in range(1, nx):
                xx = lax.rem(x + j, nx)
                push(remote(px.at[g, :, xx], rx.at[g, j - 1], rs_s1.at[g, 0, j - 1], rs_r1.at[g, 0, j - 1], at(y, xx, c)))
        else:
            for j in range(1, ny):
                yy = lax.rem(y + j, ny)
                push(remote(py.at[g, yy], ry.at[g, j - 1], rs_s1.at[g, 1, j - 1], rs_r1.at[g, 1, j - 1], at(yy, x, c)))

    def grads_start(g, top_chip):
        zst[g][1]()
        whole = merge(st_z.at[g], nz)
        top, total = whole[0:1], whole[1:2]
        grads = lt_sib[g] * (shares[g] * jnp.exp(top_chip - top) / total) - shares[g] * onehot(g)
        gt[:, g * tokens : (g + 1) * tokens] = grads.astype(bf16)
        grads_t = jnp.transpose(grads).astype(bf16)
        for buf, off in ((px, 0), (py, xw)):
            halves = [
                nn(grads_t, w2[:, :, off + k * qw : off + (k + 1) * qw].reshape(2 * vb, qw)).reshape(chips, 8, qw)
                for k in range(2)
            ]
            buf[g] = jnp.concatenate(halves, axis=1).astype(bf16).reshape(ny, nx, 16, qw)
            if g == 0:
                sum_first(g, off)
        dot = shares[g] * (whole[2:3] / total - whole[3:4])
        return (
            jnp.sum(jnp.where(iota((4, tokens), 1) == 4 * r + i4, dot, 0.0), axis=1, keepdims=True) / width
        )

    def sum_second(g):
        for axis, count, other_count, own_buf, got, out, out2 in (
            (0, ny, nx, px, rx, axs, rx2), (1, nx, ny, py, ry, ays, ry2),
        ):
            for j in range(1, other_count):
                arrived(got.at[g, j - 1], rs_r1.at[g, axis, j - 1])
            for jj in range(count):
                j = (jj + 1) % count
                k0 = lax.rem((y, x)[axis] + j, count)
                own_block = own_buf[g, k0, x] if axis == 0 else own_buf[g, y, k0]
                acc = own_block.astype(f32)
                for k in range(other_count - 1):
                    acc = acc + got[g, k, k0].astype(f32)
                for d in range(2):
                    four = jnp.concatenate([acc[4 * d : 4 * d + 4], acc[8 + 4 * d : 12 + 4 * d]], axis=0)
                    rest = four[:, cut:]
                    if 2 * cut > qw:
                        rest = jnp.concatenate([rest, jnp.zeros((8, 2 * cut - qw), f32)], axis=1)
                    out[g, j, d] = jnp.concatenate([four[:, :cut], rest], axis=0).astype(bf16)
                if j > 0:
                    for d in range(2):
                        device = at(k0, x, d) if axis == 0 else at(y, k0, d)
                        push(remote(out.at[g, j, d], out2.at[g, j, c], rs_s2.at[g, axis, j, d], rs_r2.at[g, axis, j, c], device))
                else:
                    push(remote(out.at[g, 0, 1 - c], out2.at[g, 0, c], rs_s2.at[g, axis, 0, 0], rs_r2.at[g, axis, 0, c], sibling))
                    out2[g, 0, c] = out[g, 0, c]

    zrs = [
        to_vocab(zrs_s.at[g], zrs_r.at[g], lambda zz, g=g: zs.at[g, zz], zr.at[g])
        for g in range(2)
    ]
    zag = [
        to_vocab(zag_s.at[g], zag_r.at[g], lambda zz, g=g: zo.at[g, v], zo.at[g])
        for g in range(2)
    ]

    def vocab_start(g):
        for buf, axis, count, off in ((rx2, 0, ny, 0), (ry2, 1, nx, xw)):
            for j in range(1, count):
                for s in range(2):
                    arrived(buf.at[g, j, s], rs_r2.at[g, axis, j, s])
            arrived(buf.at[g, 0, 1 - c], rs_r2.at[g, axis, 0, 1 - c])
            for s in range(2):
                acc = buf[g, 0, s].astype(f32)
                for j in range(1, count):
                    acc = acc + buf[g, j, s].astype(f32)
                wide = jnp.concatenate([acc[0:8], acc[8:16, : qw - cut]], axis=1)
                sum4[:, s * dh + off : s * dh + off + qw] = wide[0:4]
                sum4[:, s * dh + off + qw : s * dh + off + 2 * qw] = wide[4:8]
        for zz in range(nz):
            zs[g, zz] = fold4(sum4[:, starts[zz] : starts[zz] + LANES])
        zrs[g][0]()
        zr[g, v] = zs[g, v]

    def vocab_sum(g):
        zrs[g][1]()
        acc = zr[g, 0].astype(f32)
        for zz in range(1, nz):
            acc = acc + zr[g, zz].astype(f32)
        return unfold4(acc)

    def write(g, out):
        zag[g][1]()
        for zz in range(nz):
            out[:, starts[zz] : starts[zz] + LANES] = unfold4(zo[g, zz].astype(f32)).astype(bf16)

    a2a = to_rows(a2a_ss.at[0], a2a_rs.at[0], lambda rr: a2a_s.at[rr], a2a_r)
    pag = to_rows(pag_s.at[0], pag_r.at[0], lambda rr: po, pr)
    zga = to_vocab(zga_s.at[0], zga_r.at[0], lambda zz: gs.at[zz], gr)
    zgs = to_vocab(zg_s.at[0], zg_r.at[0], lambda zz: zg.at[v], zg)

    gather_first(0)
    place(1, slice(0, 4))
    gather_second(0)
    gather_first(1)

    for load in loads[3:]:
        load.wait()
    ir = iota((rows * 16, 4 * heads), 0)
    im = iota((rows * 16, 4 * heads), 1)
    kk = ir & 15
    pick = (kk < 8) & (im == (kk >> 1) * heads + 2 * (ir >> 4) + (kk & 1))
    a2a_s[...] = (
        nn(pick.astype(f32).astype(bf16), attn[...].reshape(4 * heads, hd)).astype(bf16).reshape(rows, 16, hd)
    )
    a2a_r[r] = a2a_s[r]

    it = iota((tokens, rows * 16), 0)
    il = iota((tokens, rows * 16), 1)
    base = 16 * (it >> 2) + (it & 3)
    sel[0:tokens, :] = (il == base + 4).astype(f32).astype(bf16)
    sel[tokens : 2 * tokens, :] = (il == base + 12).astype(f32).astype(bf16)
    ig = iota((16, rows * 16), 0)
    kg = iota((16, rows * 16), 1) & 15
    sel[2 * tokens : 2 * tokens + 16, :] = (
        ((ig == 0) & (kg < 2)) | ((ig == 1) & (kg >= 8) & (kg < 10))
    ).astype(f32).astype(bf16)
    base = 16 * (it >> 2) + 2 * (it & 3)
    for h in range(2):
        gather_v[h * tokens : (h + 1) * tokens, :] = (il == base + h).astype(f32).astype(bf16)
    opw[...] = jnp.zeros(opw.shape, bf16)
    shift = pl.multiple_of(v * step % 128, 16)
    opw[pl.ds(shift, step), :] = out_proj_t[...]

    w_copy.wait()
    arrived(w2.at[1 - c], sib_r.at[1])
    gather_second(1)
    gather_wait(0)
    logits_start(0)
    top_m = stats_start(0)
    gather_wait(1)
    logits_start(1)
    stats_second(0)
    top_t = stats_start(1)
    a2a[0]()
    drain()
    stats_second(1)
    dot_mean = grads_start(0, top_m)
    grads_start(1, top_t)
    sum_second(0)
    sum_first(1, 0)
    sum_first(1, xw)
    vocab_start(0)

    for n in range(0, dh, qw):
        head_out[:, n : n + qw] = nn(gt[pl.ds(pl.multiple_of((1 - c) * vb, 16), vb), :], hid[:, n : n + qw]).astype(bf16)
    push(remote(head_out, head_in, sib_s.at[4], sib_r.at[4], sibling))
    for n in range(0, dh, qw):
        head_own[:, n : n + qw] = nn(gt[pl.ds(pl.multiple_of(c * vb, 16), vb), :], hid[:, n : n + qw]).astype(bf16)
    head_stores = [
        pltpu.make_async_copy(head_own, o_head.at[:, own_cols], cp_sem.at[8]),
        pltpu.make_async_copy(head_in, o_head.at[:, sib_cols], cp_sem.at[9]),
    ]
    head_stores[0].start()

    sum_second(1)
    grad = vocab_sum(0)

    cols = pl.ds(window, LANES)
    normed4 = st4[:, cols]
    residual = inv4[:, 0:1] * (grad * gain_row[:, cols] - normed4 * dot_mean)
    gain_term = jnp.sum(grad * normed4, axis=0, keepdims=True)
    gain_high = gain_term.astype(bf16).astype(f32)
    po[...] = fold(
        jnp.concatenate([gain_high, gain_term - gain_high, jnp.zeros((2, LANES), f32), residual], axis=0)
    )
    pag[0]()
    pr[r] = po[...]
    zo[0, v] = fold4(residual)
    zag[0][0]()
    vocab_start(1)

    a2a[1]()
    received = a2a_r[...].reshape(rows * 16, hd)
    for h in range(2):
        vals[:, h * hd : (h + 1) * hd] = nn(gather_v[h * tokens : (h + 1) * tokens, :], received).astype(bf16)

    arrived(head_in, sib_r.at[4])
    head_stores[1].start()

    pag[1]()
    picked = nn(sel[...], pr[...].reshape(rows * 16, HALF))
    columns = jnp.concatenate([picked[0:tokens], picked[tokens : 2 * tokens]], axis=1)
    attn_term = nn(columns.astype(bf16), opw[...])
    for zz in range(nz):
        gs[zz] = fold(attn_term[8 * zz : 8 * zz + 8])
    zga[0]()
    gr[v] = gs[v]
    zg[v] = jnp.concatenate(
        [picked[2 * tokens + k // 2 : 2 * tokens + k // 2 + 1, k % 2 * 128 : k % 2 * 128 + 128] for k in range(LANES // 128)],
        axis=0,
    )
    zgs[0]()
    zo[1, v] = fold4(vocab_sum(1))
    zag[1][0]()

    proj_s[...] = nn(jnp.transpose(columns).astype(bf16), vals[...]).astype(bf16)
    o_proj_t[...] = proj_s[pl.ds(shift, step), :]

    drain()
    write(0, o_res)
    zgs[1]()
    for zz in range(nz):
        o_gain[starts[zz] // 128 : (starts[zz] + LANES) // 128, :] = zg[zz]
    zga[1]()
    acc = gr[0].astype(f32)
    for zz in range(1, nz):
        acc = acc + gr[zz].astype(f32)
    for h in range(2):
        attn_s[pl.ds(h, 8, stride=2), :] = acc[8 * h : 8 * h + 8]
    o_attn[...] = attn_s[...].astype(bf16)
    write(1, o_trunk)
    for store in head_stores:
        store.wait()


def finish(*refs):
    sources, targets, held, sem_in, sem_out = refs[0:6], refs[6:12], refs[12:18], refs[18], refs[19]
    pieces = []
    for src, dst, buf in zip(sources, targets, held):
        rows = src.shape[0]
        cut = rows // 9 * 3 if rows % 144 == 0 else rows
        for at in range(0, rows, cut):
            pieces.append((src.at[at : at + cut], dst.at[at : at + cut], buf.at[at : at + cut]))
    pieces.sort(key=lambda piece: -piece[0].shape[0] * piece[0].shape[1])
    loads = [pltpu.make_async_copy(src, buf, sem_in.at[i]) for i, (src, _, buf) in enumerate(pieces)]
    stores = [pltpu.make_async_copy(buf, dst, sem_out.at[i]) for i, (_, dst, buf) in enumerate(pieces)]
    for load in loads:
        load.start()
    for load, store in zip(loads, stores):
        load.wait()
        store.start()
    for store in stores:
        store.wait()


def local(dims, trunk_hidden, mtp_state, mtp_gain, head_weight, target_ids, mtp_target_ids, attn_values, out_proj):
    nx, ny, nz, width = dims
    rows = 2 * nx * ny
    tokens = 4 * rows
    vb = head_weight.shape[0]
    dh = width // 2
    qw = dh // 4
    cut = -(-qw // 256) * 128
    step = out_proj.shape[1]
    heads, hd = attn_values.shape[1:]
    vmem = pltpu.VMEM
    dma = pltpu.SemaphoreType.DMA
    scratch = [
        vmem((4, width), bf16),
        vmem((4, width), bf16),
        vmem((width // 128, 128), bf16),
        vmem((1, tokens), jnp.int32),
        vmem((1, tokens), jnp.int32),
        vmem((4, heads, hd), bf16),
        vmem((step, 2 * hd), bf16),
        vmem((1, width), f32),
        vmem((8, width), f32),
        vmem((4, width), f32),
        vmem((4, 128), f32),
        vmem((8, dh), f32),
        vmem((2, vb, dh), bf16),
        vmem((2, ny, nx, 16, qw), bf16),
        vmem((2, ny, nx, 16, qw), bf16),
        vmem((2 * tokens, dh), bf16),
        vmem((2, 2 * vb, tokens), f32),
        vmem((2, 2 * vb, tokens), f32),
        vmem((2, nx * ny, 4, tokens), f32),
        vmem((2, nz, 4, tokens), f32),
        vmem((2 * vb, 2 * tokens), bf16),
        vmem((2, ny, nx, 16, qw), bf16),
        vmem((2, ny, nx, 16, qw), bf16),
        vmem((vb, dh), bf16),
        vmem((vb, dh), bf16),
        vmem((vb, dh), bf16),
        vmem((2, max(nx - 1, 1), ny, 16, qw), bf16),
        vmem((2, max(ny - 1, 1), nx, 16, qw), bf16),
        vmem((2, ny, 2, 16, cut), bf16),
        vmem((2, nx, 2, 16, cut), bf16),
        vmem((2, ny, 2, 16, cut), bf16),
        vmem((2, nx, 2, 16, cut), bf16),
        vmem((4, width), f32),
        vmem((2, nz, 16, LANES // 4), bf16),
        vmem((2, nz, 16, LANES // 4), bf16),
        vmem((2, nz, 16, LANES // 4), bf16),
        vmem((16, HALF), bf16),
        vmem((rows, 16, HALF), bf16),
        vmem((2 * tokens + 16, rows * 16), bf16),
        vmem((2 * tokens, rows * 16), bf16),
        vmem((rows, 16, hd), bf16),
        vmem((rows, 16, hd), bf16),
        vmem((tokens, 2 * hd), bf16),
        vmem((LANES, 2 * hd), bf16),
        vmem((nz, LANES // 128, 128), f32),
        vmem((nz, 16, hd), bf16),
        vmem((nz, 16, hd), bf16),
        vmem((LANES, 2 * hd), bf16),
        vmem((16, hd), f32),
        dma((10,)),
        dma((5,)),
        dma((5,)),
        dma((2, 2, 3)),
        dma((2, 2, 4, 3)),
        dma((2, 2, ny, nx)),
        dma((2, 2)),
        dma((2,)),
        dma((2,)),
        dma((2,)),
        dma((2,)),
        dma((2, 2, 3)),
        dma((2, 2, 3)),
        dma((2, 2, 4, 2)),
        dma((2, 2, 4, 2)),
        dma((2,)),
        dma((2,)),
        dma((2,)),
        dma((2,)),
        dma((1,)),
        dma((1,)),
        dma((1,)),
        dma((1,)),
        dma((1,)),
        dma((1,)),
        dma((1,)),
        dma((1,)),
    ]
    in_vmem = pl.BlockSpec(memory_space=pltpu.VMEM)
    in_hbm = pl.BlockSpec(memory_space=pl.ANY)
    shape = jax.ShapeDtypeStruct
    shapes = [
        shape((4, width), bf16),
        shape((4, width), bf16),
        shape((width // 128, 128), f32),
        shape((vb, width), bf16),
        shape((16, hd), bf16),
        shape((step, 2 * hd), bf16),
    ]
    results = pl.pallas_call(
        functools.partial(kernel, dims),
        out_shape=shapes,
        in_specs=[pl.BlockSpec(memory_space=pltpu.HBM)] * 8,
        out_specs=[in_vmem] * 3 + [in_hbm] + [in_vmem] * 2,
        scratch_shapes=scratch,
        compiler_params=pltpu.CompilerParams(
            collective_id=0, has_side_effects=True, vmem_limit_bytes=60 * 2**20
        ),
        name="head_backward",
    )(
        trunk_hidden,
        mtp_state,
        mtp_gain.reshape(width // 128, 128),
        head_weight,
        target_ids.reshape(1, -1),
        mtp_target_ids.reshape(1, -1),
        attn_values,
        out_proj.T,
    )
    trunk_out, res_out, gain_out, head_out, attn_out, proj_out = pl.pallas_call(
        finish,
        out_shape=shapes,
        in_specs=[in_hbm] * len(shapes),
        out_specs=[in_hbm] * len(shapes),
        scratch_shapes=[vmem(s.shape, s.dtype) for s in shapes] + [dma((8,)), dma((8,))],
        compiler_params=pltpu.CompilerParams(vmem_limit_bytes=60 * 2**20),
        name="results",
    )(*results)
    grad_attn = attn_out.reshape(8, 2, hd)
    return (trunk_out, res_out, gain_out.reshape(width), head_out, grad_attn, proj_out.T)


def solution(mesh):
    nz, rows = mesh.shape["vocab"], mesh.shape["rows"]
    nx = {32: 4, 8: 2, 2: 1}[rows]

    def run(*args):
        dims = (nx, rows // 2 // nx, nz, args[0].shape[1])
        return local(dims, *args)

    return jax.shard_map(
        run,
        mesh=mesh,
        in_specs=(
            P("rows", None),
            P("rows", None),
            P(),
            P(("vocab", "rows"), None),
            P(),
            P(),
            P("rows", None, None),
            P("rows", "vocab"),
        ),
        out_specs=(
            P("rows", None),
            P("rows", None),
            P(),
            P(("vocab", "rows"), None),
            P("vocab", "rows", None),
            P("rows", "vocab"),
        ),
        check_vma=False,
    )
```

```python
import functools

import jax
import jax.numpy as jnp
from jax import lax
from jax.experimental import pallas as pl
from jax.experimental.pallas import tpu as pltpu
from jax.sharding import PartitionSpec as P

loss_scale = 8.0
mtp_share = 0.3
norm_eps = 1e-06
f32 = jnp.float32
bf16 = jnp.bfloat16
LANES = 512
HALF = LANES // 2


def nn(a, b):
    return lax.dot_general(a, b, (((1,), (0,)), ((), ())), preferred_element_type=f32)


def nt(a, b):
    return lax.dot_general(a, b, (((1,), (1,)), ((), ())), preferred_element_type=f32)


def iota(shape, axis):
    return lax.broadcasted_iota(jnp.int32, shape, axis)


def fold(block):
    w = block.shape[1] // 2
    return jnp.concatenate([block[:, :w], block[:, w:]], axis=0).astype(bf16)


def unfold(block):
    return jnp.concatenate([block[:8], block[8:]], axis=1)


def fold4(block):
    w = block.shape[1] // 4
    return jnp.concatenate([block[:, k * w : (k + 1) * w] for k in range(4)], axis=0).astype(bf16)


def unfold4(block):
    return jnp.concatenate([block[4 * k : 4 * k + 4] for k in range(4)], axis=1)


def remote(src, dst, send, recv, device):
    return pltpu.make_async_remote_copy(
        src_ref=src,
        dst_ref=dst,
        send_sem=send,
        recv_sem=recv,
        device_id=device,
        device_id_type=pl.DeviceIdType.MESH,
    )


def kernel(
    dims,
    trunk_h, state_h, gain_h, w_hbm, tids_h, mids_h, attn_h, out_proj_h,
    o_trunk, o_res, o_gain, o_head, o_attn, o_proj_t,
    trunk, state, gain, tids, mids, attn, out_proj_t,
    gain_row, own8, st4, inv4, sib8, w2, hx, hy, hid, lt_own, lt_sib, st_plane, st_z,
    gt, px, py, head_out, head_own, head_in, rx, ry, axs, ays, rx2, ry2, sum4, zs, zr, zo, po, pr, sel, gather_v,
    a2a_s, a2a_r, vals, opw, zg, gs, gr, proj_s, attn_s,
    cp_sem, sib_s, sib_r, ag_s1, ag_s2, ag_r, ag_r2, pst_s, pst_r, zst_s, zst_r,
    rs_s1, rs_r1, rs_s2, rs_r2, zrs_s, zrs_r, zag_s, zag_r, pag_s, pag_r,
    a2a_ss, a2a_rs, zg_s, zg_r, zga_s, zga_r,
):
    nx, ny, nz, width = dims
    rows = 2 * nx * ny
    chips = nx * ny
    tokens = 4 * rows
    vb = w_hbm.shape[0]
    dh = width // 2
    xw = dh // 2
    qw = xw // 2
    cut = -(-qw // 256) * 128
    heads, hd = attn.shape[1:]
    step = width // nz
    starts = [zz * step // 128 * 128 for zz in range(nz)]
    shares = (loss_scale * mtp_share, loss_scale)
    far_chip = (ny // 2) * nx + nx // 2
    far_row = 2 * far_chip

    v = lax.axis_index("vocab")
    r = lax.axis_index("rows")
    c = lax.rem(r, 2)
    chip = r // 2
    x = lax.rem(chip, nx)
    y = chip // nx
    sibling = (v, r + 1 - 2 * c)
    window = pl.multiple_of(v * step // 128 * 128, 128)

    def at(yy, xx, core):
        return (v, (yy * nx + xx) * 2 + core)

    def arrived(ref, sem):
        remote(ref, ref, sib_s.at[0], sem, sibling).wait_recv()

    sends = []

    def push(copy):
        copy.start()
        sends.append(copy)

    def drain():
        for copy in sends:
            copy.wait_send()
        sends.clear()

    def exchange(count, copy, slots, send, recv):
        def start(i, carry):
            copy(i).start()
            return carry

        def finish():
            whole = slots.at[0 : count - 1]
            done = remote(whole, whole, send, recv, sibling)
            done.wait_recv()
            done.wait_send()

        return (lambda: lax.fori_loop(1, count, start, 0)), finish

    def to_vocab(send, recv, source, slots):
        def copy(i):
            zz = lax.rem(v + nz // 2 + (1 - 2 * lax.rem(i + 1, 2)) * (i // 2), nz)
            return remote(source(zz), slots.at[v], send, recv, (zz, r))

        return exchange(nz, copy, slots, send, recv)

    def to_rows(send, recv, source, slots):
        def copy(i):
            rr = lax.rem(r + 1 + lax.rem(i + far_row - 2, rows - 1), rows)
            return remote(source(rr), slots.at[r], send, recv, (v, rr))

        return exchange(rows, copy, slots, send, recv)

    def to_chips(send, recv, slots):
        def copy(i):
            cc = lax.rem(chip + 1 + lax.rem(i + far_chip - 2, chips - 1), chips)
            return remote(slots.at[chip], slots.at[chip], send, recv, (v, 2 * cc + c))

        return exchange(chips, copy, slots, send, recv)

    own_cols = pl.ds(pl.multiple_of(c * dh, 128), dh)
    sib_cols = pl.ds(pl.multiple_of((1 - c) * dh, 128), dh)
    w_copy = pltpu.make_async_copy(w_hbm.at[:, own_cols], w2.at[c], cp_sem.at[0])
    loads = [
        pltpu.make_async_copy(src, dst, cp_sem.at[1 + i])
        for i, (src, dst) in enumerate(
            (
                (state_h, state), (gain_h, gain), (trunk_h, trunk), (tids_h, tids), (mids_h, mids),
                (attn_h, attn), (out_proj_h, out_proj_t),
            )
        )
    ]
    for load in loads:
        load.start()
    w_copy.start()

    bar = pltpu.get_barrier_semaphore()

    def greet_rows(i, carry):
        pl.semaphore_signal(
            bar, inc=1, device_id=(v, lax.rem(r + i, rows)), device_id_type=pl.DeviceIdType.MESH
        )
        return carry

    def greet_vocab(i, carry):
        zz = lax.rem(v + nz // 2 + (1 - 2 * lax.rem(i + 1, 2)) * (i // 2), nz)
        pl.semaphore_signal(bar, inc=1, device_id=(zz, r), device_id_type=pl.DeviceIdType.MESH)
        return carry

    lax.fori_loop(1, nz, greet_vocab, 0)
    lax.fori_loop(1, rows, greet_rows, 0)

    for load in loads[:3]:
        load.wait()
    sv = state[...].astype(f32)
    inverse = lax.rsqrt(jnp.mean(sv * sv, axis=-1, keepdims=True) + norm_eps)
    normed = sv * inverse
    for k in range(width // 128):
        gain_row[0:1, k * 128 : (k + 1) * 128] = gain[k : k + 1, :].astype(f32)
    own8[0:4, :] = trunk[...].astype(f32)
    own8[4:8, :] = (normed * gain_row[...]).astype(bf16).astype(f32)
    st4[...] = normed
    inv4[...] = jnp.broadcast_to(inverse, (4, 128))

    pl.semaphore_wait(bar, rows - 1 + nz - 1)

    tok_copy = remote(own8.at[:, sib_cols], sib8, sib_s.at[0], sib_r.at[0], sibling)
    push(tok_copy)
    push(remote(w_hbm.at[:, sib_cols], w2.at[c], sib_s.at[1], sib_r.at[1], sibling))
    mine = own8[:, own_cols]
    tok_copy.wait_recv()
    other = sib8[...]
    first = c == 0
    low = jnp.where(first, mine, other)
    high = jnp.where(first, other, mine)

    def place(g, rng):
        block = jnp.concatenate([low[rng], high[rng]], axis=0)
        hx[g, y, x] = fold(block[:, :xw])
        hy[g, y, x] = fold(block[:, xw:])

    place(0, slice(4, 8))

    def gather_first(g):
        for j in range(1, nx):
            blk = hx.at[g, y, x]
            push(remote(blk, blk, ag_s1.at[g, 0, j - 1], ag_r.at[g, 0, y, x], at(y, lax.rem(x + j, nx), c)))
        for j in range(1, ny):
            blk = hy.at[g, y, x]
            push(remote(blk, blk, ag_s1.at[g, 1, j - 1], ag_r.at[g, 1, y, x], at(lax.rem(y + j, ny), x, c)))

    order = {4: (0, 1, 3, 2), 2: (0, 1), 1: (0,)}

    def gather_second(g):
        for i in range(max(nx, ny)):
            if i < nx:
                xx = lax.rem(x + order[nx][i], nx)
                blk = hx.at[g, y, xx]
                if i > 0:
                    arrived(blk, ag_r.at[g, 0, y, xx])
                for j in range(1, ny):
                    push(remote(blk, blk, ag_s2.at[g, 0, i, j - 1], ag_r2.at[g, 0], at(lax.rem(y + j, ny), x, c)))
            if i < ny:
                yy = lax.rem(y + order[ny][i], ny)
                blk = hy.at[g, yy, x]
                if i > 0:
                    arrived(blk, ag_r.at[g, 1, yy, x])
                for j in range(1, nx):
                    push(remote(blk, blk, ag_s2.at[g, 1, i, j - 1], ag_r2.at[g, 1], at(y, lax.rem(x + j, nx), c)))

    def gather_wait(g):
        arrived(hx.at[g, 0 : ny - 1], ag_r2.at[g, 0])
        arrived(hy.at[g, 0 : nx - 1] if nx == ny else hy.at[g, :, 0 : nx - 1], ag_r2.at[g, 1])

    def logits_start(g):
        for buf, off in ((hx, 0), (hy, xw)):
            block = buf[g].astype(f32).reshape(chips, 2, 8, qw)
            for k in range(2):
                hid[g * tokens : (g + 1) * tokens, off + k * qw : off + (k + 1) * qw] = (
                    block[:, k].reshape(tokens, qw).astype(bf16)
                )
        lt_own[g] = nt(w2[...].reshape(2 * vb, dh), hid[g * tokens : (g + 1) * tokens, :])
        push(remote(lt_own.at[g], lt_sib.at[g], sib_s.at[2 + g], sib_r.at[2 + g], sibling))

    vocab_id = iota((2 * vb, tokens), 0) + (v * rows + 2 * chip) * vb
    i4 = iota((4, tokens), 0)

    def onehot(g):
        return (vocab_id == (mids, tids)[g][...]).astype(f32)

    pst = [to_chips(pst_s.at[g], pst_r.at[g], st_plane.at[g]) for g in range(2)]
    zst = [
        to_vocab(zst_s.at[g], zst_r.at[g], lambda zz, g=g: st_z.at[g, v], st_z.at[g])
        for g in range(2)
    ]

    def stats_start(g):
        arrived(lt_sib.at[g], sib_r.at[2 + g])
        logits = lt_own[g] + lt_sib[g]
        top = jnp.max(logits, axis=0, keepdims=True)
        e = jnp.exp(logits - top)
        lt_sib[g] = e
        st_plane[g, chip] = jnp.where(
            i4 == 0,
            top,
            jnp.where(
                i4 == 1,
                jnp.sum(e, axis=0, keepdims=True),
                jnp.where(
                    i4 == 2,
                    jnp.sum(e * logits, axis=0, keepdims=True),
                    jnp.sum(onehot(g) * logits, axis=0, keepdims=True),
                ),
            ),
        )
        pst[g][0]()
        return top

    def merge(slots, count):
        top = slots[0][0:1]
        for s in range(1, count):
            top = jnp.maximum(top, slots[s][0:1])
        acc = jnp.zeros((4, tokens), f32)
        for s in range(count):
            tile = slots[s]
            acc = acc + jnp.where(i4 == 3, tile, tile * jnp.exp(tile[0:1] - top))
        return jnp.where(i4 == 0, top, acc)

    def stats_second(g):
        pst[g][1]()
        st_z[g, v] = merge(st_plane.at[g], chips)
        zst[g][0]()

    def sum_first(g, off):
        if off == 0:
            for j in range(1, nx):
                xx = lax.rem(x + j, nx)
                push(remote(px.at[g, :, xx], rx.at[g, j - 1], rs_s1.at[g, 0, j - 1], rs_r1.at[g, 0, j - 1], at(y, xx, c)))
        else:
            for j in range(1, ny):
                yy = lax.rem(y + j, ny)
                push(remote(py.at[g, yy], ry.at[g, j - 1], rs_s1.at[g, 1, j - 1], rs_r1.at[g, 1, j - 1], at(yy, x, c)))

    def grads_start(g, top_chip):
        zst[g][1]()
        whole = merge(st_z.at[g], nz)
        top, total = whole[0:1], whole[1:2]
        grads = lt_sib[g] * (shares[g] * jnp.exp(top_chip - top) / total) - shares[g] * onehot(g)
        gt[:, g * tokens : (g + 1) * tokens] = grads.astype(bf16)
        grads_t = jnp.transpose(grads).astype(bf16)
        for buf, off in ((px, 0), (py, xw)):
            halves = [
                nn(grads_t, w2[:, :, off + k * qw : off + (k + 1) * qw].reshape(2 * vb, qw)).reshape(chips, 8, qw)
                for k in range(2)
            ]
            buf[g] = jnp.concatenate(halves, axis=1).astype(bf16).reshape(ny, nx, 16, qw)
            sum_first(g, off)
        dot = shares[g] * (whole[2:3] / total - whole[3:4])
        return (
            jnp.sum(jnp.where(iota((4, tokens), 1) == 4 * r + i4, dot, 0.0), axis=1, keepdims=True) / width
        )

    def sum_second(g):
        for axis, count, other_count, own_buf, got, out, out2 in (
            (0, ny, nx, px, rx, axs, rx2), (1, nx, ny, py, ry, ays, ry2),
        ):
            for j in range(1, other_count):
                arrived(got.at[g, j - 1], rs_r1.at[g, axis, j - 1])
            for jj in range(count):
                j = (jj + 1) % count
                k0 = lax.rem((y, x)[axis] + j, count)
                own_block = own_buf[g, k0, x] if axis == 0 else own_buf[g, y, k0]
                acc = own_block.astype(f32)
                for k in range(other_count - 1):
                    acc = acc + got[g, k, k0].astype(f32)
                for d in range(2):
                    four = jnp.concatenate([acc[4 * d : 4 * d + 4], acc[8 + 4 * d : 12 + 4 * d]], axis=0)
                    rest = four[:, cut:]
                    if 2 * cut > qw:
                        rest = jnp.concatenate([rest, jnp.zeros((8, 2 * cut - qw), f32)], axis=1)
                    out[g, j, d] = jnp.concatenate([four[:, :cut], rest], axis=0).astype(bf16)
                if j > 0:
                    for d in range(2):
                        device = at(k0, x, d) if axis == 0 else at(y, k0, d)
                        push(remote(out.at[g, j, d], out2.at[g, j, c], rs_s2.at[g, axis, j, d], rs_r2.at[g, axis, j, c], device))
                else:
                    push(remote(out.at[g, 0, 1 - c], out2.at[g, 0, c], rs_s2.at[g, axis, 0, 0], rs_r2.at[g, axis, 0, c], sibling))
                    out2[g, 0, c] = out[g, 0, c]

    zrs = [
        to_vocab(zrs_s.at[g], zrs_r.at[g], lambda zz, g=g: zs.at[g, zz], zr.at[g])
        for g in range(2)
    ]
    zag = [
        to_vocab(zag_s.at[g], zag_r.at[g], lambda zz, g=g: zo.at[g, v], zo.at[g])
        for g in range(2)
    ]

    def vocab_start(g):
        for buf, axis, count, off in ((rx2, 0, ny, 0), (ry2, 1, nx, xw)):
            for j in range(1, count):
                for s in range(2):
                    arrived(buf.at[g, j, s], rs_r2.at[g, axis, j, s])
            arrived(buf.at[g, 0, 1 - c], rs_r2.at[g, axis, 0, 1 - c])
            for s in range(2):
                acc = buf[g, 0, s].astype(f32)
                for j in range(1, count):
                    acc = acc + buf[g, j, s].astype(f32)
                wide = jnp.concatenate([acc[0:8], acc[8:16, : qw - cut]], axis=1)
                sum4[:, s * dh + off : s * dh + off + qw] = wide[0:4]
                sum4[:, s * dh + off + qw : s * dh + off + 2 * qw] = wide[4:8]
        for zz in range(nz):
            zs[g, zz] = fold4(sum4[:, starts[zz] : starts[zz] + LANES])
        zrs[g][0]()
        zr[g, v] = zs[g, v]

    def vocab_sum(g):
        zrs[g][1]()
        acc = zr[g, 0].astype(f32)
        for zz in range(1, nz):
            acc = acc + zr[g, zz].astype(f32)
        return unfold4(acc)

    def write(g, out):
        zag[g][1]()
        for zz in range(nz):
            out[:, starts[zz] : starts[zz] + LANES] = unfold4(zo[g, zz].astype(f32)).astype(bf16)

    a2a = to_rows(a2a_ss.at[0], a2a_rs.at[0], lambda rr: a2a_s.at[rr], a2a_r)
    pag = to_rows(pag_s.at[0], pag_r.at[0], lambda rr: po, pr)
    zga = to_vocab(zga_s.at[0], zga_r.at[0], lambda zz: gs.at[zz], gr)
    zgs = to_vocab(zg_s.at[0], zg_r.at[0], lambda zz: zg.at[v], zg)

    gather_first(0)
    place(1, slice(0, 4))
    gather_second(0)
    gather_first(1)

    for load in loads[3:]:
        load.wait()
    ir = iota((rows * 16, 4 * heads), 0)
    im = iota((rows * 16, 4 * heads), 1)
    kk = ir & 15
    pick = (kk < 8) & (im == (kk >> 1) * heads + 2 * (ir >> 4) + (kk & 1))
    a2a_s[...] = (
        nn(pick.astype(f32).astype(bf16), attn[...].reshape(4 * heads, hd)).astype(bf16).reshape(rows, 16, hd)
    )
    a2a_r[r] = a2a_s[r]

    it = iota((tokens, rows * 16), 0)
    il = iota((tokens, rows * 16), 1)
    base = 16 * (it >> 2) + (it & 3)
    sel[0:tokens, :] = (il == base + 4).astype(f32).astype(bf16)
    sel[tokens : 2 * tokens, :] = (il == base + 12).astype(f32).astype(bf16)
    ig = iota((16, rows * 16), 0)
    kg = iota((16, rows * 16), 1) & 15
    sel[2 * tokens : 2 * tokens + 16, :] = (
        ((ig == 0) & (kg < 2)) | ((ig == 1) & (kg >= 8) & (kg < 10))
    ).astype(f32).astype(bf16)
    base = 16 * (it >> 2) + 2 * (it & 3)
    for h in range(2):
        gather_v[h * tokens : (h + 1) * tokens, :] = (il == base + h).astype(f32).astype(bf16)
    opw[...] = jnp.zeros(opw.shape, bf16)
    shift = pl.multiple_of(v * step % 128, 16)
    opw[pl.ds(shift, step), :] = out_proj_t[...]

    w_copy.wait()
    arrived(w2.at[1 - c], sib_r.at[1])
    gather_second(1)
    gather_wait(0)
    logits_start(0)
    top_m = stats_start(0)
    gather_wait(1)
    logits_start(1)
    top_t = stats_start(1)
    stats_second(0)
    a2a[0]()
    drain()
    stats_second(1)
    dot_mean = grads_start(0, top_m)
    grads_start(1, top_t)
    sum_second(0)
    vocab_start(0)

    for n in range(0, dh, qw):
        head_out[:, n : n + qw] = nn(gt[pl.ds(pl.multiple_of((1 - c) * vb, 16), vb), :], hid[:, n : n + qw]).astype(bf16)
    push(remote(head_out, head_in, sib_s.at[4], sib_r.at[4], sibling))
    for n in range(0, dh, qw):
        head_own[:, n : n + qw] = nn(gt[pl.ds(pl.multiple_of(c * vb, 16), vb), :], hid[:, n : n + qw]).astype(bf16)
    head_stores = [
        pltpu.make_async_copy(head_own, o_head.at[:, own_cols], cp_sem.at[8]),
        pltpu.make_async_copy(head_in, o_head.at[:, sib_cols], cp_sem.at[9]),
    ]
    head_stores[0].start()

    sum_second(1)
    grad = vocab_sum(0)

    cols = pl.ds(window, LANES)
    normed4 = st4[:, cols]
    residual = inv4[:, 0:1] * (grad * gain_row[:, cols] - normed4 * dot_mean)
    gain_term = jnp.sum(grad * normed4, axis=0, keepdims=True)
    gain_high = gain_term.astype(bf16).astype(f32)
    po[...] = fold(
        jnp.concatenate([gain_high, gain_term - gain_high, jnp.zeros((2, LANES), f32), residual], axis=0)
    )
    pag[0]()
    pr[r] = po[...]
    zo[0, v] = fold4(residual)
    vocab_start(1)
    zag[0][0]()

    a2a[1]()
    received = a2a_r[...].reshape(rows * 16, hd)
    for h in range(2):
        vals[:, h * hd : (h + 1) * hd] = nn(gather_v[h * tokens : (h + 1) * tokens, :], received).astype(bf16)

    arrived(head_in, sib_r.at[4])
    head_stores[1].start()

    pag[1]()
    picked = nn(sel[...], pr[...].reshape(rows * 16, HALF))
    columns = jnp.concatenate([picked[0:tokens], picked[tokens : 2 * tokens]], axis=1)
    attn_term = nn(columns.astype(bf16), opw[...])
    for zz in range(nz):
        gs[zz] = fold(attn_term[8 * zz : 8 * zz + 8])
    zga[0]()
    gr[v] = gs[v]
    zg[v] = jnp.concatenate(
        [picked[2 * tokens + k // 2 : 2 * tokens + k // 2 + 1, k % 2 * 128 : k % 2 * 128 + 128] for k in range(LANES // 128)],
        axis=0,
    )
    zgs[0]()
    zo[1, v] = fold4(vocab_sum(1))
    zag[1][0]()

    proj_s[...] = nn(jnp.transpose(columns).astype(bf16), vals[...]).astype(bf16)
    o_proj_t[...] = proj_s[pl.ds(shift, step), :]

    drain()
    write(0, o_res)
    zgs[1]()
    for zz in range(nz):
        o_gain[starts[zz] // 128 : (starts[zz] + LANES) // 128, :] = zg[zz]
    zga[1]()
    acc = gr[0].astype(f32)
    for zz in range(1, nz):
        acc = acc + gr[zz].astype(f32)
    for h in range(2):
        attn_s[pl.ds(h, 8, stride=2), :] = acc[8 * h : 8 * h + 8]
    o_attn[...] = attn_s[...].astype(bf16)
    write(1, o_trunk)
    for store in head_stores:
        store.wait()


def finish(*refs):
    sources, targets, held, sem_in, sem_out = refs[0:6], refs[6:12], refs[12:18], refs[18], refs[19]
    pieces = []
    for src, dst, buf in zip(sources, targets, held):
        rows = src.shape[0]
        cut = rows // 9 * 3 if rows % 144 == 0 else rows
        for at in range(0, rows, cut):
            pieces.append((src.at[at : at + cut], dst.at[at : at + cut], buf.at[at : at + cut]))
    pieces.sort(key=lambda piece: -piece[0].shape[0] * piece[0].shape[1])
    loads = [pltpu.make_async_copy(src, buf, sem_in.at[i]) for i, (src, _, buf) in enumerate(pieces)]
    stores = [pltpu.make_async_copy(buf, dst, sem_out.at[i]) for i, (_, dst, buf) in enumerate(pieces)]
    for load in loads:
        load.start()
    for load, store in zip(loads, stores):
        load.wait()
        store.start()
    for store in stores:
        store.wait()


def local(dims, trunk_hidden, mtp_state, mtp_gain, head_weight, target_ids, mtp_target_ids, attn_values, out_proj):
    nx, ny, nz, width = dims
    rows = 2 * nx * ny
    tokens = 4 * rows
    vb = head_weight.shape[0]
    dh = width // 2
    qw = dh // 4
    cut = -(-qw // 256) * 128
    step = out_proj.shape[1]
    heads, hd = attn_values.shape[1:]
    vmem = pltpu.VMEM
    dma = pltpu.SemaphoreType.DMA
    scratch = [
        vmem((4, width), bf16),
        vmem((4, width), bf16),
        vmem((width // 128, 128), bf16),
        vmem((1, tokens), jnp.int32),
        vmem((1, tokens), jnp.int32),
        vmem((4, heads, hd), bf16),
        vmem((step, 2 * hd), bf16),
        vmem((1, width), f32),
        vmem((8, width), f32),
        vmem((4, width), f32),
        vmem((4, 128), f32),
        vmem((8, dh), f32),
        vmem((2, vb, dh), bf16),
        vmem((2, ny, nx, 16, qw), bf16),
        vmem((2, ny, nx, 16, qw), bf16),
        vmem((2 * tokens, dh), bf16),
        vmem((2, 2 * vb, tokens), f32),
        vmem((2, 2 * vb, tokens), f32),
        vmem((2, nx * ny, 4, tokens), f32),
        vmem((2, nz, 4, tokens), f32),
        vmem((2 * vb, 2 * tokens), bf16),
        vmem((2, ny, nx, 16, qw), bf16),
        vmem((2, ny, nx, 16, qw), bf16),
        vmem((vb, dh), bf16),
        vmem((vb, dh), bf16),
        vmem((vb, dh), bf16),
        vmem((2, max(nx - 1, 1), ny, 16, qw), bf16),
        vmem((2, max(ny - 1, 1), nx, 16, qw), bf16),
        vmem((2, ny, 2, 16, cut), bf16),
        vmem((2, nx, 2, 16, cut), bf16),
        vmem((2, ny, 2, 16, cut), bf16),
        vmem((2, nx, 2, 16, cut), bf16),
        vmem((4, width), f32),
        vmem((2, nz, 16, LANES // 4), bf16),
        vmem((2, nz, 16, LANES // 4), bf16),
        vmem((2, nz, 16, LANES // 4), bf16),
        vmem((16, HALF), bf16),
        vmem((rows, 16, HALF), bf16),
        vmem((2 * tokens + 16, rows * 16), bf16),
        vmem((2 * tokens, rows * 16), bf16),
        vmem((rows, 16, hd), bf16),
        vmem((rows, 16, hd), bf16),
        vmem((tokens, 2 * hd), bf16),
        vmem((LANES, 2 * hd), bf16),
        vmem((nz, LANES // 128, 128), f32),
        vmem((nz, 16, hd), bf16),
        vmem((nz, 16, hd), bf16),
        vmem((LANES, 2 * hd), bf16),
        vmem((16, hd), f32),
        dma((10,)),
        dma((5,)),
        dma((5,)),
        dma((2, 2, 3)),
        dma((2, 2, 4, 3)),
        dma((2, 2, ny, nx)),
        dma((2, 2)),
        dma((2,)),
        dma((2,)),
        dma((2,)),
        dma((2,)),
        dma((2, 2, 3)),
        dma((2, 2, 3)),
        dma((2, 2, 4, 2)),
        dma((2, 2, 4, 2)),
        dma((2,)),
        dma((2,)),
        dma((2,)),
        dma((2,)),
        dma((1,)),
        dma((1,)),
        dma((1,)),
        dma((1,)),
        dma((1,)),
        dma((1,)),
        dma((1,)),
        dma((1,)),
    ]
    in_vmem = pl.BlockSpec(memory_space=pltpu.VMEM)
    in_hbm = pl.BlockSpec(memory_space=pl.ANY)
    shape = jax.ShapeDtypeStruct
    shapes = [
        shape((4, width), bf16),
        shape((4, width), bf16),
        shape((width // 128, 128), f32),
        shape((vb, width), bf16),
        shape((16, hd), bf16),
        shape((step, 2 * hd), bf16),
    ]
    results = pl.pallas_call(
        functools.partial(kernel, dims),
        out_shape=shapes,
        in_specs=[pl.BlockSpec(memory_space=pltpu.HBM)] * 8,
        out_specs=[in_vmem] * 3 + [in_hbm] + [in_vmem] * 2,
        scratch_shapes=scratch,
        compiler_params=pltpu.CompilerParams(
            collective_id=0, has_side_effects=True, vmem_limit_bytes=60 * 2**20
        ),
        name="head_backward",
    )(
        trunk_hidden,
        mtp_state,
        mtp_gain.reshape(width // 128, 128),
        head_weight,
        target_ids.reshape(1, -1),
        mtp_target_ids.reshape(1, -1),
        attn_values,
        out_proj.T,
    )
    trunk_out, res_out, gain_out, head_out, attn_out, proj_out = pl.pallas_call(
        finish,
        out_shape=shapes,
        in_specs=[in_hbm] * len(shapes),
        out_specs=[in_hbm] * len(shapes),
        scratch_shapes=[vmem(s.shape, s.dtype) for s in shapes] + [dma((8,)), dma((8,))],
        compiler_params=pltpu.CompilerParams(vmem_limit_bytes=60 * 2**20),
        name="results",
    )(*results)
    grad_attn = attn_out.reshape(8, 2, hd)
    return (trunk_out, res_out, gain_out.reshape(width), head_out, grad_attn, proj_out.T)


def solution(mesh):
    nz, rows = mesh.shape["vocab"], mesh.shape["rows"]
    nx = {32: 4, 8: 2, 2: 1}[rows]

    def run(*args):
        dims = (nx, rows // 2 // nx, nz, args[0].shape[1])
        return local(dims, *args)

    return jax.shard_map(
        run,
        mesh=mesh,
        in_specs=(
            P("rows", None),
            P("rows", None),
            P(),
            P(("vocab", "rows"), None),
            P(),
            P(),
            P("rows", None, None),
            P("rows", "vocab"),
        ),
        out_specs=(
            P("rows", None),
            P("rows", None),
            P(),
            P(("vocab", "rows"), None),
            P("vocab", "rows", None),
            P("rows", "vocab"),
        ),
        check_vma=False,
    )
```

```python
import functools

import jax
import jax.numpy as jnp
from jax import lax
from jax.experimental import pallas as pl
from jax.experimental.pallas import tpu as pltpu
from jax.sharding import PartitionSpec as P

loss_scale = 8.0
mtp_share = 0.3
norm_eps = 1e-06
f32 = jnp.float32
bf16 = jnp.bfloat16
LANES = 512
HALF = LANES // 2


def nn(a, b):
    return lax.dot_general(a, b, (((1,), (0,)), ((), ())), preferred_element_type=f32)


def nt(a, b):
    return lax.dot_general(a, b, (((1,), (1,)), ((), ())), preferred_element_type=f32)


def iota(shape, axis):
    return lax.broadcasted_iota(jnp.int32, shape, axis)


def fold(block):
    w = block.shape[1] // 2
    return jnp.concatenate([block[:, :w], block[:, w:]], axis=0).astype(bf16)


def unfold(block):
    return jnp.concatenate([block[:8], block[8:]], axis=1)


def fold4(block):
    w = block.shape[1] // 4
    return jnp.concatenate([block[:, k * w : (k + 1) * w] for k in range(4)], axis=0).astype(bf16)


def unfold4(block):
    return jnp.concatenate([block[4 * k : 4 * k + 4] for k in range(4)], axis=1)


def remote(src, dst, send, recv, device):
    return pltpu.make_async_remote_copy(
        src_ref=src,
        dst_ref=dst,
        send_sem=send,
        recv_sem=recv,
        device_id=device,
        device_id_type=pl.DeviceIdType.MESH,
    )


def kernel(
    dims,
    trunk_h, state_h, gain_h, w_hbm, tids_h, mids_h, attn_h, out_proj_h,
    o_trunk, o_res, o_gain, o_head, o_attn, o_proj_t,
    trunk, state, gain, tids, mids, attn, out_proj_t,
    gain_row, own8, st4, inv4, sib8, w2, hx, hy, hid, lt_own, lt_sib, st_plane, st_z,
    gt, px, py, head_out, head_own, head_in, rx, ry, axs, ays, rx2, ry2, sum4, zs, zr, zo, po, pr, sel, gather_v,
    a2a_s, a2a_r, vals, opw, zg, gs, gr, proj_s, attn_s,
    cp_sem, sib_s, sib_r, ag_s1, ag_s2, ag_r, ag_r2, pst_s, pst_r, zst_s, zst_r,
    rs_s1, rs_r1, rs_s2, rs_r2, zrs_s, zrs_r, zag_s, zag_r, pag_s, pag_r,
    a2a_ss, a2a_rs, zg_s, zg_r, zga_s, zga_r,
):
    nx, ny, nz, width = dims
    rows = 2 * nx * ny
    chips = nx * ny
    tokens = 4 * rows
    vb = w_hbm.shape[0]
    dh = width // 2
    xw = dh // 2
    qw = xw // 2
    cut = -(-qw // 256) * 128
    heads, hd = attn.shape[1:]
    step = width // nz
    starts = [zz * step // 128 * 128 for zz in range(nz)]
    shares = (loss_scale * mtp_share, loss_scale)
    far_chip = (ny // 2) * nx + nx // 2
    far_row = 2 * far_chip

    v = lax.axis_index("vocab")
    r = lax.axis_index("rows")
    c = lax.rem(r, 2)
    chip = r // 2
    x = lax.rem(chip, nx)
    y = chip // nx
    sibling = (v, r + 1 - 2 * c)
    window = pl.multiple_of(v * step // 128 * 128, 128)

    def at(yy, xx, core):
        return (v, (yy * nx + xx) * 2 + core)

    def arrived(ref, sem):
        remote(ref, ref, sib_s.at[0], sem, sibling).wait_recv()

    sends = []

    def push(copy):
        copy.start()
        sends.append(copy)

    def drain():
        for copy in sends:
            copy.wait_send()
        sends.clear()

    def exchange(count, copy, slots, send, recv):
        def start(i, carry):
            copy(i).start()
            return carry

        def finish():
            whole = slots.at[0 : count - 1]
            done = remote(whole, whole, send, recv, sibling)
            done.wait_recv()
            done.wait_send()

        return (lambda: lax.fori_loop(1, count, start, 0)), finish

    def to_vocab(send, recv, source, slots):
        def copy(i):
            zz = lax.rem(v + nz // 2 + (1 - 2 * lax.rem(i + 1, 2)) * (i // 2), nz)
            return remote(source(zz), slots.at[v], send, recv, (zz, r))

        return exchange(nz, copy, slots, send, recv)

    def to_rows(send, recv, source, slots):
        def copy(i):
            rr = lax.rem(r + 1 + lax.rem(i + far_row - 2, rows - 1), rows)
            return remote(source(rr), slots.at[r], send, recv, (v, rr))

        return exchange(rows, copy, slots, send, recv)

    def to_chips(send, recv, slots):
        def copy(i):
            cc = lax.rem(chip + 1 + lax.rem(i + far_chip - 2, chips - 1), chips)
            return remote(slots.at[chip], slots.at[chip], send, recv, (v, 2 * cc + c))

        return exchange(chips, copy, slots, send, recv)

    own_cols = pl.ds(pl.multiple_of(c * dh, 128), dh)
    sib_cols = pl.ds(pl.multiple_of((1 - c) * dh, 128), dh)
    w_copy = pltpu.make_async_copy(w_hbm.at[:, own_cols], w2.at[c], cp_sem.at[0])
    loads = [
        pltpu.make_async_copy(src, dst, cp_sem.at[1 + i])
        for i, (src, dst) in enumerate(
            (
                (state_h, state), (gain_h, gain), (trunk_h, trunk), (tids_h, tids), (mids_h, mids),
                (attn_h, attn), (out_proj_h, out_proj_t),
            )
        )
    ]
    for load in loads:
        load.start()
    w_copy.start()

    bar = pltpu.get_barrier_semaphore()

    def greet_rows(i, carry):
        pl.semaphore_signal(
            bar, inc=1, device_id=(v, lax.rem(r + i, rows)), device_id_type=pl.DeviceIdType.MESH
        )
        return carry

    def greet_vocab(i, carry):
        zz = lax.rem(v + nz // 2 + (1 - 2 * lax.rem(i + 1, 2)) * (i // 2), nz)
        pl.semaphore_signal(bar, inc=1, device_id=(zz, r), device_id_type=pl.DeviceIdType.MESH)
        return carry

    lax.fori_loop(1, nz, greet_vocab, 0)
    lax.fori_loop(1, rows, greet_rows, 0)

    for load in loads[:3]:
        load.wait()
    sv = state[...].astype(f32)
    inverse = lax.rsqrt(jnp.mean(sv * sv, axis=-1, keepdims=True) + norm_eps)
    normed = sv * inverse
    for k in range(width // 128):
        gain_row[0:1, k * 128 : (k + 1) * 128] = gain[k : k + 1, :].astype(f32)
    own8[0:4, :] = trunk[...].astype(f32)
    own8[4:8, :] = (normed * gain_row[...]).astype(bf16).astype(f32)
    st4[...] = normed
    inv4[...] = jnp.broadcast_to(inverse, (4, 128))

    pl.semaphore_wait(bar, rows - 1 + nz - 1)

    tok_copy = remote(own8.at[:, sib_cols], sib8, sib_s.at[0], sib_r.at[0], sibling)
    push(tok_copy)
    push(remote(w_hbm.at[:, sib_cols], w2.at[c], sib_s.at[1], sib_r.at[1], sibling))
    mine = own8[:, own_cols]
    tok_copy.wait_recv()
    other = sib8[...]
    first = c == 0
    low = jnp.where(first, mine, other)
    high = jnp.where(first, other, mine)

    def place(g, rng):
        block = jnp.concatenate([low[rng], high[rng]], axis=0)
        hx[g, y, x] = fold(block[:, :xw])
        hy[g, y, x] = fold(block[:, xw:])

    place(0, slice(4, 8))

    def gather_first(g):
        for j in range(1, nx):
            blk = hx.at[g, y, x]
            push(remote(blk, blk, ag_s1.at[g, 0, j - 1], ag_r.at[g, 0, y, x], at(y, lax.rem(x + j, nx), c)))
        for j in range(1, ny):
            blk = hy.at[g, y, x]
            push(remote(blk, blk, ag_s1.at[g, 1, j - 1], ag_r.at[g, 1, y, x], at(lax.rem(y + j, ny), x, c)))

    order = {4: (0, 1, 3, 2), 2: (0, 1), 1: (0,)}

    def gather_second(g):
        for i in range(max(nx, ny)):
            if i < nx:
                xx = lax.rem(x + order[nx][i], nx)
                blk = hx.at[g, y, xx]
                if i > 0:
                    arrived(blk, ag_r.at[g, 0, y, xx])
                for j in range(1, ny):
                    push(remote(blk, blk, ag_s2.at[g, 0, i, j - 1], ag_r2.at[g, 0], at(lax.rem(y + j, ny), x, c)))
            if i < ny:
                yy = lax.rem(y + order[ny][i], ny)
                blk = hy.at[g, yy, x]
                if i > 0:
                    arrived(blk, ag_r.at[g, 1, yy, x])
                for j in range(1, nx):
                    push(remote(blk, blk, ag_s2.at[g, 1, i, j - 1], ag_r2.at[g, 1], at(y, lax.rem(x + j, nx), c)))

    def gather_wait(g):
        arrived(hx.at[g, 0 : ny - 1], ag_r2.at[g, 0])
        arrived(hy.at[g, 0 : nx - 1] if nx == ny else hy.at[g, :, 0 : nx - 1], ag_r2.at[g, 1])

    def logits_start(g):
        for buf, off in ((hx, 0), (hy, xw)):
            block = buf[g].astype(f32).reshape(chips, 2, 8, qw)
            for k in range(2):
                hid[g * tokens : (g + 1) * tokens, off + k * qw : off + (k + 1) * qw] = (
                    block[:, k].reshape(tokens, qw).astype(bf16)
                )
        lt_own[g] = nt(w2[...].reshape(2 * vb, dh), hid[g * tokens : (g + 1) * tokens, :])
        push(remote(lt_own.at[g], lt_sib.at[g], sib_s.at[2 + g], sib_r.at[2 + g], sibling))

    vocab_id = iota((2 * vb, tokens), 0) + (v * rows + 2 * chip) * vb
    i4 = iota((4, tokens), 0)

    def onehot(g):
        return (vocab_id == (mids, tids)[g][...]).astype(f32)

    pst = [to_chips(pst_s.at[g], pst_r.at[g], st_plane.at[g]) for g in range(2)]
    zst = [
        to_vocab(zst_s.at[g], zst_r.at[g], lambda zz, g=g: st_z.at[g, v], st_z.at[g])
        for g in range(2)
    ]

    def stats_start(g):
        arrived(lt_sib.at[g], sib_r.at[2 + g])
        logits = lt_own[g] + lt_sib[g]
        top = jnp.max(logits, axis=0, keepdims=True)
        e = jnp.exp(logits - top)
        lt_sib[g] = e
        st_plane[g, chip] = jnp.where(
            i4 == 0,
            top,
            jnp.where(
                i4 == 1,
                jnp.sum(e, axis=0, keepdims=True),
                jnp.where(
                    i4 == 2,
                    jnp.sum(e * logits, axis=0, keepdims=True),
                    jnp.sum(onehot(g) * logits, axis=0, keepdims=True),
                ),
            ),
        )
        pst[g][0]()
        return top

    def merge(slots, count):
        top = slots[0][0:1]
        for s in range(1, count):
            top = jnp.maximum(top, slots[s][0:1])
        acc = jnp.zeros((4, tokens), f32)
        for s in range(count):
            tile = slots[s]
            acc = acc + jnp.where(i4 == 3, tile, tile * jnp.exp(tile[0:1] - top))
        return jnp.where(i4 == 0, top, acc)

    def stats_second(g):
        pst[g][1]()
        st_z[g, v] = merge(st_plane.at[g], chips)
        zst[g][0]()

    def sum_first(g, off):
        if off == 0:
            for j in range(1, nx):
                xx = lax.rem(x + j, nx)
                push(remote(px.at[g, :, xx], rx.at[g, j - 1], rs_s1.at[g, 0, j - 1], rs_r1.at[g, 0, j - 1], at(y, xx, c)))
        else:
            for j in range(1, ny):
                yy = lax.rem(y + j, ny)
                push(remote(py.at[g, yy], ry.at[g, j - 1], rs_s1.at[g, 1, j - 1], rs_r1.at[g, 1, j - 1], at(yy, x, c)))

    def grads_start(g, top_chip):
        zst[g][1]()
        whole = merge(st_z.at[g], nz)
        top, total = whole[0:1], whole[1:2]
        grads = lt_sib[g] * (shares[g] * jnp.exp(top_chip - top) / total) - shares[g] * onehot(g)
        gt[:, g * tokens : (g + 1) * tokens] = grads.astype(bf16)
        grads_t = jnp.transpose(grads).astype(bf16)
        for buf, off in ((px, 0), (py, xw)):
            halves = [
                nn(grads_t, w2[:, :, off + k * qw : off + (k + 1) * qw].reshape(2 * vb, qw)).reshape(chips, 8, qw)
                for k in range(2)
            ]
            buf[g] = jnp.concatenate(halves, axis=1).astype(bf16).reshape(ny, nx, 16, qw)
            if g == 0:
                sum_first(g, off)
        dot = shares[g] * (whole[2:3] / total - whole[3:4])
        return (
            jnp.sum(jnp.where(iota((4, tokens), 1) == 4 * r + i4, dot, 0.0), axis=1, keepdims=True) / width
        )

    def sum_second(g):
        for axis, count, other_count, own_buf, got, out, out2 in (
            (0, ny, nx, px, rx, axs, rx2), (1, nx, ny, py, ry, ays, ry2),
        ):
            for j in range(1, other_count):
                arrived(got.at[g, j - 1], rs_r1.at[g, axis, j - 1])
            for jj in range(count):
                j = (jj + 1) % count
                k0 = lax.rem((y, x)[axis] + j, count)
                own_block = own_buf[g, k0, x] if axis == 0 else own_buf[g, y, k0]
                acc = own_block.astype(f32)
                for k in range(other_count - 1):
                    acc = acc + got[g, k, k0].astype(f32)
                for d in range(2):
                    four = jnp.concatenate([acc[4 * d : 4 * d + 4], acc[8 + 4 * d : 12 + 4 * d]], axis=0)
                    rest = four[:, cut:]
                    if 2 * cut > qw:
                        rest = jnp.concatenate([rest, jnp.zeros((8, 2 * cut - qw), f32)], axis=1)
                    out[g, j, d] = jnp.concatenate([four[:, :cut], rest], axis=0).astype(bf16)
                if j > 0:
                    for d in range(2):
                        device = at(k0, x, d) if axis == 0 else at(y, k0, d)
                        push(remote(out.at[g, j, d], out2.at[g, j, c], rs_s2.at[g, axis, j, d], rs_r2.at[g, axis, j, c], device))
                else:
                    push(remote(out.at[g, 0, 1 - c], out2.at[g, 0, c], rs_s2.at[g, axis, 0, 0], rs_r2.at[g, axis, 0, c], sibling))
                    out2[g, 0, c] = out[g, 0, c]

    zrs = [
        to_vocab(zrs_s.at[g], zrs_r.at[g], lambda zz, g=g: zs.at[g, zz], zr.at[g])
        for g in range(2)
    ]
    zag = [
        to_vocab(zag_s.at[g], zag_r.at[g], lambda zz, g=g: zo.at[g, v], zo.at[g])
        for g in range(2)
    ]

    def vocab_start(g):
        for buf, axis, count, off in ((rx2, 0, ny, 0), (ry2, 1, nx, xw)):
            for j in range(1, count):
                for s in range(2):
                    arrived(buf.at[g, j, s], rs_r2.at[g, axis, j, s])
            arrived(buf.at[g, 0, 1 - c], rs_r2.at[g, axis, 0, 1 - c])
            for s in range(2):
                acc = buf[g, 0, s].astype(f32)
                for j in range(1, count):
                    acc = acc + buf[g, j, s].astype(f32)
                wide = jnp.concatenate([acc[0:8], acc[8:16, : qw - cut]], axis=1)
                sum4[:, s * dh + off : s * dh + off + qw] = wide[0:4]
                sum4[:, s * dh + off + qw : s * dh + off + 2 * qw] = wide[4:8]
        for zz in range(nz):
            zs[g, zz] = fold4(sum4[:, starts[zz] : starts[zz] + LANES])
        zrs[g][0]()
        zr[g, v] = zs[g, v]

    def vocab_sum(g):
        zrs[g][1]()
        acc = zr[g, 0].astype(f32)
        for zz in range(1, nz):
            acc = acc + zr[g, zz].astype(f32)
        return unfold4(acc)

    def write(g, out):
        zag[g][1]()
        for zz in range(nz):
            out[:, starts[zz] : starts[zz] + LANES] = unfold4(zo[g, zz].astype(f32)).astype(bf16)

    a2a = to_rows(a2a_ss.at[0], a2a_rs.at[0], lambda rr: a2a_s.at[rr], a2a_r)
    pag = to_rows(pag_s.at[0], pag_r.at[0], lambda rr: po, pr)
    zga = to_vocab(zga_s.at[0], zga_r.at[0], lambda zz: gs.at[zz], gr)
    zgs = to_vocab(zg_s.at[0], zg_r.at[0], lambda zz: zg.at[v], zg)

    gather_first(0)
    place(1, slice(0, 4))
    gather_second(0)
    gather_first(1)

    for load in loads[3:]:
        load.wait()
    ir = iota((rows * 16, 4 * heads), 0)
    im = iota((rows * 16, 4 * heads), 1)
    kk = ir & 15
    pick = (kk < 8) & (im == (kk >> 1) * heads + 2 * (ir >> 4) + (kk & 1))
    a2a_s[...] = (
        nn(pick.astype(f32).astype(bf16), attn[...].reshape(4 * heads, hd)).astype(bf16).reshape(rows, 16, hd)
    )
    a2a_r[r] = a2a_s[r]

    it = iota((tokens, rows * 16), 0)
    il = iota((tokens, rows * 16), 1)
    base = 16 * (it >> 2) + (it & 3)
    sel[0:tokens, :] = (il == base + 4).astype(f32).astype(bf16)
    sel[tokens : 2 * tokens, :] = (il == base + 12).astype(f32).astype(bf16)
    ig = iota((16, rows * 16), 0)
    kg = iota((16, rows * 16), 1) & 15
    sel[2 * tokens : 2 * tokens + 16, :] = (
        ((ig == 0) & (kg < 2)) | ((ig == 1) & (kg >= 8) & (kg < 10))
    ).astype(f32).astype(bf16)
    base = 16 * (it >> 2) + 2 * (it & 3)
    for h in range(2):
        gather_v[h * tokens : (h + 1) * tokens, :] = (il == base + h).astype(f32).astype(bf16)
    opw[...] = jnp.zeros(opw.shape, bf16)
    shift = pl.multiple_of(v * step % 128, 16)
    opw[pl.ds(shift, step), :] = out_proj_t[...]

    w_copy.wait()
    arrived(w2.at[1 - c], sib_r.at[1])
    gather_second(1)
    gather_wait(0)
    logits_start(0)
    top_m = stats_start(0)
    gather_wait(1)
    logits_start(1)
    stats_second(0)
    top_t = stats_start(1)
    a2a[0]()
    drain()
    stats_second(1)
    dot_mean = grads_start(0, top_m)
    grads_start(1, top_t)
    sum_second(0)
    sum_first(1, 0)
    sum_first(1, xw)
    vocab_start(0)

    for n in range(0, dh, qw):
        head_out[:, n : n + qw] = nn(gt[pl.ds(pl.multiple_of((1 - c) * vb, 16), vb), :], hid[:, n : n + qw]).astype(bf16)
    push(remote(head_out, head_in, sib_s.at[4], sib_r.at[4], sibling))
    for n in range(0, dh, qw):
        head_own[:, n : n + qw] = nn(gt[pl.ds(pl.multiple_of(c * vb, 16), vb), :], hid[:, n : n + qw]).astype(bf16)
    head_stores = [
        pltpu.make_async_copy(head_own, o_head.at[:, own_cols], cp_sem.at[8]),
        pltpu.make_async_copy(head_in, o_head.at[:, sib_cols], cp_sem.at[9]),
    ]
    head_stores[0].start()

    sum_second(1)
    grad = vocab_sum(0)

    cols = pl.ds(window, LANES)
    normed4 = st4[:, cols]
    residual = inv4[:, 0:1] * (grad * gain_row[:, cols] - normed4 * dot_mean)
    gain_term = jnp.sum(grad * normed4, axis=0, keepdims=True)
    gain_high = gain_term.astype(bf16).astype(f32)
    po[...] = fold(
        jnp.concatenate([gain_high, gain_term - gain_high, jnp.zeros((2, LANES), f32), residual], axis=0)
    )
    pag[0]()
    pr[r] = po[...]
    zo[0, v] = fold4(residual)
    vocab_start(1)
    zag[0][0]()

    a2a[1]()
    received = a2a_r[...].reshape(rows * 16, hd)
    for h in range(2):
        vals[:, h * hd : (h + 1) * hd] = nn(gather_v[h * tokens : (h + 1) * tokens, :], received).astype(bf16)

    arrived(head_in, sib_r.at[4])
    head_stores[1].start()

    pag[1]()
    picked = nn(sel[...], pr[...].reshape(rows * 16, HALF))
    columns = jnp.concatenate([picked[0:tokens], picked[tokens : 2 * tokens]], axis=1)
    attn_term = nn(columns.astype(bf16), opw[...])
    for zz in range(nz):
        gs[zz] = fold(attn_term[8 * zz : 8 * zz + 8])
    zga[0]()
    gr[v] = gs[v]
    zg[v] = jnp.concatenate(
        [picked[2 * tokens + k // 2 : 2 * tokens + k // 2 + 1, k % 2 * 128 : k % 2 * 128 + 128] for k in range(LANES // 128)],
        axis=0,
    )
    zgs[0]()
    zo[1, v] = fold4(vocab_sum(1))
    zag[1][0]()

    proj_s[...] = nn(jnp.transpose(columns).astype(bf16), vals[...]).astype(bf16)
    o_proj_t[...] = proj_s[pl.ds(shift, step), :]

    drain()
    write(0, o_res)
    zgs[1]()
    for zz in range(nz):
        o_gain[starts[zz] // 128 : (starts[zz] + LANES) // 128, :] = zg[zz]
    zga[1]()
    acc = gr[0].astype(f32)
    for zz in range(1, nz):
        acc = acc + gr[zz].astype(f32)
    for h in range(2):
        attn_s[pl.ds(h, 8, stride=2), :] = acc[8 * h : 8 * h + 8]
    o_attn[...] = attn_s[...].astype(bf16)
    write(1, o_trunk)
    for store in head_stores:
        store.wait()


def finish(*refs):
    sources, targets, held, sem_in, sem_out = refs[0:6], refs[6:12], refs[12:18], refs[18], refs[19]
    pieces = []
    for src, dst, buf in zip(sources, targets, held):
        rows = src.shape[0]
        cut = rows // 9 * 3 if rows % 144 == 0 else rows
        for at in range(0, rows, cut):
            pieces.append((src.at[at : at + cut], dst.at[at : at + cut], buf.at[at : at + cut]))
    pieces.sort(key=lambda piece: -piece[0].shape[0] * piece[0].shape[1])
    loads = [pltpu.make_async_copy(src, buf, sem_in.at[i]) for i, (src, _, buf) in enumerate(pieces)]
    stores = [pltpu.make_async_copy(buf, dst, sem_out.at[i]) for i, (_, dst, buf) in enumerate(pieces)]
    for load in loads:
        load.start()
    for load, store in zip(loads, stores):
        load.wait()
        store.start()
    for store in stores:
        store.wait()


def local(dims, trunk_hidden, mtp_state, mtp_gain, head_weight, target_ids, mtp_target_ids, attn_values, out_proj):
    nx, ny, nz, width = dims
    rows = 2 * nx * ny
    tokens = 4 * rows
    vb = head_weight.shape[0]
    dh = width // 2
    qw = dh // 4
    cut = -(-qw // 256) * 128
    step = out_proj.shape[1]
    heads, hd = attn_values.shape[1:]
    vmem = pltpu.VMEM
    dma = pltpu.SemaphoreType.DMA
    scratch = [
        vmem((4, width), bf16),
        vmem((4, width), bf16),
        vmem((width // 128, 128), bf16),
        vmem((1, tokens), jnp.int32),
        vmem((1, tokens), jnp.int32),
        vmem((4, heads, hd), bf16),
        vmem((step, 2 * hd), bf16),
        vmem((1, width), f32),
        vmem((8, width), f32),
        vmem((4, width), f32),
        vmem((4, 128), f32),
        vmem((8, dh), f32),
        vmem((2, vb, dh), bf16),
        vmem((2, ny, nx, 16, qw), bf16),
        vmem((2, ny, nx, 16, qw), bf16),
        vmem((2 * tokens, dh), bf16),
        vmem((2, 2 * vb, tokens), f32),
        vmem((2, 2 * vb, tokens), f32),
        vmem((2, nx * ny, 4, tokens), f32),
        vmem((2, nz, 4, tokens), f32),
        vmem((2 * vb, 2 * tokens), bf16),
        vmem((2, ny, nx, 16, qw), bf16),
        vmem((2, ny, nx, 16, qw), bf16),
        vmem((vb, dh), bf16),
        vmem((vb, dh), bf16),
        vmem((vb, dh), bf16),
        vmem((2, max(nx - 1, 1), ny, 16, qw), bf16),
        vmem((2, max(ny - 1, 1), nx, 16, qw), bf16),
        vmem((2, ny, 2, 16, cut), bf16),
        vmem((2, nx, 2, 16, cut), bf16),
        vmem((2, ny, 2, 16, cut), bf16),
        vmem((2, nx, 2, 16, cut), bf16),
        vmem((4, width), f32),
        vmem((2, nz, 16, LANES // 4), bf16),
        vmem((2, nz, 16, LANES // 4), bf16),
        vmem((2, nz, 16, LANES // 4), bf16),
        vmem((16, HALF), bf16),
        vmem((rows, 16, HALF), bf16),
        vmem((2 * tokens + 16, rows * 16), bf16),
        vmem((2 * tokens, rows * 16), bf16),
        vmem((rows, 16, hd), bf16),
        vmem((rows, 16, hd), bf16),
        vmem((tokens, 2 * hd), bf16),
        vmem((LANES, 2 * hd), bf16),
        vmem((nz, LANES // 128, 128), f32),
        vmem((nz, 16, hd), bf16),
        vmem((nz, 16, hd), bf16),
        vmem((LANES, 2 * hd), bf16),
        vmem((16, hd), f32),
        dma((10,)),
        dma((5,)),
        dma((5,)),
        dma((2, 2, 3)),
        dma((2, 2, 4, 3)),
        dma((2, 2, ny, nx)),
        dma((2, 2)),
        dma((2,)),
        dma((2,)),
        dma((2,)),
        dma((2,)),
        dma((2, 2, 3)),
        dma((2, 2, 3)),
        dma((2, 2, 4, 2)),
        dma((2, 2, 4, 2)),
        dma((2,)),
        dma((2,)),
        dma((2,)),
        dma((2,)),
        dma((1,)),
        dma((1,)),
        dma((1,)),
        dma((1,)),
        dma((1,)),
        dma((1,)),
        dma((1,)),
        dma((1,)),
    ]
    in_vmem = pl.BlockSpec(memory_space=pltpu.VMEM)
    in_hbm = pl.BlockSpec(memory_space=pl.ANY)
    shape = jax.ShapeDtypeStruct
    shapes = [
        shape((4, width), bf16),
        shape((4, width), bf16),
        shape((width // 128, 128), f32),
        shape((vb, width), bf16),
        shape((16, hd), bf16),
        shape((step, 2 * hd), bf16),
    ]
    results = pl.pallas_call(
        functools.partial(kernel, dims),
        out_shape=shapes,
        in_specs=[pl.BlockSpec(memory_space=pltpu.HBM)] * 8,
        out_specs=[in_vmem] * 3 + [in_hbm] + [in_vmem] * 2,
        scratch_shapes=scratch,
        compiler_params=pltpu.CompilerParams(
            collective_id=0, has_side_effects=True, vmem_limit_bytes=60 * 2**20
        ),
        name="head_backward",
    )(
        trunk_hidden,
        mtp_state,
        mtp_gain.reshape(width // 128, 128),
        head_weight,
        target_ids.reshape(1, -1),
        mtp_target_ids.reshape(1, -1),
        attn_values,
        out_proj.T,
    )
    trunk_out, res_out, gain_out, head_out, attn_out, proj_out = pl.pallas_call(
        finish,
        out_shape=shapes,
        in_specs=[in_hbm] * len(shapes),
        out_specs=[in_hbm] * len(shapes),
        scratch_shapes=[vmem(s.shape, s.dtype) for s in shapes] + [dma((8,)), dma((8,))],
        compiler_params=pltpu.CompilerParams(vmem_limit_bytes=60 * 2**20),
        name="results",
    )(*results)
    grad_attn = attn_out.reshape(8, 2, hd)
    return (trunk_out, res_out, gain_out.reshape(width), head_out, grad_attn, proj_out.T)


def solution(mesh):
    nz, rows = mesh.shape["vocab"], mesh.shape["rows"]
    nx = {32: 4, 8: 2, 2: 1}[rows]

    def run(*args):
        dims = (nx, rows // 2 // nx, nz, args[0].shape[1])
        return local(dims, *args)

    return jax.shard_map(
        run,
        mesh=mesh,
        in_specs=(
            P("rows", None),
            P("rows", None),
            P(),
            P(("vocab", "rows"), None),
            P(),
            P(),
            P("rows", None, None),
            P("rows", "vocab"),
        ),
        out_specs=(
            P("rows", None),
            P("rows", None),
            P(),
            P(("vocab", "rows"), None),
            P("vocab", "rows", None),
            P("rows", "vocab"),
        ),
        check_vma=False,
    )
```
